128 devices in a mesh: gx: 4 (over z), gy: 4 (over x_lo, core), gz: 8 (over x_hi, y).
Axes of the slice: x: 4 (x_hi: 2, x_lo: 2; x = x_hi * 2 + x_lo), y: 4, z: 4, core: 2. Of those that a mesh axis runs over, the one named last changes fastest.
Arguments:
- charge: float32 [131072, 128], P(('gx', 'gy', 'gz')), may hold values from -4 to 4
- positions: float32 [3, 131072, 128], P(None, ('gx', 'gy', 'gz')), may hold values from 0 to 4
- counts: int32 [131072], P(('gx', 'gy', 'gz')), may hold values from 64 to 128, as said below
- corner: int32 [131072], P(('gx', 'gy', 'gz')), may hold values from 5462 to 81962, as said below
- fine_taps: float32 [2, 23], replicated, may hold values from 0 to 3, as said below
- coarse_taps: float32 [2, 23], replicated, may hold values from 0 to 3, as said below
Outputs:
- atom_potential: float32 [131072, 128], P(('gx', 'gy', 'gz'))
- grid_potential: float32 [128, 128, 512], P('gx', 'gy', 'gz')
The draws below stay inside these ranges and needn't reach their ends.
Inputs may be any that keep to these rules, and one draw needn't show every extreme that they name: `counts`: every cell holds 64 to 128 atoms; in every draw some cell is full. Each device lists its own cells once each, in some order; the cell with local cell coordinates (a, b, c) has corner ((4a + 2)(38) + 4b + 2)(70) + 4c + 2. `fine_taps`: positive taps. `coarse_taps`: positive taps.
All inputs are finite; a program needn't handle non-finite values.
Results may differ from the reference program's by a relative error of at most 0.0003.
Values sent between devices are 32-bit elements; how exact they have to be, the bound alone decides.
A program may use at most 192 MiB of HBM per device.

```python
import jax
import jax.numpy as jnp
from jax import lax

CX = 32
CY = 32
CZ = 64
RADIUS = 11
SLOTS = 128
TERMS = 2
CELLS_DEV = 1024
CELLS = 131072
NX = 128
NY = 128
NZ = 512
N_GX = 4
N_GY = 4
N_GZ = 8


def draw_counts(key, part):
    key = jax.random.fold_in(key, 1)
    values = jax.random.randint(key, (CELLS,), SLOTS // 2, SLOTS + 1)
    place = jax.random.randint(jax.random.fold_in(key, 7), (), 0, CELLS)
    return values.at[place].set(SLOTS).astype(jnp.int32)


def draw_corner(key, part):
    key = jax.random.fold_in(key, 2)
    devices = CELLS // CELLS_DEV
    keys = jax.random.split(key, devices)
    orders = jax.vmap(lambda single: jax.random.permutation(single, CELLS_DEV))(keys)
    along_y = CY // 4
    along_z = CZ // 4
    cell_x = orders // (along_y * along_z)
    cell_y = orders // along_z % along_y
    cell_z = orders % along_z
    flat = ((4 * cell_x + 2) * (CY + 6) + 4 * cell_y + 2) * (CZ + 6) + 4 * cell_z + 2
    return flat.reshape(CELLS).astype(jnp.int32)


def tap_table(key, low, high):
    length = 2 * RADIUS + 1
    spot = jnp.arange(length).astype(jnp.float32) - RADIUS
    widths = jnp.array([1.0, 0.5], jnp.float32)[:TERMS] * RADIUS
    envelope = jnp.exp(-(spot[None, :] / widths[:, None]) ** 2)
    factor = jnp.exp(jax.random.uniform(key, (TERMS, length), jnp.float32, jnp.log(low), jnp.log(high)))
    return (envelope * factor / jnp.sqrt(1.0 * RADIUS)).astype(jnp.float32)


def draw_fine_taps(key, part):
    key = jax.random.fold_in(key, 3)
    return tap_table(key, 0.5, 2.0)


def draw_coarse_taps(key, part):
    key = jax.random.fold_in(key, 4)
    return tap_table(key, 0.5, 2.0)


def steps_of(rng, shape, pieces, least, top_value):
    def one(position, parts):
        draws = jax.random.uniform(jax.random.fold_in(jax.random.fold_in(rng, 6), position), (parts,), jnp.float32, least / len(pieces), top_value / len(pieces))
        return jnp.repeat(jnp.exp(draws), shape[position] // parts).reshape((-1,) + (1,) * (len(shape) - position - 1))

    level = one(*pieces[0])
    for cut in pieces[1:]:
        level = level * one(*cut)
    return level


def scatter_about(rng, extent, scale, most, pieces=(), kind=jnp.bfloat16):
    level = steps_of(rng, extent, pieces, -0.22, 0.18) if pieces else 1.0
    values = jax.random.normal(rng, extent, jnp.float32) * scale * level
    return jnp.minimum(jnp.maximum(values, -most), most).astype(kind)


def setup_inputs(seed: int = 0) -> dict:
    seeds = jax.random.split(jax.random.key(seed), 7)
    return {
        "charge": scatter_about(seeds[0], (CELLS, SLOTS), 0.8, 4.0, ((0, 128),), jnp.float32),
        "positions": jnp.clip(4.0 * jax.random.uniform(seeds[1], (3, CELLS, SLOTS), jnp.float32) ** steps_of(seeds[1], (3, CELLS, SLOTS), ((1, 128),), -0.2, 0.2), 0.0, 4.0),
        "counts": draw_counts(jax.random.fold_in(seeds[6], 71), 0),
        "corner": draw_corner(jax.random.fold_in(seeds[6], 71), 0),
        "fine_taps": draw_fine_taps(jax.random.fold_in(seeds[6], 71), 0),
        "coarse_taps": draw_coarse_taps(jax.random.fold_in(seeds[6], 71), 0),
    }


highest = lax.Precision.HIGHEST


def bspline(shift):
    mag = jnp.abs(shift)
    inner = 2.0 / 3.0 - mag * mag + 0.5 * mag * mag * mag
    rest = 2.0 - mag
    outer = rest * rest * rest / 6.0
    return jnp.where(mag < 1.0, inner, jnp.where(mag < 2.0, outer, 0.0 * mag))


def spline_weights(coords):
    nodes = jnp.arange(8).astype(coords.dtype) - 1.0
    return bspline(coords[..., None] - nodes)


def live_charge(charge, counts):
    live = jnp.arange(charge.shape[1])[None, :] < counts[:, None]
    return jnp.where(live, charge, 0.0 * charge)


def make_tiles(charge, positions, counts):
    weighted = live_charge(charge, counts)
    total = charge.shape[0]
    block = math_gcd(total, 256)

    def one_block(start):
        part = lax.dynamic_slice_in_dim(weighted, start, block, 0)
        coords = lax.dynamic_slice_in_dim(positions, start, block, 1)
        weights = spline_weights(coords)
        first = part[:, :, None, None] * weights[0][:, :, :, None] * weights[1][:, :, None, :]
        tiles = jnp.einsum('nsab,nsc->nabc', first, weights[2], precision=highest)
        return tiles.reshape(block, 512)

    starts = (jnp.arange(total // block) * block).astype(jnp.int32)
    return lax.map(one_block, starts).reshape(total, 512)


def math_gcd(first, second):
    while second:
        first, second = second, first % second
    return first


def sample_tiles(values, positions, counts):
    total = values.shape[0]
    block = math_gcd(total, 256)
    slots = positions.shape[2]

    def one_block(start):
        part = lax.dynamic_slice_in_dim(values, start, block, 0).reshape(block, 8, 8, 8)
        coords = lax.dynamic_slice_in_dim(positions, start, block, 1)
        weights = spline_weights(coords)
        first = jnp.einsum('nabc,nsc->nsab', part, weights[2], precision=highest)
        return jnp.sum(first * weights[0][:, :, :, None] * weights[1][:, :, None, :], axis=(2, 3))

    starts = (jnp.arange(total // block) * block).astype(jnp.int32)
    result = lax.map(one_block, starts).reshape(total, slots)
    live = jnp.arange(slots)[None, :] < counts[:, None]
    return jnp.where(live, result, 0.0 * result)


def restrict_weight(gap):
    size = jnp.abs(gap)
    return jnp.where(size == 0, 1.0, jnp.where(size == 1, 0.5625, jnp.where(size == 3, -0.0625, 0.0)))


def periodic_conv(field, taps):
    reach = (taps.shape[1] - 1) // 2
    total = jnp.zeros_like(field)
    for term in range(taps.shape[0]):
        current = field
        for axis in range(3):
            acc = jnp.zeros_like(current)
            for tap in range(taps.shape[1]):
                acc = acc + taps[term, tap] * jnp.roll(current, -(tap - reach), axis)
            current = acc
        total = total + current
    return total


def restrict_grid(field):
    current = field
    for axis in range(3):
        acc = jnp.zeros_like(current)
        for gap in (-3, -1, 0, 1, 3):
            acc = acc + restrict_weight(jnp.int32(gap)).astype(field.dtype) * jnp.roll(current, -gap, axis)
        current = lax.slice_in_dim(acc, 0, acc.shape[axis], 2, axis)
    return current


def prolong_grid(field):
    current = field
    for axis in range(3):
        spaced = jnp.stack([current, jnp.zeros_like(current)], axis=axis + 1)
        shape = list(current.shape)
        shape[axis] = 2 * shape[axis]
        spaced = spaced.reshape(shape)
        acc = jnp.zeros_like(spaced)
        for gap in (-3, -1, 0, 1, 3):
            acc = acc + restrict_weight(jnp.int32(gap)).astype(field.dtype) * jnp.roll(spaced, gap, axis)
        current = acc
    return current


def global_points(corner, device):
    ext_y = CY + 6
    ext_z = CZ + 6
    grid_x = jnp.arange(8).astype(jnp.int32)
    offsets = (grid_x[:, None, None] * (ext_y * ext_z) + grid_x[None, :, None] * ext_z + grid_x[None, None, :]).reshape(512)
    flat = corner[:, None] + offsets[None, :]
    local_x = flat // (ext_y * ext_z)
    local_y = (flat // ext_z) % ext_y
    local_z = flat % ext_z
    mesh_x = device // (N_GY * N_GZ)
    mesh_y = (device // N_GZ) % N_GY
    mesh_z = device % N_GZ
    point_x = (mesh_x * CX + local_x - 3) % NX
    point_y = (mesh_y * CY + local_y - 3) % NY
    point_z = (mesh_z * CZ + local_z - 3) % NZ
    return ((point_x * NY + point_y) * NZ + point_z).astype(jnp.int32)


def reference(charge, positions, counts, corner, fine_taps, coarse_taps):
    devices = N_GX * N_GY * N_GZ
    per_device = charge.shape[0] // devices

    def add_device(grid, device):
        start = (device * per_device).astype(jnp.int32)
        part_charge = lax.dynamic_slice_in_dim(charge, start, per_device, 0)
        part_coords = lax.dynamic_slice_in_dim(positions, start, per_device, 1)
        part_counts = lax.dynamic_slice_in_dim(counts, start, per_device, 0)
        part_corner = lax.dynamic_slice_in_dim(corner, start, per_device, 0)
        tiles = make_tiles(part_charge, part_coords, part_counts)
        points = global_points(part_corner, device)
        return grid.at[points.reshape(-1)].add(tiles.reshape(-1)), None

    empty = jnp.zeros((NX * NY * NZ,), charge.dtype)
    flat_charge, unused = lax.scan(add_device, empty, jnp.arange(devices).astype(jnp.int32))
    fine_charge = flat_charge.reshape(NX, NY, NZ)
    near = periodic_conv(fine_charge, fine_taps)
    coarse_charge = restrict_grid(fine_charge)
    far = periodic_conv(coarse_charge, coarse_taps)
    grid_potential = near + prolong_grid(far)
    flat_potential = grid_potential.reshape(-1)

    def sample_device(device):
        start = (device * per_device).astype(jnp.int32)
        part_coords = lax.dynamic_slice_in_dim(positions, start, per_device, 1)
        part_counts = lax.dynamic_slice_in_dim(counts, start, per_device, 0)
        part_corner = lax.dynamic_slice_in_dim(corner, start, per_device, 0)
        points = global_points(part_corner, device)
        return sample_tiles(flat_potential[points], part_coords, part_counts)

    atom_potential = lax.map(sample_device, jnp.arange(devices).astype(jnp.int32))
    return atom_potential.reshape(charge.shape), grid_potential
```

```python
import jax
import jax.numpy as jnp
from jax import lax
from jax.experimental import pallas as pl
from jax.experimental.pallas import tpu as pltpu
from jax.sharding import PartitionSpec as P

CX = 32
CY = 32
CZ = 64
RADIUS = 11


highest = lax.Precision.HIGHEST


def padded_2(block, sides, width):
    for axis, dim in sides:
        count = lax.axis_size(axis)
        forward = [(i, i + 1) for i in range(count - 1)]
        forward.append((count - 1, 0))
        backward = [(target, source) for source, target in forward]
        low = lax.ppermute(
            lax.slice_in_dim(block, block.shape[dim] - width, None, axis=dim), axis, forward
        )
        high = lax.ppermute(lax.slice_in_dim(block, 0, width, axis=dim), axis, backward)
        block = jnp.concatenate([low, block, high], axis=dim)
    return block


f32 = jnp.float32
bf16 = jnp.bfloat16


def split(v):
    hi = v.astype(bf16)
    return hi, (v - hi.astype(f32)).astype(bf16)


def spline8(u, node):
    m = jnp.abs(u - node)
    t = jnp.maximum(2.0 - m, 0.0)
    v = jnp.maximum(1.0 - m, 0.0)
    return t * t * t - 4.0 * (v * v * v)


def row8(ref, lead, n):
    v = ref[pl.ds(n, 1), :] if lead is None else ref[lead, pl.ds(n, 1), :]
    return jnp.broadcast_to(v, (8, 128))


def spread_kernel(inv_ref, cnt_ref, q_ref, pos_ref, out_ref, acc, lhs, rhs):
    node = lax.broadcasted_iota(jnp.int32, (8, 128), 0).astype(f32) - 1.0
    lane = lax.broadcasted_iota(jnp.int32, (8, 128), 1)
    zero = jnp.zeros((8, 128), f32)
    acc[...] = jnp.zeros_like(acc)
    rhs[...] = jnp.zeros_like(rhs)

    def build(row, slot):
        for cz in range(16):
            n = inv_ref[row * 16 + cz]
            q = row8(q_ref, None, n)
            q = jnp.where(lane < cnt_ref[n], q * (1.0 / 216.0), 0.0)
            qx = q * spline8(row8(pos_ref, 0, n), node)
            wy = spline8(row8(pos_ref, 1, n), node)
            wz = spline8(row8(pos_ref, 2, n), node)
            prod = jnp.concatenate([qx[a : a + 1] * wy for a in range(8)], axis=0)
            hi, lo = split(prod)
            here = slice(cz * 128, cz * 128 + 128)
            lhs[slot, 0:64, here] = hi
            lhs[slot, 64:128, here] = lo
            pair = cz // 2
            base = 64 * (cz % 2) + 16 * (pair // 2)
            tile = jnp.concatenate([zero, wz] if pair % 2 else [wz, zero], axis=0)
            hi, lo = split(tile)
            rhs[slot, base : base + 16, here] = hi
            rhs[slot, 128 + base : 144 + base, here] = lo

    def finish(cx, start, odd, slot):
        r = lax.dot_general(
            lhs[slot], rhs[slot], (((1,), (1,)), ((), ())), preferred_element_type=f32
        )
        s = r[0:64] + r[64:128]
        t = s[:, 0:128] + s[:, 128:256]
        for a in range(8):
            acc[odd, 4 * cx + a, pl.ds(pl.multiple_of(start, 8), 8), :] += t[8 * a : 8 * a + 8]

    build(0, 0)

    def step(i, carry):
        cx = i // 4
        start = (i % 4) * 8
        build(2 * i + 1, 1)
        finish(cx, start, 0, 0)
        build(lax.rem(2 * i + 2, 64), 0)
        finish(cx, start, 1, 1)
        return carry

    lax.fori_loop(0, 32, step, 0)
    for x in range(36):
        out_ref[x, 0:32, :] = acc[0, x]
        out_ref[x, 32:40, :] = jnp.zeros((8, 128), f32)
        out_ref[x, 4:36, :] += acc[1, x]


SMEM = pl.BlockSpec(memory_space=pltpu.SMEM)
VMEM = pl.BlockSpec(memory_space=pltpu.VMEM)


def spread(inv, counts, charge, positions):
    return pl.pallas_call(
        spread_kernel,
        out_shape=jax.ShapeDtypeStruct((36, 40, 128), f32),
        in_specs=[SMEM, SMEM, VMEM, VMEM],
        out_specs=VMEM,
        scratch_shapes=[
            pltpu.VMEM((2, 36, 32, 128), f32),
            pltpu.VMEM((2, 128, 2048), bf16),
            pltpu.VMEM((2, 256, 2048), bf16),
        ],
        compiler_params=pltpu.CompilerParams(vmem_limit_bytes=48 * 1024 * 1024),
    )(inv, counts, charge, positions)


def sample_kernel(inv_ref, cnt_ref, pos_ref, v_ref, out_ref, vs, rhs):
    node = lax.broadcasted_iota(jnp.int32, (8, 128), 0).astype(f32) - 1.0
    lane = lax.broadcasted_iota(jnp.int32, (1, 128), 1)
    lane40 = lax.broadcasted_iota(jnp.int32, (40, 128), 1)
    zero = jnp.zeros((8, 128), f32)
    rhs[...] = jnp.zeros_like(rhs)
    for x in range(36):
        v = jnp.where(lane40 < 68, v_ref[x], 0.0) * (1.0 / 216.0)
        hi = v.astype(bf16).astype(f32)
        lo = (v - hi).astype(bf16).astype(f32)
        first = jnp.where(lane40 < 80, hi, pltpu.roll(lo, 80, 1))
        second = jnp.where(lane40 < 32, pltpu.roll(lo, 80, 1), pltpu.roll(hi, 32, 1))
        vs[0, x, :, 0:128] = first[0:32]
        vs[0, x, :, 128:256] = second[0:32]
        vs[1, x, :, 0:128] = first[4:36]
        vs[1, x, :, 128:256] = second[4:36]

    def one(cx, start, odd, row):
        left = vs[odd, pl.ds(4 * cx, 8), pl.ds(pl.multiple_of(start, 8), 8), :]
        left = left.reshape(64, 256).astype(bf16)
        for k in range(8):
            ns, ws = [], []
            for p in range(2):
                n = inv_ref[row * 16 + 2 * k + p]
                wz = spline8(row8(pos_ref, 2, n), node)
                if k % 2 == 0:
                    parts = [wz, zero]
                    if p:
                        parts = [pltpu.roll(jnp.concatenate(parts, 0), 4, 0)]
                else:
                    parts = [zero, wz, zero, zero]
                    if p:
                        parts = [zero, pltpu.roll(jnp.concatenate([wz, zero], 0), 4, 0), zero]
                hi, lo = split(jnp.concatenate(parts, 0))
                base = 16 * (k // 2)
                size = hi.shape[0]
                here = slice(p * 128, p * 128 + 128)
                rhs[odd, k, base : base + size, here] = hi
                rhs[odd, k, 80 + base : 80 + base + size, here] = hi
                rhs[odd, k, 160 + base : 160 + base + size, here] = lo
                ns.append(n)
            f = jnp.dot(left[:, 0:240], rhs[odd, k], preferred_element_type=f32)
            for p in range(2):
                n = ns[p]
                wx = spline8(row8(pos_ref, 0, n), node)
                wy = spline8(row8(pos_ref, 1, n), node)
                here = slice(p * 128, p * 128 + 128)
                g = wx[0:1] * f[0:8, here]
                for a in range(1, 8):
                    g = g + wx[a : a + 1] * f[8 * a : 8 * a + 8, here]
                r = jnp.sum(g * wy, axis=0, keepdims=True)
                out_ref[pl.ds(n, 1), :] = jnp.where(lane < cnt_ref[n], r, 0.0)

    def step(i, carry):
        cx = i // 4
        start = (i % 4) * 8
        one(cx, start, 0, 2 * i)
        one(cx, start, 1, 2 * i + 1)
        return carry

    lax.fori_loop(0, 32, step, 0)


def sample(inv, counts, positions, grid):
    return pl.pallas_call(
        sample_kernel,
        out_shape=jax.ShapeDtypeStruct((1024, 128), f32),
        in_specs=[SMEM, SMEM, VMEM, VMEM],
        out_specs=VMEM,
        scratch_shapes=[
            pltpu.VMEM((2, 36, 32, 256), f32),
            pltpu.VMEM((2, 8, 240, 256), bf16),
        ],
        compiler_params=pltpu.CompilerParams(vmem_limit_bytes=48 * 1024 * 1024),
    )(inv, counts, positions, grid)


def pad_along(piece, dim, before, after):
    widths = [(0, 0)] * piece.ndim
    widths[dim] = (before, after)
    return jnp.pad(piece, widths)


def place(piece, dim, before, after):
    return pad_along(piece, dim, before, after)


def fold_rims(padded, dim, size):
    middle = lax.slice_in_dim(padded, 6, size + 6, 1, dim)
    lower = lax.slice_in_dim(padded, 0, 3, 1, dim)
    upper = lax.slice_in_dim(padded, size + 9, size + 12, 1, dim)
    return middle + place(lower, dim, 0, size - 3) + place(upper, dim, size - 3, 0)


def conv_matrix(taps, inputs, outputs):
    length = taps.shape[1]
    gap = jnp.arange(inputs)[:, None] - jnp.arange(outputs)[None, :]
    pick = (gap[:, :, None] == jnp.arange(length)[None, None, :]).astype(taps.dtype)
    return jnp.einsum("iok,tk->tio", pick, taps, precision=highest)


def restrict_weight(gap):
    size = jnp.abs(gap)
    return jnp.where(
        size == 0, 1.0, jnp.where(size == 1, 0.5625, jnp.where(size == 3, -0.0625, 0.0))
    ).astype(jnp.float32)


def restrict_matrix(size, reach):
    gap = (
        jnp.arange(size + 2 * reach + 6)[:, None] - (reach + 3) - 2 * jnp.arange(size // 2)[None, :]
    )
    return restrict_weight(gap)


def prolong_matrix(size):
    gap = jnp.arange(size + 6)[None, :] - 3 - 2 * (jnp.arange(size // 2 + 6)[:, None] - 3)
    return restrict_weight(gap)


def convolve(field, first, second, third):
    section = jnp.einsum("xyz,txo->toyz", field, first, precision=highest)
    section = jnp.einsum("toyz,typ->topz", section, second, precision=highest)
    return jnp.einsum("topz,tzq->opq", section, third, precision=highest)


def apply_three(field, first, second, third):
    section = jnp.einsum("xyz,xo->oyz", field, first, precision=highest)
    section = jnp.einsum("oyz,yp->opz", section, second, precision=highest)
    return jnp.einsum("opz,zq->opq", section, third, precision=highest)


def body(charge, positions, counts, corner, fine_taps, coarse_taps):
    ext_y = CY + 6
    ext_z = CZ + 6
    along_x = CX // 4
    along_y = CY // 4
    along_z = CZ // 4
    cell_x = (corner // (ext_y * ext_z) - 2) // 4
    cell_y = (corner // ext_z % ext_y - 2) // 4
    cell_z = (corner % ext_z - 2) // 4
    lattice = (cell_x * along_y + cell_y) * along_z + cell_z
    spots = jnp.arange(along_x * along_y * along_z)
    inv = jnp.sum(jnp.where(lattice[None, :] == spots[:, None], spots[None, :], 0), axis=1)
    inv = inv.astype(jnp.int32)
    grid = spread(inv, counts, charge, positions)
    grid = pad_along(grid[:36, :36, :64], 2, 0, 4) + pad_along(grid[:36, :36, 64:], 2, 4, 0)
    spread_grid = jnp.pad(grid, ((2, 0), (2, 0), (2, 0)))
    sizes = (CX, CY, CZ)
    summed = padded_2(spread_grid, (("gx", 0), ("gy", 1), ("gz", 2)), 3)
    for dim in range(3):
        summed = fold_rims(summed, dim, sizes[dim])
    charges = padded_2(summed, (("gx", 0), ("gy", 1), ("gz", 2)), RADIUS + 3)
    fine_mats = [conv_matrix(fine_taps, size + 2 * RADIUS + 6, size + 6) for size in sizes]
    near = convolve(charges, fine_mats[0], fine_mats[1], fine_mats[2])
    shrink = [restrict_matrix(size, RADIUS) for size in sizes]
    coarse_charge = apply_three(charges, shrink[0], shrink[1], shrink[2])
    coarse_ext = padded_2(coarse_charge, (("gx", 0), ("gy", 1), ("gz", 2)), RADIUS + 3)
    coarse_mats = [
        conv_matrix(coarse_taps, size // 2 + 2 * RADIUS + 6, size // 2 + 6) for size in sizes
    ]
    far = convolve(coarse_ext, coarse_mats[0], coarse_mats[1], coarse_mats[2])
    widen = [prolong_matrix(size) for size in sizes]
    potential_grid = near + apply_three(far, widen[0], widen[1], widen[2])
    grid_potential = potential_grid[3 : CX + 3, 3 : CY + 3, 3 : CZ + 3]
    values = jnp.pad(potential_grid[2:, 2:, 2:], ((0, 0), (0, 4), (0, 60)))
    atom_potential = sample(inv, counts, positions, values)
    return (atom_potential, grid_potential)


def solution(mesh):
    placed = (
        P(("gx", "gy", "gz"), None),
        P(None, ("gx", "gy", "gz"), None),
        P(("gx", "gy", "gz")),
        P(("gx", "gy", "gz")),
        P(),
        P(),
    )
    return jax.shard_map(
        body,
        mesh=mesh,
        in_specs=placed,
        out_specs=(P(("gx", "gy", "gz"), None), P("gx", "gy", "gz")),
        check_vma=False,
    )
```

```python
import jax
import jax.numpy as jnp
from jax import lax
from jax.experimental import pallas as pl
from jax.experimental.pallas import tpu as pltpu
from jax.sharding import PartitionSpec as P

CX = 32
CY = 32
CZ = 64
f32 = jnp.float32
bf16 = jnp.bfloat16


def split(v):
    hi = v.astype(bf16)
    return hi, (v - hi.astype(f32)).astype(bf16)


def spline8(u, node):
    m = jnp.abs(u - node)
    t = jnp.maximum(2.0 - m, 0.0)
    v = jnp.maximum(1.0 - m, 0.0)
    return t * t * t - 4.0 * (v * v * v)


def row8(ref, lead, n):
    v = ref[pl.ds(n, 1), :] if lead is None else ref[lead, pl.ds(n, 1), :]
    return jnp.broadcast_to(v, (8, 128))


def spread_kernel(inv_ref, cnt_ref, q_ref, pos_ref, out_ref, acc, lhs, rhs):
    node = lax.broadcasted_iota(jnp.int32, (8, 128), 0).astype(f32) - 1.0
    lane = lax.broadcasted_iota(jnp.int32, (8, 128), 1)
    zero = jnp.zeros((8, 128), f32)
    acc[...] = jnp.zeros_like(acc)
    rhs[...] = jnp.zeros_like(rhs)

    def build(row, slot):
        for cz in range(16):
            n = inv_ref[row * 16 + cz]
            q = row8(q_ref, None, n)
            q = jnp.where(lane < cnt_ref[n], q * (1.0 / 216.0), 0.0)
            qx = q * spline8(row8(pos_ref, 0, n), node)
            wy = spline8(row8(pos_ref, 1, n), node)
            wz = spline8(row8(pos_ref, 2, n), node)
            prod = jnp.concatenate([qx[a : a + 1] * wy for a in range(8)], axis=0)
            hi, lo = split(prod)
            here = slice(cz * 128, cz * 128 + 128)
            lhs[slot, 0:64, here] = hi
            lhs[slot, 64:128, here] = lo
            pair = cz // 2
            base = 64 * (cz % 2) + 16 * (pair // 2)
            tile = jnp.concatenate([zero, wz] if pair % 2 else [wz, zero], axis=0)
            hi, lo = split(tile)
            rhs[slot, base : base + 16, here] = hi
            rhs[slot, 128 + base : 144 + base, here] = lo

    def finish(cx, start, odd, slot):
        r = lax.dot_general(
            lhs[slot], rhs[slot], (((1,), (1,)), ((), ())), preferred_element_type=f32
        )
        s = r[0:64] + r[64:128]
        t = s[:, 0:128] + s[:, 128:256]
        for a in range(8):
            acc[odd, 4 * cx + a, pl.ds(pl.multiple_of(start, 8), 8), :] += t[8 * a : 8 * a + 8]

    build(0, 0)

    def step(i, carry):
        cx = i // 4
        start = (i % 4) * 8
        build(2 * i + 1, 1)
        finish(cx, start, 0, 0)
        build(lax.rem(2 * i + 2, 64), 0)
        finish(cx, start, 1, 1)
        return carry

    lax.fori_loop(0, 32, step, 0)
    lane32 = lax.broadcasted_iota(jnp.int32, (32, 128), 1)
    for x in range(6):
        out_ref[x] = jnp.zeros((40, 128), f32)
    for x in range(42, 54):
        out_ref[x] = jnp.zeros((40, 128), f32)
    for x in range(36):
        joined = []
        for odd in range(2):
            v = acc[odd, x]
            low = jnp.where(lane32 < 64, v, 0.0)
            joined.append(pltpu.roll(low, 11, 1) + pltpu.roll(v - low, 79, 1))
        out_ref[6 + x, 0:32, :] = joined[0]
        out_ref[6 + x, 32:40, :] = jnp.zeros((8, 128), f32)
        out_ref[6 + x, 4:36, :] += joined[1]


SMEM = pl.BlockSpec(memory_space=pltpu.SMEM)
VMEM = pl.BlockSpec(memory_space=pltpu.VMEM)


def spread(inv, counts, charge, positions):
    return pl.pallas_call(
        spread_kernel,
        out_shape=jax.ShapeDtypeStruct((54, 40, 128), f32),
        in_specs=[SMEM, SMEM, VMEM, VMEM],
        out_specs=VMEM,
        scratch_shapes=[
            pltpu.VMEM((2, 36, 32, 128), f32),
            pltpu.VMEM((2, 128, 2048), bf16),
            pltpu.VMEM((2, 256, 2048), bf16),
        ],
        compiler_params=pltpu.CompilerParams(vmem_limit_bytes=48 * 1024 * 1024),
    )(inv, counts, charge, positions)


def sample_kernel(inv_ref, cnt_ref, pos_ref, v_ref, out_ref, grid_ref, vs, rhs):
    node = lax.broadcasted_iota(jnp.int32, (8, 128), 0).astype(f32) - 1.0
    lane = lax.broadcasted_iota(jnp.int32, (1, 128), 1)
    lane40 = lax.broadcasted_iota(jnp.int32, (40, 128), 1)
    zero = jnp.zeros((8, 128), f32)
    rhs[...] = jnp.zeros_like(rhs)
    for x in range(36):
        v = v_ref[x]
        if 1 <= x < 33:
            grid_ref[x - 1] = v[1:33, 0:64]
        v = jnp.where(lane40 < 68, pltpu.roll(v, 1, 1), 0.0) * (1.0 / 216.0)
        hi = v.astype(bf16).astype(f32)
        lo = (v - hi).astype(bf16).astype(f32)
        first = jnp.where(lane40 < 80, hi, pltpu.roll(lo, 80, 1))
        second = jnp.where(lane40 < 32, pltpu.roll(lo, 80, 1), pltpu.roll(hi, 32, 1))
        vs[0, x, :, 0:128] = first[0:32]
        vs[0, x, :, 128:256] = second[0:32]
        vs[1, x, :, 0:128] = first[4:36]
        vs[1, x, :, 128:256] = second[4:36]

    def one(cx, start, odd, row):
        left = vs[odd, pl.ds(4 * cx, 8), pl.ds(pl.multiple_of(start, 8), 8), :]
        left = left.reshape(64, 256).astype(bf16)
        for k in range(8):
            ns, ws = [], []
            for p in range(2):
                n = inv_ref[row * 16 + 2 * k + p]
                wz = spline8(row8(pos_ref, 2, n), node)
                if k % 2 == 0:
                    parts = [wz, zero]
                    if p:
                        parts = [pltpu.roll(jnp.concatenate(parts, 0), 4, 0)]
                else:
                    parts = [zero, wz, zero, zero]
                    if p:
                        parts = [zero, pltpu.roll(jnp.concatenate([wz, zero], 0), 4, 0), zero]
                hi, lo = split(jnp.concatenate(parts, 0))
                base = 16 * (k // 2)
                size = hi.shape[0]
                here = slice(p * 128, p * 128 + 128)
                rhs[odd, k, base : base + size, here] = hi
                rhs[odd, k, 80 + base : 80 + base + size, here] = hi
                rhs[odd, k, 160 + base : 160 + base + size, here] = lo
                ns.append(n)
            f = jnp.dot(left[:, 0:240], rhs[odd, k], preferred_element_type=f32)
            for p in range(2):
                n = ns[p]
                wx = spline8(row8(pos_ref, 0, n), node)
                wy = spline8(row8(pos_ref, 1, n), node)
                here = slice(p * 128, p * 128 + 128)
                g = wx[0:1] * f[0:8, here]
                for a in range(1, 8):
                    g = g + wx[a : a + 1] * f[8 * a : 8 * a + 8, here]
                r = jnp.sum(g * wy, axis=0, keepdims=True)
                out_ref[pl.ds(n, 1), :] = jnp.where(lane < cnt_ref[n], r, 0.0)

    def step(i, carry):
        cx = i // 4
        start = (i % 4) * 8
        one(cx, start, 0, 2 * i)
        one(cx, start, 1, 2 * i + 1)
        return carry

    lax.fori_loop(0, 32, step, 0)


def sample(inv, counts, positions, grid):
    return pl.pallas_call(
        sample_kernel,
        out_shape=(
            jax.ShapeDtypeStruct((1024, 128), f32),
            jax.ShapeDtypeStruct((32, 32, 64), f32),
        ),
        in_specs=[SMEM, SMEM, VMEM, VMEM],
        out_specs=(VMEM, VMEM),
        scratch_shapes=[
            pltpu.VMEM((2, 36, 32, 256), f32),
            pltpu.VMEM((2, 8, 240, 256), bf16),
        ],
        compiler_params=pltpu.CompilerParams(vmem_limit_bytes=48 * 1024 * 1024),
    )(inv, counts, positions, grid)


MESH = pl.DeviceIdType.MESH


def iota(shape, dim):
    return lax.broadcasted_iota(jnp.int32, shape, dim)


def weight_of(gap):
    size = jnp.abs(gap)
    return jnp.where(
        size == 0, 1.0, jnp.where(size == 1, 0.5625, jnp.where(size == 3, -0.0625, 0.0))
    )


def banded(gap, values, reach):
    total = jnp.zeros(gap.shape, f32)
    for m in range(-reach, reach + 1):
        total = total + jnp.where(gap == m, values[m + reach], 0.0)
    return total


def right(v, twice, rest):
    hi, lo = split(v)
    r = jnp.dot(jnp.concatenate([hi, lo], 1), twice, preferred_element_type=f32)
    return r + jnp.dot(hi, rest, preferred_element_type=f32)


def right_exact(v, twice):
    hi, lo = split(v)
    return jnp.dot(jnp.concatenate([hi, lo], 1), twice, preferred_element_type=f32)


def field_kernel(
    ft, ct, q_ref, v_ref,
    zs, zr, a_ref, ys, yr, xr, ext, rs, rr,
    c_ref, cxs, cxr, cext, d_ref, czs, czr, e_ref, cys, cyr, g_ref,
    cz_m, my_m, rz_m, ry_m, ccz_m, cmy_m, pz_m, ssem, rsem,
):
    ids = {name: lax.axis_index(name) for name in ("gx", "gy", "gz")}
    size_of = {"gx": 4, "gy": 4, "gz": 8}

    def away(name, step):
        count = size_of[name]
        return {name: lax.rem(ids[name] + (step + count), count)}

    for s in range(2):
        for j in range(21, 24):
            cyr[s, j] = jnp.zeros((16, 128), f32)
    barrier = pltpu.get_barrier_semaphore()
    for name in ("gx", "gy", "gz"):
        for step in (1, -1):
            pl.semaphore_signal(barrier, inc=1, device_id=away(name, step), device_id_type=MESH)

    lane = iota((1, 128), 1)
    lane40 = iota((40, 128), 1)
    lane24 = iota((24, 128), 1)
    half40 = lane40 % 64
    half24 = lane24 % 64

    def send(stage, name, up_src, up_dst, down_src, down_dst):
        copies = []
        for k, (step, src, dst) in enumerate(((1, up_src, up_dst), (-1, down_src, down_dst))):
            copy = pltpu.make_async_remote_copy(
                src_ref=src,
                dst_ref=dst,
                send_sem=ssem.at[stage, k],
                recv_sem=rsem.at[stage, k],
                device_id=away(name, step),
                device_id_type=MESH,
            )
            copy.start()
            copies.append(copy)
        return copies

    def finish(copies):
        for copy in copies:
            copy.wait()

    def pack_z(g, carry):
        up = jnp.zeros((40, 128), f32)
        down = jnp.zeros((40, 128), f32)
        for i in range(8):
            v = q_ref[6 + 8 * g + i]
            here = lane40 // 16 == i
            up = jnp.where(here, pltpu.roll(v, (16 * i - 64) % 128, 1), up)
            down = jnp.where(here, pltpu.roll(v, (16 * i - 11) % 128, 1), down)
        zs[0, g] = up
        zs[1, g] = down
        return carry

    lax.fori_loop(0, 5, pack_z, 0)
    pl.semaphore_wait(barrier, 6)
    z_copies = send(0, "gz", zs.at[0], zr.at[0], zs.at[1], zr.at[1])

    gap = iota((256, 128), 0) % 128 - 12 - 2 * (iota((256, 128), 1) % 64 - 13)
    node = iota((256, 128), 1) % 64 - 13
    rz_m[...] = jnp.where((node >= -2) & (node <= 34), weight_of(gap), 0.0).astype(bf16)
    gap = iota((24, 96), 1) % 48 - 2 * iota((24, 96), 0) + 3
    ry_m[...] = jnp.where(iota((24, 96), 1) % 48 < 40, weight_of(gap), 0.0).astype(bf16)

    def shrink(g, carry):
        rows = []
        for i in range(4):
            first = 2 * (4 * g + i)
            near = q_ref[first + 2] + q_ref[first + 4]
            wide = q_ref[first] + q_ref[first + 6]
            rows.append(q_ref[first + 3] + 0.5625 * near - 0.0625 * wide)
        r = right_exact(jnp.concatenate(rows, 0), rz_m[...])
        r = jnp.concatenate([r[40 * i : 40 * i + 40] for i in range(4)], 1)
        r = jnp.concatenate([r, jnp.zeros((8, 512), f32)], 0)
        hi, lo = split(r)
        r = jnp.dot(ry_m[...], jnp.concatenate([hi, lo], 0), preferred_element_type=f32)
        for i in range(4):
            c_ref[4 * g + i] = r[:, 128 * i : 128 * i + 128]
        return carry

    lax.fori_loop(0, 6, shrink, 0)
    for k in range(8):
        cxs[0, k] = jnp.where(lane24 < 64, c_ref[5 + k], c_ref[13 + k])
        cxs[1, k] = jnp.where(lane24 < 64, c_ref[k], c_ref[8 + k])
    cx_copies = send(1, "gx", cxs.at[0], cxr.at[0], cxs.at[1], cxr.at[1])

    ftap = [jnp.where(lane < 64, ft[0, m], ft[1, m]) for m in range(23)]
    gap = iota((128, 128), 0) - 12 - iota((128, 128), 1) % 64
    full = banded(gap, ftap, 11)
    hi, lo = split(full)
    cz_m[0:128] = hi
    cz_m[128:256] = hi
    cz_m[256:384] = lo

    def three_parts(rows, width, spots, values, reach):
        col = iota((rows, 256), 1)
        part = col // width
        total = banded(spots(col % width), values, reach)
        hi = total.astype(bf16).astype(f32)
        return jnp.where(part == 2, total - hi, hi).astype(bf16)

    row40 = iota((40, 256), 0)

    def spots_y(col):
        off = jnp.where(col < 40, col, jnp.where(col < 56, col - 52, col - 24))
        return jnp.where(col < 72, off - row40, 99)

    for t in range(2):
        taps = [ft[t, m] for m in range(23)]
        my_m[40 * t : 40 * t + 40] = three_parts(40, 80, spots_y, taps, 11)

    finish(z_copies)

    def conv_z(g, carry):
        up = zr[0, g]
        down = zr[1, g]
        rows = []
        for i in range(8):
            v = q_ref[6 + 8 * g + i]
            v = v + jnp.where(lane40 < 16, pltpu.roll(up, (-16 * i) % 128, 1), 0.0)
            here = (lane40 >= 75) & (lane40 < 91)
            v = v + jnp.where(here, pltpu.roll(down, (75 - 16 * i) % 128, 1), 0.0)
            rows.append(v)
        r = right(jnp.concatenate(rows, 0), cz_m[0:256], cz_m[256:384])
        for i in range(8):
            part = r[40 * i : 40 * i + 40]
            a_ref[8 * g + i] = part
            ys[0, 8 * g + i] = part[20:36]
            ys[1, 8 * g + i] = part[0:16]
        return carry

    lax.fori_loop(0, 5, conv_z, 0)
    own = pl.ds(0, 36)
    y_copies = send(2, "gy", ys.at[0, own], yr.at[0, own], ys.at[1, own], yr.at[1, own])

    ctap = [jnp.where(lane < 64, ct[0, m], ct[1, m]) for m in range(23)]
    gap = iota((128, 128), 0) % 64 - iota((128, 128), 1) % 64 - 11
    gap = jnp.where(iota((128, 128), 0) // 64 == iota((128, 128), 1) // 64, gap, 99)
    hi, lo = split(banded(gap, ctap, 11))
    ccz_m[0:128] = hi
    ccz_m[128:256] = hi
    ccz_m[256:384] = lo
    finish(cx_copies)
    for k in range(21):
        cext[11 + k] = c_ref[k]
    for s in range(2):
        base = 0 if s == 0 else 27
        for k in range(8):
            v = cxr[s, k]
            w = pltpu.roll(v, 64, 1)
            first = jnp.where(lane24 < 64, v, w)
            second = jnp.where(lane24 < 64, w, v)
            if s == 0:
                cext[k] = first
                if 8 + k >= 11:
                    cext[8 + k] += second
                else:
                    cext[8 + k] = second
            else:
                if 27 + k < 32:
                    cext[27 + k] += first
                else:
                    cext[27 + k] = first
                cext[35 + k] = second

    def conv_cx(c, carry):
        rows = pl.ds(pl.multiple_of(8 * c, 8), 8)
        for first in (0, 7, 14):
            acc = ctap[0] * cext[first : first + 7, rows, :]
            for m in range(1, 23):
                acc = acc + ctap[m] * cext[first + m : first + m + 7, rows, :]
            d_ref[first : first + 7, rows, :] = acc
        return carry

    lax.fori_loop(0, 3, conv_cx, 0)
    for j in range(21, 24):
        d_ref[j] = jnp.zeros((24, 128), f32)

    def pack_cz(g, carry):
        up = jnp.zeros((24, 128), f32)
        down = jnp.zeros((24, 128), f32)
        for i in range(4):
            v = d_ref[4 * g + i]
            here = half24 // 16 == i
            up = jnp.where(here, pltpu.roll(v, (16 * i - 32) % 128, 1), up)
            down = jnp.where(here, pltpu.roll(v, (16 * i - 11) % 128, 1), down)
        czs[0, g] = up
        czs[1, g] = down
        return carry

    lax.fori_loop(0, 6, pack_cz, 0)
    cz_copies = send(3, "gz", czs.at[0], czr.at[0], czs.at[1], czr.at[1])

    finish(y_copies)

    def conv_y(h, carry):
        both = []
        for p in range(2):
            x = 2 * h + p
            rows = [a_ref[x], yr[0, x], yr[1, x], jnp.zeros((8, 128), f32)]
            both.append(jnp.concatenate(rows, 0))
        hi, lo = split(jnp.concatenate(both, 1))
        stack = jnp.concatenate([hi, lo, hi], 0)
        r = jnp.dot(my_m[:, 0:240], stack, preferred_element_type=f32)
        for p in range(2):
            part = r[:, 128 * p : 128 * p + 128]
            ext[11 + 2 * h + p] = jnp.where(lane40 < 64, part[0:40], part[40:80])
        return carry

    lax.fori_loop(0, 18, conv_y, 0, unroll=3)
    x_copies = send(
        4, "gx", ext.at[pl.ds(32, 15)], xr.at[0], ext.at[pl.ds(11, 15)], xr.at[1]
    )

    finish(cz_copies)

    def conv_cz(g, carry):
        up = czr[0, g]
        down = czr[1, g]
        rows = []
        for i in range(4):
            v = d_ref[4 * g + i]
            v = v + jnp.where(half24 < 16, pltpu.roll(up, (-16 * i) % 128, 1), 0.0)
            here = (half24 >= 43) & (half24 < 59)
            v = v + jnp.where(here, pltpu.roll(down, (43 - 16 * i) % 128, 1), 0.0)
            rows.append(v)
        r = right(jnp.concatenate(rows, 0), ccz_m[0:256], ccz_m[256:384])
        for i in range(4):
            part = r[24 * i : 24 * i + 24]
            e_ref[4 * g + i] = part
            cys[0, 4 * g + i] = part[5:21]
            cys[1, 4 * g + i] = part[0:16]
        return carry

    lax.fori_loop(0, 6, conv_cz, 0)
    own = pl.ds(0, 21)
    cy_copies = send(5, "gy", cys.at[0, own], cyr.at[0, own], cys.at[1, own], cyr.at[1, own])

    def spots_cy(col):
        spot = jnp.where(col < 24, col - 2, jnp.where(col < 40, col - 37, col - 26))
        valid = ((col < 21) | (col >= 24)) & (col < 56)
        return jnp.where(valid, 2 * spot - (row40 - 1), 99)

    for t in range(2):
        taps = []
        for d in range(-25, 26):
            total = 0.0
            for g, weight in ((0, 1.0), (1, 0.5625), (-1, 0.5625), (3, -0.0625), (-3, -0.0625)):
                if (d + g) % 2 == 0 and abs((d + g) // 2) <= 11:
                    total = total + weight * ct[t, (d + g) // 2 + 11]
            taps.append(total)
        cmy_m[40 * t : 40 * t + 40] = three_parts(40, 64, spots_cy, taps, 25)
    spot = iota((256, 128), 0) % 64 - 2
    point = iota((256, 128), 1)
    point = jnp.where(point == 127, -1, point)
    good = (spot <= 34) & (point <= 66)
    pz_m[...] = jnp.where(good, weight_of(point - 2 * spot), 0.0).astype(bf16)

    finish(x_copies)
    ext[0:11] = xr[0, 0:11]
    ext[11:15] += xr[0, 11:15]
    ext[43:47] += xr[1, 0:4]
    ext[47:58] = xr[1, 4:15]

    def conv_x(k, carry):
        rows = pl.ds(pl.multiple_of(8 * (k // 3), 8), 8)
        first = 12 * lax.rem(k, 3)
        acc = ftap[0] * ext[pl.ds(first, 12), rows, :]
        for m in range(1, 23):
            acc = acc + ftap[m] * ext[pl.ds(first + m, 12), rows, :]
        for i in range(12):
            part = acc[i]
            v_ref[first + i, rows, :] = part + pltpu.roll(part, 64, 1)
        return carry

    lax.fori_loop(0, 15, conv_x, 0)
    for g in range(2):
        up = jnp.zeros((40, 128), f32)
        down = jnp.zeros((40, 128), f32)
        for i in range(32 if g == 0 else 4):
            v = v_ref[32 * g + i]
            here = lane40 // 4 == i
            up = jnp.where(here, pltpu.roll(v, (4 * i - 60) % 128, 1), up)
            down = jnp.where(here, pltpu.roll(v, (4 * i) % 128, 1), down)
        rs[0, g] = up
        rs[1, g] = down
    r_copies = send(6, "gz", rs.at[0], rr.at[0], rs.at[1], rr.at[1])

    finish(cy_copies)

    def conv_cy(h, carry):
        both = []
        for p in range(2):
            j = 2 * h + p
            rows = [e_ref[j], cyr[0, j], cyr[1, j], jnp.zeros((8, 128), f32)]
            both.append(jnp.concatenate(rows, 0))
        hi, lo = split(jnp.concatenate(both, 1))
        stack = jnp.concatenate([hi, lo, hi], 0)
        r = jnp.dot(cmy_m[:, 0:192], stack, preferred_element_type=f32)
        parts = []
        for p in range(2):
            part = r[:, 128 * p : 128 * p + 128]
            parts.append(jnp.where(lane40 < 64, part[0:40], part[40:80]))
        r = right_exact(jnp.concatenate(parts, 0), pz_m[...])
        g_ref[2 * h] = r[0:40]
        g_ref[2 * h + 1] = r[40:80]
        return carry

    lax.fori_loop(0, 11, conv_cy, 0)
    finish(r_copies)
    for x in range(36):
        g, i = x // 32, x % 32
        h = x // 2
        if x % 2:
            far = g_ref[h + 2]
        else:
            far = 0.5625 * (g_ref[h + 1] + g_ref[h + 2]) - 0.0625 * (g_ref[h] + g_ref[h + 3])
        near = jnp.where(lane40 < 64, v_ref[x], 0.0)
        above = pltpu.roll(rr[1, g], (64 - 4 * i) % 128, 1)
        below = pltpu.roll(rr[0, g], (124 - 4 * i) % 128, 1)
        near = jnp.where((lane40 >= 64) & (lane40 < 67), above, near)
        near = jnp.where(lane40 == 127, below, near)
        v_ref[x] = near + far


def field(fine_taps, coarse_taps, grid):
    def scratch(*shape):
        return pltpu.VMEM(shape, f32)

    return pl.pallas_call(
        field_kernel,
        out_shape=jax.ShapeDtypeStruct((36, 40, 128), f32),
        in_specs=[SMEM, SMEM, VMEM],
        out_specs=VMEM,
        scratch_shapes=[
            scratch(2, 5, 40, 128),
            scratch(2, 5, 40, 128),
            scratch(40, 40, 128),
            scratch(2, 40, 16, 128),
            scratch(2, 40, 16, 128),
            scratch(2, 15, 40, 128),
            scratch(58, 40, 128),
            scratch(2, 2, 40, 128),
            scratch(2, 2, 40, 128),
            scratch(24, 24, 128),
            scratch(2, 8, 24, 128),
            scratch(2, 8, 24, 128),
            scratch(43, 24, 128),
            scratch(24, 24, 128),
            scratch(2, 6, 24, 128),
            scratch(2, 6, 24, 128),
            scratch(24, 24, 128),
            scratch(2, 24, 16, 128),
            scratch(2, 24, 16, 128),
            scratch(22, 40, 128),
            pltpu.VMEM((384, 128), bf16),
            pltpu.VMEM((80, 256), bf16),
            pltpu.VMEM((256, 128), bf16),
            pltpu.VMEM((24, 96), bf16),
            pltpu.VMEM((384, 128), bf16),
            pltpu.VMEM((80, 256), bf16),
            pltpu.VMEM((256, 128), bf16),
            pltpu.SemaphoreType.DMA((7, 2)),
            pltpu.SemaphoreType.DMA((7, 2)),
        ],
        compiler_params=pltpu.CompilerParams(
            collective_id=0, has_side_effects=True, vmem_limit_bytes=48 * 1024 * 1024
        ),
    )(fine_taps, coarse_taps, grid)


def body(charge, positions, counts, corner, fine_taps, coarse_taps):
    ext_y = CY + 6
    ext_z = CZ + 6
    cell_x = (corner // (ext_y * ext_z) - 2) // 4
    cell_y = (corner // ext_z % ext_y - 2) // 4
    cell_z = (corner % ext_z - 2) // 4
    lattice = (cell_x * (CY // 4) + cell_y) * (CZ // 4) + cell_z
    spots = jnp.arange(lattice.shape[0])
    inv = jnp.sum(jnp.where(lattice[None, :] == spots[:, None], spots[None, :], 0), axis=1)
    inv = inv.astype(jnp.int32)
    grid = spread(inv, counts, charge, positions)
    values = field(fine_taps, coarse_taps, grid)
    return sample(inv, counts, positions, values)


def solution(mesh):
    placed = (
        P(("gx", "gy", "gz"), None),
        P(None, ("gx", "gy", "gz"), None),
        P(("gx", "gy", "gz")),
        P(("gx", "gy", "gz")),
        P(),
        P(),
    )
    return jax.shard_map(
        body,
        mesh=mesh,
        in_specs=placed,
        out_specs=(P(("gx", "gy", "gz"), None), P("gx", "gy", "gz")),
        check_vma=False,
    )
```

```python
import jax
import jax.numpy as jnp
import numpy as np
from jax import lax
from jax.experimental import pallas as pl
from jax.experimental.pallas import tpu as pltpu
from jax.sharding import PartitionSpec as P

CX = 32
CY = 32
CZ = 64
f32 = jnp.float32
bf16 = jnp.bfloat16


def split(v):
    hi = v.astype(bf16)
    return hi, (v - hi.astype(f32)).astype(bf16)


def spline8(u, node):
    m = jnp.abs(u - node)
    t = jnp.maximum(2.0 - m, 0.0)
    v = jnp.maximum(1.0 - m, 0.0)
    return t * t * t - 4.0 * (v * v * v)


def row8(ref, lead, n):
    v = ref[pl.ds(n, 1), :] if lead is None else ref[lead, pl.ds(n, 1), :]
    return jnp.broadcast_to(v, (8, 128))


def row8_at(ref, at, a):
    return jnp.broadcast_to(ref[at, 0, a : a + 1, :], (8, 128))


def spread_kernel(inv_ref, cnt_ref, q_ref, pos_ref, out_ref, xy_ref, z_ref, acc, place, qs, ts):
    node = lax.broadcasted_iota(jnp.int32, (8, 128), 0).astype(f32) - 1.0
    lane = lax.broadcasted_iota(jnp.int32, (8, 128), 1)
    zero = jnp.zeros((8, 128), f32)
    acc[...] = jnp.zeros_like(acc)
    ts[...] = jnp.zeros_like(ts)

    def cell(row, cz, spot):
        at = row * 16 + cz
        n = inv_ref[at]
        q = jnp.where(lane < cnt_ref[at], row8(q_ref, None, n), 0.0)
        wx = spline8(row8(pos_ref, 0, n), node)
        wy = spline8(row8(pos_ref, 1, n), node)
        wz = spline8(row8(pos_ref, 2, n), node)
        xy_ref[at, 0] = wx
        xy_ref[at, 1] = wy
        qs[spot] = q * wx
        prod = jnp.concatenate([row8(qs, spot, a) * wy for a in range(8)], axis=0)
        tile = jnp.concatenate([zero, wz] if cz % 2 else [wz, zero], axis=0)
        hi, lo = split(tile)
        z_ref[at, 0] = hi
        z_ref[at, 1] = lo
        return split(prod), (hi, lo)

    def line(odd, row):
        parts = []
        for half in range(2):
            for k in range(4):
                (ah, al), (bh, bl) = cell(row, 8 * half + 2 * k, 16 * odd + 8 * half + 2 * k)
                (ch, cl), (dh, dl) = cell(row, 8 * half + 2 * k + 1, 16 * odd + 8 * half + 2 * k + 1)
                left = jnp.concatenate(
                    [jnp.concatenate([ah, ch], 1), jnp.concatenate([al, cl], 1)], 0
                )
                down = jnp.concatenate(
                    [jnp.concatenate([bh, dh], 1), jnp.concatenate([bl, dl], 1)], 0
                )
                r = lax.dot_general(
                    down, left, (((1,), (1,)), ((), ())), preferred_element_type=f32
                )
                parts.append(r[0:16] + r[16:32])
        ts[odd] = jnp.concatenate(parts, 0)

    def finish(i, odd):
        spot = pl.ds(pl.multiple_of(i % 4 * 8, 8), 8)
        t = ts[odd].T
        t = t[0:64] + t[64:128]
        for a in range(8):
            acc[odd, 4 * (i // 4) + a, spot, :] += t[8 * a : 8 * a + 8]

    def step(i, carry):
        before = jnp.maximum(i - 1, 0)
        finish(before, 0)
        finish(before, 1)
        line(0, 2 * i)
        line(1, 2 * i + 1)
        return carry

    lax.fori_loop(0, 32, step, 0)
    finish(31, 0)
    finish(31, 1)

    lin = lax.broadcasted_iota(jnp.int32, (256, 128), 0) % 128
    z = 4 * (lin // 8) + lin % 8 + 11
    place[...] = jnp.where(z == lax.broadcasted_iota(jnp.int32, (256, 128), 1), 1.0, 0.0).astype(bf16)
    for x in range(6):
        out_ref[x] = jnp.zeros((40, 128), f32)
    for x in range(42, 54):
        out_ref[x] = jnp.zeros((40, 128), f32)

    def close(g, carry):
        joined = []
        for i in range(4):
            x = 4 * g + i
            pad = jnp.zeros((4, 128), f32)
            even = jnp.concatenate([acc[0, x], pad, pad], 0)
            odd = jnp.concatenate([pad, acc[1, x], pad], 0)
            joined.append(even + odd)
        hi, lo = split(jnp.concatenate(joined, 0))
        r = jnp.dot(jnp.concatenate([hi, lo], 1), place[...], preferred_element_type=f32)
        for i in range(4):
            out_ref[6 + 4 * g + i] = r[40 * i : 40 * i + 40] * (1.0 / 216.0)
        return carry

    lax.fori_loop(0, 9, close, 0)


SMEM = pl.BlockSpec(memory_space=pltpu.SMEM)
VMEM = pl.BlockSpec(memory_space=pltpu.VMEM)


def spread(inv, counts, charge, positions):
    return pl.pallas_call(
        spread_kernel,
        out_shape=(
            jax.ShapeDtypeStruct((54, 40, 128), f32),
            jax.ShapeDtypeStruct((1024, 2, 8, 128), f32),
            jax.ShapeDtypeStruct((1024, 2, 16, 128), bf16),
        ),
        in_specs=[SMEM, SMEM, VMEM, VMEM],
        out_specs=(VMEM, VMEM, VMEM),
        scratch_shapes=[
            pltpu.VMEM((2, 36, 32, 128), f32),
            pltpu.VMEM((256, 128), bf16),
            pltpu.VMEM((32, 8, 128), f32),
            pltpu.VMEM((2, 128, 128), f32),
        ],
        compiler_params=pltpu.CompilerParams(vmem_limit_bytes=28 * 1024 * 1024),
    )(inv, counts, charge, positions)


def sample_kernel(inv_ref, cnt_ref, xy_ref, z_ref, v_ref, out_ref, grid_ref, vs, place):
    lane = lax.broadcasted_iota(jnp.int32, (1, 128), 1)

    lin = lax.broadcasted_iota(jnp.int32, (256, 1024), 0)
    out = lax.broadcasted_iota(jnp.int32, (256, 1024), 1)
    within = out % 128
    z = (8 * (out // 128) + 4 * (within // 8 % 2) + within % 8 - 1) % 128
    part = within // 16
    hit = (z == lin % 128) & (part < 3) & ((part == 1) == (lin >= 128))
    place[...] = jnp.where(hit, 1.0, 0.0).astype(bf16)

    def open_rows(g, carry):
        rows = []
        for i in range(4):
            rows.append(v_ref[4 * g + i])
        hi, lo = split(jnp.concatenate(rows, 0) * (1.0 / 216.0))
        both = jnp.concatenate([hi, lo], 1)
        for k in range(0, 8, 2):
            r = jnp.dot(both, place[:, 128 * k : 128 * k + 256], preferred_element_type=f32)
            for i in range(4):
                for p in range(2):
                    here = r[40 * i : 40 * i + 40, 128 * p : 128 * p + 128]
                    vs[0, k + p, 4 * g + i] = here[0:32]
                    vs[1, k + p, 4 * g + i] = here[4:36]
        return carry

    lax.fori_loop(0, 9, open_rows, 0)
    for x in range(32):
        grid_ref[x] = v_ref[x + 1, 1:33, 0:64]

    def one(cx, start, odd, row):
        for k in range(8):
            spot = pl.ds(pl.multiple_of(start, 8), 8)
            left = vs[odd, k, pl.ds(4 * cx, 8), spot, :].reshape(64, 128).astype(bf16)
            at = row * 16 + 2 * k
            hi = jnp.concatenate([z_ref[at, 0], z_ref[at + 1, 0]], 1)
            lo = jnp.concatenate([z_ref[at, 1], z_ref[at + 1, 1]], 1)
            right_side = jnp.concatenate([hi, hi, lo], 0)
            f = jnp.dot(left[:, 0:48], right_side, preferred_element_type=f32)
            for p in range(2):
                here = slice(p * 128, p * 128 + 128)
                g = row8_at(xy_ref, at + p, 0) * f[0:8, here]
                for a in range(1, 8):
                    g = g + row8_at(xy_ref, at + p, a) * f[8 * a : 8 * a + 8, here]
                r = jnp.sum(g * xy_ref[at + p, 1], axis=0, keepdims=True)
                out_ref[pl.ds(inv_ref[at + p], 1), :] = jnp.where(lane < cnt_ref[at + p], r, 0.0)

    def step(i, carry):
        cx = i // 4
        start = (i % 4) * 8
        one(cx, start, 0, 2 * i)
        one(cx, start, 1, 2 * i + 1)
        return carry

    lax.fori_loop(0, 32, step, 0)


def sample(inv, counts, planes, depths, grid):
    return pl.pallas_call(
        sample_kernel,
        out_shape=(
            jax.ShapeDtypeStruct((1024, 128), f32),
            jax.ShapeDtypeStruct((32, 32, 64), f32),
        ),
        in_specs=[SMEM, SMEM, VMEM, VMEM, VMEM],
        out_specs=(VMEM, VMEM),
        scratch_shapes=[
            pltpu.VMEM((2, 8, 36, 32, 128), f32),
            pltpu.VMEM((256, 1024), bf16),
        ],
        compiler_params=pltpu.CompilerParams(vmem_limit_bytes=32 * 1024 * 1024),
    )(inv, counts, planes, depths, grid)


MESH = pl.DeviceIdType.MESH


def iota(shape, dim):
    return lax.broadcasted_iota(jnp.int32, shape, dim)


def weight_of(gap):
    size = jnp.abs(gap)
    return jnp.where(
        size == 0, 1.0, jnp.where(size == 1, 0.5625, jnp.where(size == 3, -0.0625, 0.0))
    )


def banded(gap, values, reach):
    total = jnp.zeros(gap.shape, f32)
    for m in range(-reach, reach + 1):
        total = total + jnp.where(gap == m, values[m + reach], 0.0)
    return total


def right(v, twice, rest):
    hi, lo = split(v)
    r = jnp.dot(jnp.concatenate([hi, lo], 1), twice, preferred_element_type=f32)
    return r + jnp.dot(hi, rest, preferred_element_type=f32)


def right_exact(v, twice):
    hi, lo = split(v)
    return jnp.dot(jnp.concatenate([hi, lo], 1), twice, preferred_element_type=f32)


def field_kernel(
    taps_ref, q_ref, v_ref,
    zs, zr, a_ref, ys, yr, xr, ext, rs, rr,
    c_ref, cxs, cxr, cext, d_ref, czs, czr, e_ref, cys, cyr, g_ref,
    cz_m, my_m, rz_m, ry_m, ccz_m, cmy_m, pz_m, ssem, rsem,
):
    ids = {name: lax.axis_index(name) for name in ("gx", "gy", "gz")}
    size_of = {"gx": 4, "gy": 4, "gz": 8}

    def away(name, step):
        count = size_of[name]
        return {name: lax.rem(ids[name] + (step + count), count)}

    for s in range(2):
        for j in range(21, 24):
            cyr[s, j] = jnp.zeros((16, 128), f32)
    barrier = pltpu.get_barrier_semaphore()
    for name in ("gx", "gy", "gz"):
        for step in (1, -1):
            pl.semaphore_signal(barrier, inc=1, device_id=away(name, step), device_id_type=MESH)

    lane = iota((1, 128), 1)
    lane40 = iota((40, 128), 1)
    lane24 = iota((24, 128), 1)
    half40 = lane40 % 64
    half24 = lane24 % 64

    def send(stage, name, up_src, up_dst, down_src, down_dst):
        copies = []
        for k, (step, src, dst) in enumerate(((1, up_src, up_dst), (-1, down_src, down_dst))):
            copy = pltpu.make_async_remote_copy(
                src_ref=src,
                dst_ref=dst,
                send_sem=ssem.at[stage, k],
                recv_sem=rsem.at[stage, k],
                device_id=away(name, step),
                device_id_type=MESH,
            )
            copy.start()
            copies.append(copy)
        return copies

    def finish(copies):
        for copy in copies:
            copy.wait()

    def pack_z(g, carry):
        up = jnp.zeros((40, 128), f32)
        down = jnp.zeros((40, 128), f32)
        for i in range(8):
            v = q_ref[6 + 8 * g + i]
            here = lane40 // 16 == i
            up = jnp.where(here, pltpu.roll(v, (16 * i - 64) % 128, 1), up)
            down = jnp.where(here, pltpu.roll(v, (16 * i - 11) % 128, 1), down)
        zs[0, g] = up
        zs[1, g] = down
        return carry

    lax.fori_loop(0, 5, pack_z, 0)
    pl.semaphore_wait(barrier, 6)
    z_copies = send(0, "gz", zs.at[0], zr.at[0], zs.at[1], zr.at[1])

    gap = iota((256, 128), 0) % 128 - 12 - 2 * (iota((256, 128), 1) % 64 - 13)
    node = iota((256, 128), 1) % 64 - 13
    rz_m[...] = jnp.where((node >= -2) & (node <= 34), weight_of(gap), 0.0).astype(bf16)
    gap = iota((24, 96), 1) % 48 - 2 * iota((24, 96), 0) + 3
    ry_m[...] = jnp.where(iota((24, 96), 1) % 48 < 40, weight_of(gap), 0.0).astype(bf16)

    def shrink(g, carry):
        rows = []
        for i in range(4):
            first = 2 * (4 * g + i)
            near = q_ref[first + 2] + q_ref[first + 4]
            wide = q_ref[first] + q_ref[first + 6]
            rows.append(q_ref[first + 3] + 0.5625 * near - 0.0625 * wide)
        r = right_exact(jnp.concatenate(rows, 0), rz_m[...])
        r = jnp.concatenate([r[40 * i : 40 * i + 40] for i in range(4)], 1)
        r = jnp.concatenate([r, jnp.zeros((8, 512), f32)], 0)
        hi, lo = split(r)
        r = jnp.dot(ry_m[...], jnp.concatenate([hi, lo], 0), preferred_element_type=f32)
        for i in range(4):
            c_ref[4 * g + i] = r[:, 128 * i : 128 * i + 128]
        return carry

    lax.fori_loop(0, 6, shrink, 0)
    for k in range(8):
        cxs[0, k] = jnp.where(lane24 < 64, c_ref[5 + k], c_ref[13 + k])
        cxs[1, k] = jnp.where(lane24 < 64, c_ref[k], c_ref[8 + k])
    cx_copies = send(1, "gx", cxs.at[0], cxr.at[0], cxs.at[1], cxr.at[1])

    ftap = [jnp.where(lane < 64, taps_ref[0, m], taps_ref[1, m]) for m in range(23)]
    gap = iota((128, 128), 0) - 12 - iota((128, 128), 1) % 64
    full = banded(gap, ftap, 11)
    hi, lo = split(full)
    cz_m[0:128] = hi
    cz_m[128:256] = hi
    cz_m[256:384] = lo

    def three_parts(rows, width, spots, values, reach):
        col = iota((rows, 256), 1)
        part = col // width
        total = banded(spots(col % width), values, reach)
        hi = total.astype(bf16).astype(f32)
        return jnp.where(part == 2, total - hi, hi).astype(bf16)

    row40 = iota((40, 256), 0)

    def spots_y(col):
        off = jnp.where(col < 40, col, jnp.where(col < 56, col - 52, col - 24))
        return jnp.where(col < 72, off - row40, 99)

    for t in range(2):
        taps = [taps_ref[t, m] for m in range(23)]
        my_m[40 * t : 40 * t + 40] = three_parts(40, 80, spots_y, taps, 11)

    finish(z_copies)

    def conv_z(g, carry):
        up = zr[0, g]
        down = zr[1, g]
        rows = []
        for i in range(8):
            v = q_ref[6 + 8 * g + i]
            v = v + jnp.where(lane40 < 16, pltpu.roll(up, (-16 * i) % 128, 1), 0.0)
            here = (lane40 >= 75) & (lane40 < 91)
            v = v + jnp.where(here, pltpu.roll(down, (75 - 16 * i) % 128, 1), 0.0)
            rows.append(v)
        r = right(jnp.concatenate(rows, 0), cz_m[0:256], cz_m[256:384])
        for i in range(8):
            part = r[40 * i : 40 * i + 40]
            a_ref[8 * g + i] = part
            ys[0, 8 * g + i] = part[20:36]
            ys[1, 8 * g + i] = part[0:16]
        return carry

    lax.fori_loop(0, 5, conv_z, 0)
    own = pl.ds(0, 36)
    y_copies = send(2, "gy", ys.at[0, own], yr.at[0, own], ys.at[1, own], yr.at[1, own])

    ctap = [jnp.where(lane < 64, taps_ref[2, m], taps_ref[3, m]) for m in range(23)]
    gap = iota((128, 128), 0) % 64 - iota((128, 128), 1) % 64 - 11
    gap = jnp.where(iota((128, 128), 0) // 64 == iota((128, 128), 1) // 64, gap, 99)
    hi, lo = split(banded(gap, ctap, 11))
    ccz_m[0:128] = hi
    ccz_m[128:256] = hi
    ccz_m[256:384] = lo
    finish(cx_copies)
    for k in range(21):
        cext[11 + k] = c_ref[k]
    for s in range(2):
        base = 0 if s == 0 else 27
        for k in range(8):
            v = cxr[s, k]
            w = pltpu.roll(v, 64, 1)
            first = jnp.where(lane24 < 64, v, w)
            second = jnp.where(lane24 < 64, w, v)
            if s == 0:
                cext[k] = first
                if 8 + k >= 11:
                    cext[8 + k] += second
                else:
                    cext[8 + k] = second
            else:
                if 27 + k < 32:
                    cext[27 + k] += first
                else:
                    cext[27 + k] = first
                cext[35 + k] = second

    def conv_cx(c, carry):
        rows = pl.ds(pl.multiple_of(8 * c, 8), 8)
        for first in (0, 7, 14):
            acc = ctap[0] * cext[first : first + 7, rows, :]
            for m in range(1, 23):
                acc = acc + ctap[m] * cext[first + m : first + m + 7, rows, :]
            d_ref[first : first + 7, rows, :] = acc
        return carry

    lax.fori_loop(0, 3, conv_cx, 0)
    for j in range(21, 24):
        d_ref[j] = jnp.zeros((24, 128), f32)

    def pack_cz(g, carry):
        up = jnp.zeros((24, 128), f32)
        down = jnp.zeros((24, 128), f32)
        for i in range(4):
            v = d_ref[4 * g + i]
            here = half24 // 16 == i
            up = jnp.where(here, pltpu.roll(v, (16 * i - 32) % 128, 1), up)
            down = jnp.where(here, pltpu.roll(v, (16 * i - 11) % 128, 1), down)
        czs[0, g] = up
        czs[1, g] = down
        return carry

    lax.fori_loop(0, 6, pack_cz, 0)
    cz_copies = send(3, "gz", czs.at[0], czr.at[0], czs.at[1], czr.at[1])

    finish(y_copies)

    def conv_y(h, carry):
        both = []
        for p in range(2):
            x = 2 * h + p
            rows = [a_ref[x], yr[0, x], yr[1, x], jnp.zeros((8, 128), f32)]
            both.append(jnp.concatenate(rows, 0))
        hi, lo = split(jnp.concatenate(both, 1))
        stack = jnp.concatenate([hi, lo, hi], 0)
        r = jnp.dot(my_m[:, 0:240], stack, preferred_element_type=f32)
        for p in range(2):
            part = r[:, 128 * p : 128 * p + 128]
            ext[11 + 2 * h + p] = jnp.where(lane40 < 64, part[0:40], part[40:80])
        return carry

    lax.fori_loop(0, 18, conv_y, 0, unroll=3)
    x_copies = send(
        4, "gx", ext.at[pl.ds(32, 15)], xr.at[0], ext.at[pl.ds(11, 15)], xr.at[1]
    )

    finish(cz_copies)

    def conv_cz(g, carry):
        up = czr[0, g]
        down = czr[1, g]
        rows = []
        for i in range(4):
            v = d_ref[4 * g + i]
            v = v + jnp.where(half24 < 16, pltpu.roll(up, (-16 * i) % 128, 1), 0.0)
            here = (half24 >= 43) & (half24 < 59)
            v = v + jnp.where(here, pltpu.roll(down, (43 - 16 * i) % 128, 1), 0.0)
            rows.append(v)
        r = right(jnp.concatenate(rows, 0), ccz_m[0:256], ccz_m[256:384])
        for i in range(4):
            part = r[24 * i : 24 * i + 24]
            e_ref[4 * g + i] = part
            cys[0, 4 * g + i] = part[5:21]
            cys[1, 4 * g + i] = part[0:16]
        return carry

    lax.fori_loop(0, 6, conv_cz, 0)
    own = pl.ds(0, 21)
    cy_copies = send(5, "gy", cys.at[0, own], cyr.at[0, own], cys.at[1, own], cyr.at[1, own])

    def spots_cy(col):
        spot = jnp.where(col < 24, col - 2, jnp.where(col < 40, col - 37, col - 26))
        valid = ((col < 21) | (col >= 24)) & (col < 56)
        return jnp.where(valid, 2 * spot - (row40 - 1), 99)

    for t in range(2):
        taps = []
        for d in range(-25, 26):
            total = 0.0
            for g, weight in ((0, 1.0), (1, 0.5625), (-1, 0.5625), (3, -0.0625), (-3, -0.0625)):
                if (d + g) % 2 == 0 and abs((d + g) // 2) <= 11:
                    total = total + weight * taps_ref[2 + t, (d + g) // 2 + 11]
            taps.append(total)
        cmy_m[40 * t : 40 * t + 40] = three_parts(40, 64, spots_cy, taps, 25)
    spot = iota((256, 128), 0) % 64 - 2
    point = iota((256, 128), 1)
    point = jnp.where(point == 127, -1, point)
    good = (spot <= 34) & (point <= 66)
    pz_m[...] = jnp.where(good, weight_of(point - 2 * spot), 0.0).astype(bf16)

    finish(x_copies)
    ext[0:11] = xr[0, 0:11]
    ext[11:15] += xr[0, 11:15]
    ext[43:47] += xr[1, 0:4]
    ext[47:58] = xr[1, 4:15]

    def conv_x(k, carry):
        rows = pl.ds(pl.multiple_of(8 * (k // 3), 8), 8)
        first = 12 * lax.rem(k, 3)
        acc = ftap[0] * ext[pl.ds(first, 12), rows, :]
        for m in range(1, 23):
            acc = acc + ftap[m] * ext[pl.ds(first + m, 12), rows, :]
        for i in range(12):
            part = acc[i]
            v_ref[first + i, rows, :] = part + pltpu.roll(part, 64, 1)
        return carry

    lax.fori_loop(0, 15, conv_x, 0)
    for g in range(2):
        up = jnp.zeros((40, 128), f32)
        down = jnp.zeros((40, 128), f32)
        for i in range(32 if g == 0 else 4):
            v = v_ref[32 * g + i]
            here = lane40 // 4 == i
            up = jnp.where(here, pltpu.roll(v, (4 * i - 60) % 128, 1), up)
            down = jnp.where(here, pltpu.roll(v, (4 * i) % 128, 1), down)
        rs[0, g] = up
        rs[1, g] = down
    r_copies = send(6, "gz", rs.at[0], rr.at[0], rs.at[1], rr.at[1])

    finish(cy_copies)

    def conv_cy(h, carry):
        both = []
        for p in range(2):
            j = 2 * h + p
            rows = [e_ref[j], cyr[0, j], cyr[1, j], jnp.zeros((8, 128), f32)]
            both.append(jnp.concatenate(rows, 0))
        hi, lo = split(jnp.concatenate(both, 1))
        stack = jnp.concatenate([hi, lo, hi], 0)
        r = jnp.dot(cmy_m[:, 0:192], stack, preferred_element_type=f32)
        parts = []
        for p in range(2):
            part = r[:, 128 * p : 128 * p + 128]
            parts.append(jnp.where(lane40 < 64, part[0:40], part[40:80]))
        r = right_exact(jnp.concatenate(parts, 0), pz_m[...])
        g_ref[2 * h] = r[0:40]
        g_ref[2 * h + 1] = r[40:80]
        return carry

    lax.fori_loop(0, 11, conv_cy, 0)
    finish(r_copies)
    for x in range(36):
        g, i = x // 32, x % 32
        h = x // 2
        if x % 2:
            far = g_ref[h + 2]
        else:
            far = 0.5625 * (g_ref[h + 1] + g_ref[h + 2]) - 0.0625 * (g_ref[h] + g_ref[h + 3])
        near = jnp.where(lane40 < 64, v_ref[x], 0.0)
        above = pltpu.roll(rr[1, g], (64 - 4 * i) % 128, 1)
        below = pltpu.roll(rr[0, g], (124 - 4 * i) % 128, 1)
        near = jnp.where((lane40 >= 64) & (lane40 < 67), above, near)
        near = jnp.where(lane40 == 127, below, near)
        v_ref[x] = near + far


def field(taps, grid):
    def scratch(*shape):
        return pltpu.VMEM(shape, f32)

    return pl.pallas_call(
        field_kernel,
        out_shape=jax.ShapeDtypeStruct((36, 40, 128), f32),
        in_specs=[SMEM, VMEM],
        out_specs=VMEM,
        scratch_shapes=[
            scratch(2, 5, 40, 128),
            scratch(2, 5, 40, 128),
            scratch(40, 40, 128),
            scratch(2, 40, 16, 128),
            scratch(2, 40, 16, 128),
            scratch(2, 15, 40, 128),
            scratch(58, 40, 128),
            scratch(2, 2, 40, 128),
            scratch(2, 2, 40, 128),
            scratch(24, 24, 128),
            scratch(2, 8, 24, 128),
            scratch(2, 8, 24, 128),
            scratch(43, 24, 128),
            scratch(24, 24, 128),
            scratch(2, 6, 24, 128),
            scratch(2, 6, 24, 128),
            scratch(24, 24, 128),
            scratch(2, 24, 16, 128),
            scratch(2, 24, 16, 128),
            scratch(22, 40, 128),
            pltpu.VMEM((384, 128), bf16),
            pltpu.VMEM((80, 256), bf16),
            pltpu.VMEM((256, 128), bf16),
            pltpu.VMEM((24, 96), bf16),
            pltpu.VMEM((384, 128), bf16),
            pltpu.VMEM((80, 256), bf16),
            pltpu.VMEM((256, 128), bf16),
            pltpu.SemaphoreType.DMA((7, 2)),
            pltpu.SemaphoreType.DMA((7, 2)),
        ],
        compiler_params=pltpu.CompilerParams(
            collective_id=0, has_side_effects=True, vmem_limit_bytes=24 * 1024 * 1024
        ),
    )(taps, grid)


def body(charge, positions, counts, corner, fine_taps, coarse_taps):
    ext_y = CY + 6
    ext_z = CZ + 6
    count = corner.shape[0]
    spots = np.arange(count, dtype=np.int32)
    along_y, along_z = CY // 4, CZ // 4
    cell_x, cell_y, cell_z = spots // (along_y * along_z), spots // along_z % along_y, spots % along_z
    wanted = ((4 * cell_x + 2) * ext_y + 4 * cell_y + 2) * ext_z + 4 * cell_z + 2
    same = corner[None, :] == wanted[:, None]
    number = lax.broadcasted_iota(jnp.int32, (count, count), 1)
    inv = jnp.sum(jnp.where(same, number, 0), axis=1, dtype=jnp.int32)
    live = jnp.sum(jnp.where(same, counts[None, :], 0), axis=1, dtype=jnp.int32)
    grid, planes, depths = spread(inv, live, charge, positions)
    values = field(jnp.concatenate([fine_taps, coarse_taps], 0), grid)
    return sample(inv, live, planes, depths, values)


def solution(mesh):
    placed = (
        P(("gx", "gy", "gz"), None),
        P(None, ("gx", "gy", "gz"), None),
        P(("gx", "gy", "gz")),
        P(("gx", "gy", "gz")),
        P(),
        P(),
    )
    return jax.shard_map(
        body,
        mesh=mesh,
        in_specs=placed,
        out_specs=(P(("gx", "gy", "gz"), None), P("gx", "gy", "gz")),
        check_vma=False,
    )
```

```python
import jax
import jax.numpy as jnp
import numpy as np
from jax import lax
from jax.experimental import pallas as pl
from jax.experimental.pallas import tpu as pltpu
from jax.sharding import PartitionSpec as P

CX = 32
CY = 32
CZ = 64
f32 = jnp.float32
bf16 = jnp.bfloat16


def split(v):
    hi = v.astype(bf16)
    return hi, (v - hi.astype(f32)).astype(bf16)


def spline8(u, node):
    m = jnp.abs(u - node)
    t = jnp.maximum(2.0 - m, 0.0)
    v = jnp.maximum(1.0 - m, 0.0)
    return t * t * t - 4.0 * (v * v * v)


def row8(ref, lead, n):
    v = ref[pl.ds(n, 1), :] if lead is None else ref[lead, pl.ds(n, 1), :]
    return jnp.broadcast_to(v, (8, 128))


def row8_at(ref, at, a):
    return jnp.broadcast_to(ref[at, 0, a : a + 1, :], (8, 128))


def spread_kernel(inv_ref, cnt_ref, q_ref, pos_ref, out_ref, xy_ref, z_ref, acc, place, qs, ts):
    node = lax.broadcasted_iota(jnp.int32, (8, 128), 0).astype(f32) - 1.0
    lane = lax.broadcasted_iota(jnp.int32, (8, 128), 1)
    zero = jnp.zeros((8, 128), f32)
    acc[...] = jnp.zeros_like(acc)
    ts[...] = jnp.zeros_like(ts)

    def cell(row, cz, spot):
        at = row * 16 + cz
        n = inv_ref[at]
        q = jnp.where(lane < cnt_ref[at], row8(q_ref, None, n), 0.0)
        wx = spline8(row8(pos_ref, 0, n), node)
        wy = spline8(row8(pos_ref, 1, n), node)
        wz = spline8(row8(pos_ref, 2, n), node)
        xy_ref[at, 0] = wx
        xy_ref[at, 1] = wy
        qs[spot] = q * wx
        prod = jnp.concatenate([row8(qs, spot, a) * wy for a in range(8)], axis=0)
        tile = jnp.concatenate([zero, wz] if cz % 2 else [wz, zero], axis=0)
        hi, lo = split(tile)
        z_ref[at, 0] = hi
        z_ref[at, 1] = lo
        return split(prod), (hi, lo)

    def line(odd, row):
        parts = []
        for half in range(2):
            for k in range(4):
                (ah, al), (bh, bl) = cell(row, 8 * half + 2 * k, 16 * odd + 8 * half + 2 * k)
                (ch, cl), (dh, dl) = cell(row, 8 * half + 2 * k + 1, 16 * odd + 8 * half + 2 * k + 1)
                left = jnp.concatenate(
                    [jnp.concatenate([ah, ch], 1), jnp.concatenate([al, cl], 1)], 0
                )
                down = jnp.concatenate(
                    [jnp.concatenate([bh, dh], 1), jnp.concatenate([bl, dl], 1)], 0
                )
                r = lax.dot_general(
                    down, left, (((1,), (1,)), ((), ())), preferred_element_type=f32
                )
                parts.append(r[0:16] + r[16:32])
        ts[odd] = jnp.concatenate(parts, 0)

    def finish(i, odd):
        spot = pl.ds(pl.multiple_of(i % 4 * 8, 8), 8)
        t = ts[odd].T
        t = t[0:64] + t[64:128]
        for a in range(8):
            acc[odd, 4 * (i // 4) + a, spot, :] += t[8 * a : 8 * a + 8]

    def step(i, carry):
        before = jnp.maximum(i - 1, 0)
        finish(before, 0)
        finish(before, 1)
        line(0, 2 * i)
        line(1, 2 * i + 1)
        return carry

    lax.fori_loop(0, 32, step, 0)
    finish(31, 0)
    finish(31, 1)

    lin = lax.broadcasted_iota(jnp.int32, (256, 128), 0) % 128
    z = 4 * (lin // 8) + lin % 8 + 11
    place[...] = jnp.where(z == lax.broadcasted_iota(jnp.int32, (256, 128), 1), 1.0, 0.0).astype(bf16)
    for x in range(6):
        out_ref[x] = jnp.zeros((40, 128), f32)
    for x in range(42, 54):
        out_ref[x] = jnp.zeros((40, 128), f32)

    def close(g, carry):
        joined = []
        for i in range(4):
            x = 4 * g + i
            pad = jnp.zeros((4, 128), f32)
            even = jnp.concatenate([acc[0, x], pad, pad], 0)
            odd = jnp.concatenate([pad, acc[1, x], pad], 0)
            joined.append(even + odd)
        hi, lo = split(jnp.concatenate(joined, 0))
        r = jnp.dot(jnp.concatenate([hi, lo], 1), place[...], preferred_element_type=f32)
        for i in range(4):
            out_ref[6 + 4 * g + i] = r[40 * i : 40 * i + 40] * (1.0 / 216.0)
        return carry

    lax.fori_loop(0, 9, close, 0)


SMEM = pl.BlockSpec(memory_space=pltpu.SMEM)
VMEM = pl.BlockSpec(memory_space=pltpu.VMEM)


def spread(inv, counts, charge, positions):
    return pl.pallas_call(
        spread_kernel,
        out_shape=(
            jax.ShapeDtypeStruct((54, 40, 128), f32),
            jax.ShapeDtypeStruct((1024, 2, 8, 128), f32),
            jax.ShapeDtypeStruct((1024, 2, 16, 128), bf16),
        ),
        in_specs=[SMEM, SMEM, VMEM, VMEM],
        out_specs=(VMEM, VMEM, VMEM),
        scratch_shapes=[
            pltpu.VMEM((2, 36, 32, 128), f32),
            pltpu.VMEM((256, 128), bf16),
            pltpu.VMEM((32, 8, 128), f32),
            pltpu.VMEM((2, 128, 128), f32),
        ],
        compiler_params=pltpu.CompilerParams(vmem_limit_bytes=28 * 1024 * 1024),
    )(inv, counts, charge, positions)


def sample_kernel(inv_ref, cnt_ref, xy_ref, z_ref, v_ref, out_ref, grid_ref, vs, place):
    lane = lax.broadcasted_iota(jnp.int32, (1, 128), 1)

    lin = lax.broadcasted_iota(jnp.int32, (256, 1024), 0)
    out = lax.broadcasted_iota(jnp.int32, (256, 1024), 1)
    within = out % 128
    z = (8 * (out // 128) + 4 * (within // 8 % 2) + within % 8 - 1) % 128
    part = within // 16
    hit = (z == lin % 128) & (part < 3) & ((part == 1) == (lin >= 128))
    place[...] = jnp.where(hit, 1.0, 0.0).astype(bf16)

    def open_rows(g, carry):
        rows = []
        for i in range(4):
            rows.append(v_ref[4 * g + i])
        hi, lo = split(jnp.concatenate(rows, 0) * (1.0 / 216.0))
        both = jnp.concatenate([hi, lo], 1)
        for k in range(0, 8, 2):
            r = jnp.dot(both, place[:, 128 * k : 128 * k + 256], preferred_element_type=f32)
            for i in range(4):
                for p in range(2):
                    here = r[40 * i : 40 * i + 40, 128 * p : 128 * p + 128]
                    vs[0, k + p, 4 * g + i] = here[0:32]
                    vs[1, k + p, 4 * g + i] = here[4:36]
        return carry

    lax.fori_loop(0, 9, open_rows, 0)
    for x in range(32):
        grid_ref[x] = v_ref[x + 1, 1:33, 0:64]

    def one(cx, start, odd, row):
        for k in range(8):
            spot = pl.ds(pl.multiple_of(start, 8), 8)
            left = vs[odd, k, pl.ds(4 * cx, 8), spot, :].reshape(64, 128).astype(bf16)
            at = row * 16 + 2 * k
            hi = jnp.concatenate([z_ref[at, 0], z_ref[at + 1, 0]], 1)
            lo = jnp.concatenate([z_ref[at, 1], z_ref[at + 1, 1]], 1)
            right_side = jnp.concatenate([hi, hi, lo], 0)
            f = jnp.dot(left[:, 0:48], right_side, preferred_element_type=f32)
            for p in range(2):
                here = slice(p * 128, p * 128 + 128)
                g = row8_at(xy_ref, at + p, 0) * f[0:8, here]
                for a in range(1, 8):
                    g = g + row8_at(xy_ref, at + p, a) * f[8 * a : 8 * a + 8, here]
                r = jnp.sum(g * xy_ref[at + p, 1], axis=0, keepdims=True)
                out_ref[pl.ds(inv_ref[at + p], 1), :] = jnp.where(lane < cnt_ref[at + p], r, 0.0)

    def step(i, carry):
        cx = i // 4
        start = (i % 4) * 8
        one(cx, start, 0, 2 * i)
        one(cx, start, 1, 2 * i + 1)
        return carry

    lax.fori_loop(0, 32, step, 0)


def sample(inv, counts, planes, depths, grid):
    return pl.pallas_call(
        sample_kernel,
        out_shape=(
            jax.ShapeDtypeStruct((1024, 128), f32),
            jax.ShapeDtypeStruct((32, 32, 64), f32),
        ),
        in_specs=[SMEM, SMEM, VMEM, VMEM, VMEM],
        out_specs=(VMEM, VMEM),
        scratch_shapes=[
            pltpu.VMEM((2, 8, 36, 32, 128), f32),
            pltpu.VMEM((256, 1024), bf16),
        ],
        compiler_params=pltpu.CompilerParams(vmem_limit_bytes=32 * 1024 * 1024),
    )(inv, counts, planes, depths, grid)


MESH = pl.DeviceIdType.MESH


def iota(shape, dim):
    return lax.broadcasted_iota(jnp.int32, shape, dim)


def weight_of(gap):
    size = jnp.abs(gap)
    return jnp.where(
        size == 0, 1.0, jnp.where(size == 1, 0.5625, jnp.where(size == 3, -0.0625, 0.0))
    )


def banded(gap, values, reach):
    total = jnp.zeros(gap.shape, f32)
    for m in range(-reach, reach + 1):
        total = jnp.where(gap == m, values[m + reach], total)
    return total


def right(v, twice, rest):
    hi, lo = split(v)
    r = jnp.dot(jnp.concatenate([hi, lo], 1), twice, preferred_element_type=f32)
    return r + jnp.dot(hi, rest, preferred_element_type=f32)


def right_exact(v, twice):
    hi, lo = split(v)
    return jnp.dot(jnp.concatenate([hi, lo], 1), twice, preferred_element_type=f32)


ORDER = (0, 4, 1, 3, 2)


def field_kernel(
    taps_ref, q_ref, v_ref,
    zs, zr, a_ref, ys, yr, xr, ext, rs, rr,
    c_ref, cxs, cxr, cext, d_ref, czs, czr, e_ref, cys, cyr, g_ref,
    cz_m, my_m, rz_m, ry_m, ccz_m, cmy_m, pz_m,
    zsem, ysem, xsem, csem, rsem,
):
    ids = {name: lax.axis_index(name) for name in ("gx", "gy", "gz")}
    size_of = {"gx": 4, "gy": 4, "gz": 8}

    def away(name, step):
        count = size_of[name]
        return {name: lax.rem(ids[name] + (step + count), count)}

    for s in range(2):
        for j in range(21, 24):
            cyr[s, j] = jnp.zeros((16, 128), f32)
    barrier = pltpu.get_barrier_semaphore()
    for name in ("gx", "gy", "gz"):
        for step in (1, -1):
            pl.semaphore_signal(barrier, inc=1, device_id=away(name, step), device_id_type=MESH)

    lane = iota((1, 128), 1)
    lane40 = iota((40, 128), 1)
    lane24 = iota((24, 128), 1)
    half24 = lane24 % 64

    def send(name, k, src, dst, sems, *spot):
        copy = pltpu.make_async_remote_copy(
            src_ref=src,
            dst_ref=dst,
            send_sem=sems.at[(0, *spot)],
            recv_sem=sems.at[(1, *spot)],
            device_id=away(name, 1 - 2 * k),
            device_id_type=MESH,
        )
        copy.start()
        return copy

    z_copies = {}
    for g in ORDER:
        up = jnp.zeros((40, 128), f32)
        down = jnp.zeros((40, 128), f32)
        for i in range(8 if g < 4 else 4):
            v = q_ref[6 + 8 * g + i]
            here = lane40 // 16 == i
            up = jnp.where(here, pltpu.roll(v, (16 * i - 64) % 128, 1), up)
            down = jnp.where(here, pltpu.roll(v, (16 * i - 11) % 128, 1), down)
        zs[0, g] = up
        zs[1, g] = down
        if g == 0:
            pl.semaphore_wait(barrier, 6)
        z_copies[g] = [send("gz", k, zs.at[k, g], zr.at[k, g], zsem, g, k) for k in range(2)]

    gap = iota((256, 128), 0) % 128 - 12 - 2 * (iota((256, 128), 1) % 64 - 13)
    node = iota((256, 128), 1) % 64 - 13
    rz_m[...] = jnp.where((node >= -2) & (node <= 34), weight_of(gap), 0.0).astype(bf16)
    gap = iota((24, 96), 1) % 48 - 2 * iota((24, 96), 0) + 3
    ry_m[...] = jnp.where(iota((24, 96), 1) % 48 < 40, weight_of(gap), 0.0).astype(bf16)

    def shrink(g, carry):
        rows = []
        for i in range(4):
            first = 2 * (4 * g + i)
            near = q_ref[first + 2] + q_ref[first + 4]
            wide = q_ref[first] + q_ref[first + 6]
            rows.append(q_ref[first + 3] + 0.5625 * near - 0.0625 * wide)
        r = right_exact(jnp.concatenate(rows, 0), rz_m[...])
        r = jnp.concatenate([r[40 * i : 40 * i + 40] for i in range(4)], 1)
        r = jnp.concatenate([r, jnp.zeros((8, 512), f32)], 0)
        hi, lo = split(r)
        r = jnp.dot(ry_m[...], jnp.concatenate([hi, lo], 0), preferred_element_type=f32)
        for i in range(4):
            c_ref[4 * g + i] = r[:, 128 * i : 128 * i + 128]
        return carry

    lax.fori_loop(0, 6, shrink, 0, unroll=2)
    for k in range(8):
        cxs[0, k] = jnp.where(lane24 < 64, c_ref[5 + k], c_ref[13 + k])
        cxs[1, k] = jnp.where(lane24 < 64, c_ref[k], c_ref[8 + k])
    cx_copies = [send("gx", k, cxs.at[k], cxr.at[k], csem, 0, k) for k in range(2)]

    ftap = [jnp.where(lane < 64, taps_ref[0, m], taps_ref[1, m]) for m in range(23)]
    gap = iota((128, 128), 0) - 12 - iota((128, 128), 1) % 64
    hi, lo = split(banded(gap, ftap, 11))
    cz_m[0:128] = hi
    cz_m[128:256] = hi
    cz_m[256:384] = lo
    row40 = iota((40, 128), 0)

    def make_my():
        off = jnp.where(lane40 < 40, lane40, jnp.where(lane40 < 56, lane40 - 52, lane40 - 24))
        gap = jnp.where(lane40 < 72, off - row40, 99)
        for t in range(2):
            full = banded(gap, [taps_ref[t, m] for m in range(23)], 11)
            hi = full.astype(bf16).astype(f32)
            lo = full - hi
            turned = pltpu.roll(hi, 80, 1)
            first = jnp.where(lane40 < 80, hi, turned)
            second = jnp.where(lane40 < 32, turned, pltpu.roll(lo, 32, 1))
            my_m[40 * t : 40 * t + 40] = jnp.concatenate([first, second], 1).astype(bf16)

    y_copies = {}
    for n, g in enumerate(ORDER):
        for copy in z_copies[g]:
            copy.wait()
        up = zr[0, g]
        down = zr[1, g]
        rows = []
        count = 8 if g < 4 else 4
        for i in range(count):
            v = q_ref[6 + 8 * g + i]
            v = v + jnp.where(lane40 < 16, pltpu.roll(up, (-16 * i) % 128, 1), 0.0)
            here = (lane40 >= 75) & (lane40 < 91)
            v = v + jnp.where(here, pltpu.roll(down, (75 - 16 * i) % 128, 1), 0.0)
            rows.append(v)
        r = right(jnp.concatenate(rows, 0), cz_m[0:256], cz_m[256:384])
        for i in range(count):
            part = r[40 * i : 40 * i + 40]
            a_ref[8 * g + i] = part
            ys[0, 8 * g + i] = part[20:36]
            ys[1, 8 * g + i] = part[0:16]
        own = pl.ds(8 * g, count)
        y_copies[g] = [
            send("gy", k, ys.at[k, own], yr.at[k, own], ysem, g, k) for k in range(2)
        ]

    make_my()

    ctap = [jnp.where(lane < 64, taps_ref[2, m], taps_ref[3, m]) for m in range(23)]
    gap = iota((128, 128), 0) % 64 - iota((128, 128), 1) % 64 - 11
    gap = jnp.where(iota((128, 128), 0) // 64 == iota((128, 128), 1) // 64, gap, 99)
    hi, lo = split(banded(gap, ctap, 11))
    ccz_m[0:128] = hi
    ccz_m[128:256] = hi
    ccz_m[256:384] = lo
    for copy in cx_copies:
        copy.wait()
    for k in range(21):
        cext[11 + k] = c_ref[k]
    for s in range(2):
        for k in range(8):
            v = cxr[s, k]
            w = pltpu.roll(v, 64, 1)
            first = jnp.where(lane24 < 64, v, w)
            second = jnp.where(lane24 < 64, w, v)
            if s == 0:
                cext[k] = first
                if 8 + k >= 11:
                    cext[8 + k] += second
                else:
                    cext[8 + k] = second
            else:
                if 27 + k < 32:
                    cext[27 + k] += first
                else:
                    cext[27 + k] = first
                cext[35 + k] = second

    def conv_cx(c, carry):
        rows = pl.ds(pl.multiple_of(8 * c, 8), 8)
        for first in (0, 7, 14):
            acc = ctap[0] * cext[first : first + 7, rows, :]
            for m in range(1, 23):
                acc = acc + ctap[m] * cext[first + m : first + m + 7, rows, :]
            d_ref[first : first + 7, rows, :] = acc
        return carry

    lax.fori_loop(0, 3, conv_cx, 0)
    for j in range(21, 24):
        d_ref[j] = jnp.zeros((24, 128), f32)

    def pack_cz(g, carry):
        up = jnp.zeros((24, 128), f32)
        down = jnp.zeros((24, 128), f32)
        for i in range(4):
            v = d_ref[4 * g + i]
            here = half24 // 16 == i
            up = jnp.where(here, pltpu.roll(v, (16 * i - 32) % 128, 1), up)
            down = jnp.where(here, pltpu.roll(v, (16 * i - 11) % 128, 1), down)
        czs[0, g] = up
        czs[1, g] = down
        return carry

    lax.fori_loop(0, 6, pack_cz, 0, unroll=2)
    cz_copies = [send("gz", k, czs.at[k], czr.at[k], csem, 1, k) for k in range(2)]

    pieces = {0: (1, 0, 8), 1: (1, 8, 15), 2: (0, 21, 24), 3: (0, 24, 32), 4: (0, 32, 36)}
    x_copies = []

    def conv_y(g):
        for copy in y_copies[g]:
            copy.wait()
        for h in range(4 if g < 4 else 2):
            both = []
            for p in range(2):
                x = 8 * g + 2 * h + p
                rows = [a_ref[x], yr[0, x], yr[1, x], jnp.zeros((8, 128), f32)]
                both.append(jnp.concatenate(rows, 0))
            hi, lo = split(jnp.concatenate(both, 1))
            stack = jnp.concatenate([hi, lo, hi], 0)
            r = jnp.dot(my_m[:, 0:240], stack, preferred_element_type=f32)
            for p in range(2):
                part = r[:, 128 * p : 128 * p + 128]
                ext[11 + 8 * g + 2 * h + p] = jnp.where(lane40 < 64, part[0:40], part[40:80])
        k, low, high = pieces[g]
        base = 0 if k else 21
        src = ext.at[pl.ds(11 + low, high - low)]
        dst = xr.at[k, pl.ds(low - base, high - low)]
        x_copies.append(send("gx", k, src, dst, xsem, g))

    conv_y(0)
    conv_y(4)

    for copy in cz_copies:
        copy.wait()

    def conv_cz(g, carry):
        up = czr[0, g]
        down = czr[1, g]
        rows = []
        for i in range(4):
            v = d_ref[4 * g + i]
            v = v + jnp.where(half24 < 16, pltpu.roll(up, (-16 * i) % 128, 1), 0.0)
            here = (half24 >= 43) & (half24 < 59)
            v = v + jnp.where(here, pltpu.roll(down, (43 - 16 * i) % 128, 1), 0.0)
            rows.append(v)
        r = right(jnp.concatenate(rows, 0), ccz_m[0:256], ccz_m[256:384])
        for i in range(4):
            part = r[24 * i : 24 * i + 24]
            e_ref[4 * g + i] = part
            cys[0, 4 * g + i] = part[5:21]
            cys[1, 4 * g + i] = part[0:16]
        return carry

    lax.fori_loop(0, 6, conv_cz, 0, unroll=2)
    conv_y(1)
    conv_y(3)
    conv_y(2)
    own = pl.ds(0, 21)
    cy_copies = [send("gy", k, cys.at[k, own], cyr.at[k, own], csem, 2, k) for k in range(2)]

    spot = jnp.where(lane40 < 24, lane40 - 2, jnp.where(lane40 < 40, lane40 - 37, lane40 - 26))
    valid = ((lane40 < 21) | (lane40 >= 24)) & (lane40 < 56)
    gap = jnp.where(valid, 2 * spot - (row40 - 1), 99)
    for t in range(2):
        taps = []
        for d in range(-25, 26):
            total = 0.0
            for g, weight in ((0, 1.0), (1, 0.5625), (-1, 0.5625), (3, -0.0625), (-3, -0.0625)):
                if (d + g) % 2 == 0 and abs((d + g) // 2) <= 11:
                    total = total + weight * taps_ref[2 + t, (d + g) // 2 + 11]
            taps.append(total)
        full = banded(gap, taps, 25)
        hi = full.astype(bf16).astype(f32)
        first = jnp.where(lane40 < 64, hi, pltpu.roll(hi, 64, 1))
        cmy_m[40 * t : 40 * t + 40] = jnp.concatenate([first, full - hi], 1).astype(bf16)
    spot = iota((256, 128), 0) % 64 - 2
    point = iota((256, 128), 1)
    point = jnp.where(point == 127, -1, point)
    good = (spot <= 34) & (point <= 66)
    pz_m[...] = jnp.where(good, weight_of(point - 2 * spot), 0.0).astype(bf16)

    for copy in x_copies:
        copy.wait()
    ext[0:11] = xr[0, 0:11]
    ext[11:15] += xr[0, 11:15]
    ext[43:47] += xr[1, 0:4]
    ext[47:58] = xr[1, 4:15]

    def conv_x(k, carry):
        rows = pl.ds(pl.multiple_of(8 * (k // 3), 8), 8)
        first = 12 * lax.rem(k, 3)
        acc = ftap[0] * ext[pl.ds(first, 12), rows, :]
        for m in range(1, 23):
            acc = acc + ftap[m] * ext[pl.ds(first + m, 12), rows, :]
        for i in range(12):
            part = acc[i]
            v_ref[first + i, rows, :] = part + pltpu.roll(part, 64, 1)
        return carry

    lax.fori_loop(0, 15, conv_x, 0)
    for g in range(2):
        up = jnp.zeros((40, 128), f32)
        down = jnp.zeros((40, 128), f32)
        for i in range(32 if g == 0 else 4):
            v = v_ref[32 * g + i]
            here = lane40 // 4 == i
            up = jnp.where(here, pltpu.roll(v, (4 * i - 60) % 128, 1), up)
            down = jnp.where(here, pltpu.roll(v, (4 * i) % 128, 1), down)
        rs[0, g] = up
        rs[1, g] = down
    r_copies = [send("gz", k, rs.at[k], rr.at[k], rsem, k) for k in range(2)]

    for copy in cy_copies:
        copy.wait()

    def conv_cy(h, carry):
        both = []
        for p in range(2):
            j = 2 * h + p
            rows = [e_ref[j], cyr[0, j], cyr[1, j], jnp.zeros((8, 128), f32)]
            both.append(jnp.concatenate(rows, 0))
        hi, lo = split(jnp.concatenate(both, 1))
        stack = jnp.concatenate([hi, lo, hi], 0)
        r = jnp.dot(cmy_m[:, 0:192], stack, preferred_element_type=f32)
        parts = []
        for p in range(2):
            part = r[:, 128 * p : 128 * p + 128]
            parts.append(jnp.where(lane40 < 64, part[0:40], part[40:80]))
        r = right_exact(jnp.concatenate(parts, 0), pz_m[...])
        g_ref[2 * h] = r[0:40]
        g_ref[2 * h + 1] = r[40:80]
        return carry

    lax.fori_loop(0, 11, conv_cy, 0, unroll=11)
    for x in range(36):
        h = x // 2
        if x % 2:
            far = g_ref[h + 2]
        else:
            far = 0.5625 * (g_ref[h + 1] + g_ref[h + 2]) - 0.0625 * (g_ref[h] + g_ref[h + 3])
        v_ref[x] = jnp.where(lane40 < 64, v_ref[x], 0.0) + far
    for copy in r_copies:
        copy.wait()
    for x in range(36):
        g, i = x // 32, x % 32
        above = pltpu.roll(rr[1, g], (64 - 4 * i) % 128, 1)
        below = pltpu.roll(rr[0, g], (124 - 4 * i) % 128, 1)
        rim = jnp.where((lane40 >= 64) & (lane40 < 67), above, 0.0)
        v_ref[x] += jnp.where(lane40 == 127, below, rim)


def field(taps, grid):
    def scratch(*shape):
        return pltpu.VMEM(shape, f32)

    return pl.pallas_call(
        field_kernel,
        out_shape=jax.ShapeDtypeStruct((36, 40, 128), f32),
        in_specs=[SMEM, VMEM],
        out_specs=VMEM,
        scratch_shapes=[
            scratch(2, 5, 40, 128),
            scratch(2, 5, 40, 128),
            scratch(40, 40, 128),
            scratch(2, 40, 16, 128),
            scratch(2, 40, 16, 128),
            scratch(2, 15, 40, 128),
            scratch(58, 40, 128),
            scratch(2, 2, 40, 128),
            scratch(2, 2, 40, 128),
            scratch(24, 24, 128),
            scratch(2, 8, 24, 128),
            scratch(2, 8, 24, 128),
            scratch(43, 24, 128),
            scratch(24, 24, 128),
            scratch(2, 6, 24, 128),
            scratch(2, 6, 24, 128),
            scratch(24, 24, 128),
            scratch(2, 24, 16, 128),
            scratch(2, 24, 16, 128),
            scratch(22, 40, 128),
            pltpu.VMEM((384, 128), bf16),
            pltpu.VMEM((80, 256), bf16),
            pltpu.VMEM((256, 128), bf16),
            pltpu.VMEM((24, 96), bf16),
            pltpu.VMEM((384, 128), bf16),
            pltpu.VMEM((80, 256), bf16),
            pltpu.VMEM((256, 128), bf16),
            pltpu.SemaphoreType.DMA((2, 5, 2)),
            pltpu.SemaphoreType.DMA((2, 5, 2)),
            pltpu.SemaphoreType.DMA((2, 5)),
            pltpu.SemaphoreType.DMA((2, 3, 2)),
            pltpu.SemaphoreType.DMA((2, 2)),
        ],
        compiler_params=pltpu.CompilerParams(
            collective_id=0, has_side_effects=True, vmem_limit_bytes=24 * 1024 * 1024
        ),
    )(taps, grid)


def body(charge, positions, counts, corner, fine_taps, coarse_taps):
    ext_y = CY + 6
    ext_z = CZ + 6
    count = corner.shape[0]
    spots = np.arange(count, dtype=np.int32)
    along_y, along_z = CY // 4, CZ // 4
    cell_x, cell_y, cell_z = spots // (along_y * along_z), spots // along_z % along_y, spots % along_z
    wanted = ((4 * cell_x + 2) * ext_y + 4 * cell_y + 2) * ext_z + 4 * cell_z + 2
    same = corner[None, :] == wanted[:, None]
    number = lax.broadcasted_iota(jnp.int32, (count, count), 1)
    inv = jnp.sum(jnp.where(same, number, 0), axis=1, dtype=jnp.int32)
    live = jnp.sum(jnp.where(same, counts[None, :], 0), axis=1, dtype=jnp.int32)
    grid, planes, depths = spread(inv, live, charge, positions)
    values = field(jnp.concatenate([fine_taps, coarse_taps], 0), grid)
    return sample(inv, live, planes, depths, values)


def solution(mesh):
    placed = (
        P(("gx", "gy", "gz"), None),
        P(None, ("gx", "gy", "gz"), None),
        P(("gx", "gy", "gz")),
        P(("gx", "gy", "gz")),
        P(),
        P(),
    )
    return jax.shard_map(
        body,
        mesh=mesh,
        in_specs=placed,
        out_specs=(P(("gx", "gy", "gz"), None), P("gx", "gy", "gz")),
        check_vma=False,
    )
```

```python
import jax
import jax.numpy as jnp
import numpy as np
from jax import lax
from jax.experimental import pallas as pl
from jax.experimental.pallas import tpu as pltpu
from jax.sharding import PartitionSpec as P

CX = 32
CY = 32
CZ = 64
f32 = jnp.float32
bf16 = jnp.bfloat16


def split(v):
    hi = v.astype(bf16)
    return hi, (v - hi.astype(f32)).astype(bf16)


def spline8(u, node):
    m = jnp.abs(u - node)
    t = jnp.maximum(2.0 - m, 0.0)
    v = jnp.maximum(1.0 - m, 0.0)
    return t * t * t - 4.0 * (v * v * v)


def row8(ref, lead, n):
    v = ref[pl.ds(n, 1), :] if lead is None else ref[lead, pl.ds(n, 1), :]
    return jnp.broadcast_to(v, (8, 128))


def row8_at(ref, at, a):
    return jnp.broadcast_to(ref[at, 0, a : a + 1, :], (8, 128))


SMEM = pl.BlockSpec(memory_space=pltpu.SMEM)
VMEM = pl.BlockSpec(memory_space=pltpu.VMEM)


def sample_kernel(inv_ref, cnt_ref, xy_ref, z_ref, v_ref, out_ref, grid_ref, vs, place):
    lane = lax.broadcasted_iota(jnp.int32, (1, 128), 1)

    lin = lax.broadcasted_iota(jnp.int32, (256, 1024), 0)
    out = lax.broadcasted_iota(jnp.int32, (256, 1024), 1)
    within = out % 128
    z = (8 * (out // 128) + 4 * (within // 8 % 2) + within % 8 - 1) % 128
    part = within // 16
    hit = (z == lin % 128) & (part < 3) & ((part == 1) == (lin >= 128))
    place[...] = jnp.where(hit, 1.0, 0.0).astype(bf16)

    def open_rows(g, carry):
        rows = []
        for i in range(4):
            rows.append(v_ref[4 * g + i])
        hi, lo = split(jnp.concatenate(rows, 0) * (1.0 / 216.0))
        both = jnp.concatenate([hi, lo], 1)
        for k in range(0, 8, 2):
            r = jnp.dot(both, place[:, 128 * k : 128 * k + 256], preferred_element_type=f32)
            for i in range(4):
                for p in range(2):
                    here = r[40 * i : 40 * i + 40, 128 * p : 128 * p + 128]
                    vs[0, k + p, 4 * g + i] = here[0:32]
                    vs[1, k + p, 4 * g + i] = here[4:36]
        return carry

    lax.fori_loop(0, 9, open_rows, 0)
    for x in range(32):
        grid_ref[x] = v_ref[x + 1, 1:33, 0:64]

    def one(cx, start, odd, row):
        for k in range(8):
            spot = pl.ds(pl.multiple_of(start, 8), 8)
            left = vs[odd, k, pl.ds(4 * cx, 8), spot, :].reshape(64, 128).astype(bf16)
            at = row * 16 + 2 * k
            hi = jnp.concatenate([z_ref[at, 0], z_ref[at + 1, 0]], 1)
            lo = jnp.concatenate([z_ref[at, 1], z_ref[at + 1, 1]], 1)
            right_side = jnp.concatenate([hi, hi, lo], 0)
            f = jnp.dot(left[:, 0:48], right_side, preferred_element_type=f32)
            for p in range(2):
                here = slice(p * 128, p * 128 + 128)
                g = row8_at(xy_ref, at + p, 0) * f[0:8, here]
                for a in range(1, 8):
                    g = g + row8_at(xy_ref, at + p, a) * f[8 * a : 8 * a + 8, here]
                r = jnp.sum(g * xy_ref[at + p, 1], axis=0, keepdims=True)
                out_ref[pl.ds(inv_ref[at + p], 1), :] = jnp.where(lane < cnt_ref[at + p], r, 0.0)

    def step(i, carry):
        cx = i // 4
        start = (i % 4) * 8
        one(cx, start, 0, 2 * i)
        one(cx, start, 1, 2 * i + 1)
        return carry

    lax.fori_loop(0, 32, step, 0)


def sample(inv, counts, planes, depths, grid):
    return pl.pallas_call(
        sample_kernel,
        out_shape=(
            jax.ShapeDtypeStruct((1024, 128), f32),
            jax.ShapeDtypeStruct((32, 32, 64), f32),
        ),
        in_specs=[SMEM, SMEM, VMEM, VMEM, VMEM],
        out_specs=(VMEM, VMEM),
        scratch_shapes=[
            pltpu.VMEM((2, 8, 36, 32, 128), f32),
            pltpu.VMEM((256, 1024), bf16),
        ],
        compiler_params=pltpu.CompilerParams(vmem_limit_bytes=32 * 1024 * 1024),
    )(inv, counts, planes, depths, grid)


MESH = pl.DeviceIdType.MESH


def iota(shape, dim):
    return lax.broadcasted_iota(jnp.int32, shape, dim)


def weight_of(gap):
    size = jnp.abs(gap)
    return jnp.where(
        size == 0, 1.0, jnp.where(size == 1, 0.5625, jnp.where(size == 3, -0.0625, 0.0))
    )


def banded(gap, values, reach):
    total = jnp.zeros(gap.shape, f32)
    for m in range(-reach, reach + 1):
        total = jnp.where(gap == m, values[m + reach], total)
    return total


def right(v, twice, rest):
    hi, lo = split(v)
    r = jnp.dot(jnp.concatenate([hi, lo], 1), twice, preferred_element_type=f32)
    return r + jnp.dot(hi, rest, preferred_element_type=f32)


def right_exact(v, twice):
    hi, lo = split(v)
    return jnp.dot(jnp.concatenate([hi, lo], 1), twice, preferred_element_type=f32)


def field_kernel(
    inv_ref, cnt_ref, taps_ref, charge_ref, pos_ref, v_ref, xy_ref, z_ref,
    acc, place, qs, ts, q_ref,
    zs, zr, a_ref, ys, yr, xr, ext, rs, rr,
    c_ref, cxs, cxr, cext, d_ref, czs, czr, e_ref, cys, cyr, g_ref,
    cz_m, my_m, rz_m, ry_m, ccz_m, cmy_m, pz_m,
    zsem, ysem, xsem, csem, rsem,
):
    ids = {name: lax.axis_index(name) for name in ("gx", "gy", "gz")}
    size_of = {"gx": 4, "gy": 4, "gz": 8}

    def away(name, step):
        count = size_of[name]
        return {name: lax.rem(ids[name] + (step + count), count)}

    for s in range(2):
        for j in range(21, 24):
            cyr[s, j] = jnp.zeros((16, 128), f32)
    barrier = pltpu.get_barrier_semaphore()
    for name in ("gx", "gy", "gz"):
        for step in (1, -1):
            pl.semaphore_signal(barrier, inc=1, device_id=away(name, step), device_id_type=MESH)

    lane = iota((1, 128), 1)
    lane40 = iota((40, 128), 1)
    lane24 = iota((24, 128), 1)
    half24 = lane24 % 64

    def link(name, k, src, dst, sems, *spot):
        return pltpu.make_async_remote_copy(
            src_ref=src,
            dst_ref=dst,
            send_sem=sems.at[(0, *spot)],
            recv_sem=sems.at[(1, *spot)],
            device_id=away(name, 1 - 2 * k),
            device_id_type=MESH,
        )

    def send(*args):
        copy = link(*args)
        copy.start()
        return copy

    def links_z(g):
        return [link("gz", k, zs.at[k, g], zr.at[k, g], zsem, g, k) for k in range(2)]

    def links_y(g):
        own = pl.ds(8 * g, 8 if g < 4 else 4)
        return [link("gy", k, ys.at[k, own], yr.at[k, own], ysem, g, k) for k in range(2)]

    pieces = {0: (1, 0, 8), 1: (1, 8, 15), 2: (0, 21, 24), 3: (0, 24, 32), 4: (0, 32, 36)}

    def link_x(g):
        k, low, high = pieces[g]
        base = 0 if k else 21
        src = ext.at[pl.ds(11 + low, high - low)]
        dst = xr.at[k, pl.ds(low - base, high - low)]
        return link("gx", k, src, dst, xsem, g)

    knot = iota((8, 128), 0).astype(f32) - 1.0
    lane8 = iota((8, 128), 1)
    zero = jnp.zeros((8, 128), f32)
    acc[...] = jnp.zeros_like(acc)
    ts[...] = jnp.zeros_like(ts)
    for x in range(6):
        q_ref[x] = jnp.zeros((40, 128), f32)
    for x in range(42, 54):
        q_ref[x] = jnp.zeros((40, 128), f32)

    def cell(row, cz, spot):
        at = row * 16 + cz
        n = inv_ref[at]
        q = jnp.where(lane8 < cnt_ref[at], row8(charge_ref, None, n), 0.0)
        wx = spline8(row8(pos_ref, 0, n), knot)
        wy = spline8(row8(pos_ref, 1, n), knot)
        wz = spline8(row8(pos_ref, 2, n), knot)
        xy_ref[at, 0] = wx
        xy_ref[at, 1] = wy
        qs[spot] = q * wx
        prod = jnp.concatenate([row8(qs, spot, a) * wy for a in range(8)], axis=0)
        tile = jnp.concatenate([zero, wz] if cz % 2 else [wz, zero], axis=0)
        hi, lo = split(tile)
        z_ref[at, 0] = hi
        z_ref[at, 1] = lo
        return split(prod), (hi, lo)

    def line(odd, row):
        parts = []
        for k in range(8):
            (ah, al), (bh, bl) = cell(row, 2 * k, 16 * odd + 2 * k)
            (ch, cl), (dh, dl) = cell(row, 2 * k + 1, 16 * odd + 2 * k + 1)
            left = jnp.concatenate(
                [jnp.concatenate([ah, ch], 1), jnp.concatenate([al, cl], 1)], 0
            )
            down = jnp.concatenate(
                [jnp.concatenate([bh, dh], 1), jnp.concatenate([bl, dl], 1)], 0
            )
            r = lax.dot_general(down, left, (((1,), (1,)), ((), ())), preferred_element_type=f32)
            parts.append(r[0:16] + r[16:32])
        ts[odd] = jnp.concatenate(parts, 0)

    def slab_of(n):
        late = jnp.minimum(n // 2, 1)
        last = jnp.minimum(n // 5, 1)
        return n + (late - last) * (9 - 2 * n) - 3 * last

    def drain(i, odd):
        spot = pl.ds(pl.multiple_of(i % 4 * 8, 8), 8)
        t = ts[odd].T
        t = t[0:64] + t[64:128]
        for a in range(8):
            acc[odd, 4 * slab_of(i // 4) + a, spot, :] += t[8 * a : 8 * a + 8]

    def step(i, carry):
        before = jnp.maximum(i - 1, 0)
        drain(before, 0)
        drain(before, 1)
        row = 8 * slab_of(i // 4) + 2 * (i % 4)
        line(0, row)
        line(1, row + 1)
        return carry

    lin = iota((256, 128), 0) % 128
    place[...] = jnp.where(4 * (lin // 8) + lin % 8 + 11 == iota((256, 128), 1), 1.0, 0.0).astype(bf16)

    def close(g):
        count = 8 if g < 4 else 4
        joined = []
        for i in range(count):
            x = 8 * g + i
            pad = jnp.zeros((4, 128), f32)
            even = jnp.concatenate([acc[0, x], pad, pad], 0)
            odd = jnp.concatenate([pad, acc[1, x], pad], 0)
            joined.append(even + odd)
        hi, lo = split(jnp.concatenate(joined, 0))
        r = jnp.dot(jnp.concatenate([hi, lo], 1), place[...], preferred_element_type=f32)
        up = jnp.zeros((40, 128), f32)
        down = jnp.zeros((40, 128), f32)
        for i in range(count):
            v = r[40 * i : 40 * i + 40] * (1.0 / 216.0)
            q_ref[6 + 8 * g + i] = v
            here = lane40 // 16 == i
            up = jnp.where(here, pltpu.roll(v, (16 * i - 64) % 128, 1), up)
            down = jnp.where(here, pltpu.roll(v, (16 * i - 11) % 128, 1), down)
        zs[0, g] = up
        zs[1, g] = down
        for copy in links_z(g):
            copy.start()

    gap = iota((256, 128), 0) % 128 - 12 - 2 * (iota((256, 128), 1) % 64 - 13)
    node = iota((256, 128), 1) % 64 - 13
    rz_m[...] = jnp.where((node >= -2) & (node <= 34), weight_of(gap), 0.0).astype(bf16)
    gap = iota((24, 96), 1) % 48 - 2 * iota((24, 96), 0) + 3
    ry_m[...] = jnp.where(iota((24, 96), 1) % 48 < 40, weight_of(gap), 0.0).astype(bf16)

    def shrink(g, carry):
        rows = []
        for i in range(4):
            first = 2 * (4 * g + i)
            near = q_ref[first + 2] + q_ref[first + 4]
            wide = q_ref[first] + q_ref[first + 6]
            rows.append(q_ref[first + 3] + 0.5625 * near - 0.0625 * wide)
        r = right_exact(jnp.concatenate(rows, 0), rz_m[...])
        r = jnp.concatenate([r[40 * i : 40 * i + 40] for i in range(4)], 1)
        r = jnp.concatenate([r, jnp.zeros((8, 512), f32)], 0)
        hi, lo = split(r)
        r = jnp.dot(ry_m[...], jnp.concatenate([hi, lo], 0), preferred_element_type=f32)
        for i in range(4):
            c_ref[4 * g + i] = r[:, 128 * i : 128 * i + 128]
        return carry

    ftap = [jnp.where(lane < 64, taps_ref[0, m], taps_ref[1, m]) for m in range(23)]
    gap = iota((128, 128), 0) - 12 - iota((128, 128), 1) % 64
    hi, lo = split(banded(gap, ftap, 11))
    cz_m[0:128] = hi
    cz_m[128:256] = hi
    cz_m[256:384] = lo
    row40 = iota((40, 128), 0)

    def make_my():
        off = jnp.where(lane40 < 40, lane40, jnp.where(lane40 < 56, lane40 - 52, lane40 - 24))
        gap = jnp.where(lane40 < 72, off - row40, 99)
        for t in range(2):
            full = banded(gap, [taps_ref[t, m] for m in range(23)], 11)
            hi = full.astype(bf16).astype(f32)
            lo = full - hi
            turned = pltpu.roll(hi, 80, 1)
            first = jnp.where(lane40 < 80, hi, turned)
            second = jnp.where(lane40 < 32, turned, pltpu.roll(lo, 32, 1))
            my_m[40 * t : 40 * t + 40] = jnp.concatenate([first, second], 1).astype(bf16)

    make_my()

    def conv_z(g):
        for copy in links_z(g):
            copy.wait()
        up = zr[0, g]
        down = zr[1, g]
        rows = []
        count = 8 if g < 4 else 4
        for i in range(count):
            v = q_ref[6 + 8 * g + i]
            v = v + jnp.where(lane40 < 16, pltpu.roll(up, (-16 * i) % 128, 1), 0.0)
            here = (lane40 >= 75) & (lane40 < 91)
            v = v + jnp.where(here, pltpu.roll(down, (75 - 16 * i) % 128, 1), 0.0)
            rows.append(v)
        r = right(jnp.concatenate(rows, 0), cz_m[0:256], cz_m[256:384])
        for i in range(count):
            part = r[40 * i : 40 * i + 40]
            a_ref[8 * g + i] = part
            ys[0, 8 * g + i] = part[20:36]
            ys[1, 8 * g + i] = part[0:16]
        for copy in links_y(g):
            copy.start()

    def conv_y(g):
        for copy in links_y(g):
            copy.wait()
        for h in range(4 if g < 4 else 2):
            both = []
            for p in range(2):
                x = 8 * g + 2 * h + p
                rows = [a_ref[x], yr[0, x], yr[1, x], jnp.zeros((8, 128), f32)]
                both.append(jnp.concatenate(rows, 0))
            hi, lo = split(jnp.concatenate(both, 1))
            stack = jnp.concatenate([hi, lo, hi], 0)
            r = jnp.dot(my_m[:, 0:240], stack, preferred_element_type=f32)
            for p in range(2):
                part = r[:, 128 * p : 128 * p + 128]
                ext[11 + 8 * g + 2 * h + p] = jnp.where(lane40 < 64, part[0:40], part[40:80])
        link_x(g).start()
    def flush(i):
        for odd in range(2):
            drain(i, odd)
        ts[...] = jnp.zeros_like(ts)

    lax.fori_loop(0, 8, step, 0)
    flush(7)
    pl.semaphore_wait(barrier, 6)
    close(0)
    shrink(0, 0)

    def slab(n, carry):
        lax.fori_loop(4 * n, 4 * n + 4, step, 0)

        @pl.when(n == 2)
        def _():
            flush(11)
            close(4)
            shrink(5, 0)
            conv_z(0)

        @pl.when(n == 3)
        def _():
            conv_z(4)
            conv_y(0)

        @pl.when(n == 4)
        def _():
            flush(19)
            close(3)
            shrink(4, 0)
            conv_y(4)

        @pl.when(n == 5)
        def _():
            conv_z(3)

        @pl.when(n == 6)
        def _():
            flush(27)
            close(1)
            shrink(1, 0)
            conv_y(3)

        return carry

    lax.fori_loop(2, 8, slab, 0)
    flush(31)
    close(2)
    shrink(2, 0)
    shrink(3, 0)
    for k in range(8):
        cxs[0, k] = jnp.where(lane24 < 64, c_ref[5 + k], c_ref[13 + k])
        cxs[1, k] = jnp.where(lane24 < 64, c_ref[k], c_ref[8 + k])
    cx_copies = [send("gx", k, cxs.at[k], cxr.at[k], csem, 0, k) for k in range(2)]

    conv_z(1)
    conv_z(2)
    conv_y(1)

    ctap = [jnp.where(lane < 64, taps_ref[2, m], taps_ref[3, m]) for m in range(23)]
    gap = iota((128, 128), 0) % 64 - iota((128, 128), 1) % 64 - 11
    gap = jnp.where(iota((128, 128), 0) // 64 == iota((128, 128), 1) // 64, gap, 99)
    hi, lo = split(banded(gap, ctap, 11))
    ccz_m[0:128] = hi
    ccz_m[128:256] = hi
    ccz_m[256:384] = lo
    for copy in cx_copies:
        copy.wait()
    for k in range(21):
        cext[11 + k] = c_ref[k]
    for s in range(2):
        for k in range(8):
            v = cxr[s, k]
            w = pltpu.roll(v, 64, 1)
            first = jnp.where(lane24 < 64, v, w)
            second = jnp.where(lane24 < 64, w, v)
            if s == 0:
                cext[k] = first
                if 8 + k >= 11:
                    cext[8 + k] += second
                else:
                    cext[8 + k] = second
            else:
                if 27 + k < 32:
                    cext[27 + k] += first
                else:
                    cext[27 + k] = first
                cext[35 + k] = second

    def conv_cx(c, carry):
        rows = pl.ds(pl.multiple_of(8 * c, 8), 8)
        for first in (0, 7, 14):
            acc = ctap[0] * cext[first : first + 7, rows, :]
            for m in range(1, 23):
                acc = acc + ctap[m] * cext[first + m : first + m + 7, rows, :]
            d_ref[first : first + 7, rows, :] = acc
        return carry

    lax.fori_loop(0, 3, conv_cx, 0)
    for j in range(21, 24):
        d_ref[j] = jnp.zeros((24, 128), f32)

    def pack_cz(g, carry):
        up = jnp.zeros((24, 128), f32)
        down = jnp.zeros((24, 128), f32)
        for i in range(4):
            v = d_ref[4 * g + i]
            here = half24 // 16 == i
            up = jnp.where(here, pltpu.roll(v, (16 * i - 32) % 128, 1), up)
            down = jnp.where(here, pltpu.roll(v, (16 * i - 11) % 128, 1), down)
        czs[0, g] = up
        czs[1, g] = down
        return carry

    lax.fori_loop(0, 6, pack_cz, 0, unroll=2)
    cz_copies = [send("gz", k, czs.at[k], czr.at[k], csem, 1, k) for k in range(2)]

    conv_y(2)

    for copy in cz_copies:
        copy.wait()

    def conv_cz(g, carry):
        up = czr[0, g]
        down = czr[1, g]
        rows = []
        for i in range(4):
            v = d_ref[4 * g + i]
            v = v + jnp.where(half24 < 16, pltpu.roll(up, (-16 * i) % 128, 1), 0.0)
            here = (half24 >= 43) & (half24 < 59)
            v = v + jnp.where(here, pltpu.roll(down, (43 - 16 * i) % 128, 1), 0.0)
            rows.append(v)
        r = right(jnp.concatenate(rows, 0), ccz_m[0:256], ccz_m[256:384])
        for i in range(4):
            part = r[24 * i : 24 * i + 24]
            e_ref[4 * g + i] = part
            cys[0, 4 * g + i] = part[5:21]
            cys[1, 4 * g + i] = part[0:16]
        return carry

    lax.fori_loop(0, 6, conv_cz, 0, unroll=2)
    own = pl.ds(0, 21)
    cy_copies = [send("gy", k, cys.at[k, own], cyr.at[k, own], csem, 2, k) for k in range(2)]

    spot = jnp.where(lane40 < 24, lane40 - 2, jnp.where(lane40 < 40, lane40 - 37, lane40 - 26))
    valid = ((lane40 < 21) | (lane40 >= 24)) & (lane40 < 56)
    gap = jnp.where(valid, 2 * spot - (row40 - 1), 99)
    for t in range(2):
        taps = []
        for d in range(-25, 26):
            total = 0.0
            for g, weight in ((0, 1.0), (1, 0.5625), (-1, 0.5625), (3, -0.0625), (-3, -0.0625)):
                if (d + g) % 2 == 0 and abs((d + g) // 2) <= 11:
                    total = total + weight * taps_ref[2 + t, (d + g) // 2 + 11]
            taps.append(total)
        full = banded(gap, taps, 25)
        hi = full.astype(bf16).astype(f32)
        first = jnp.where(lane40 < 64, hi, pltpu.roll(hi, 64, 1))
        cmy_m[40 * t : 40 * t + 40] = jnp.concatenate([first, full - hi], 1).astype(bf16)
    spot = iota((256, 128), 0) % 64 - 2
    point = iota((256, 128), 1)
    point = jnp.where(point == 127, -1, point)
    good = (spot <= 34) & (point <= 66)
    pz_m[...] = jnp.where(good, weight_of(point - 2 * spot), 0.0).astype(bf16)

    for g in (0, 1, 3, 4):
        link_x(g).wait()
    ext[3:11] = xr[0, 3:11]
    ext[11:15] += xr[0, 11:15]
    ext[43:47] += xr[1, 0:4]
    ext[47:58] = xr[1, 4:15]

    def conv_x(k, carry):
        rows = pl.ds(pl.multiple_of(8 * (k % 5), 8), 8)
        first = 12 * (2 - k // 5)
        acc = ftap[0] * ext[pl.ds(first, 12), rows, :]
        for m in range(1, 23):
            acc = acc + ftap[m] * ext[pl.ds(first + m, 12), rows, :]
        for i in range(12):
            part = acc[i]
            v_ref[first + i, rows, :] = part + pltpu.roll(part, 64, 1)
        return carry

    lax.fori_loop(0, 10, conv_x, 0)
    link_x(2).wait()
    ext[0:3] = xr[0, 0:3]
    lax.fori_loop(10, 15, conv_x, 0)
    for g in range(2):
        up = jnp.zeros((40, 128), f32)
        down = jnp.zeros((40, 128), f32)
        for i in range(32 if g == 0 else 4):
            v = v_ref[32 * g + i]
            here = lane40 // 4 == i
            up = jnp.where(here, pltpu.roll(v, (4 * i - 60) % 128, 1), up)
            down = jnp.where(here, pltpu.roll(v, (4 * i) % 128, 1), down)
        rs[0, g] = up
        rs[1, g] = down
    r_copies = [send("gz", k, rs.at[k], rr.at[k], rsem, k) for k in range(2)]

    for copy in cy_copies:
        copy.wait()

    def conv_cy(h, carry):
        both = []
        for p in range(2):
            j = 2 * h + p
            rows = [e_ref[j], cyr[0, j], cyr[1, j], jnp.zeros((8, 128), f32)]
            both.append(jnp.concatenate(rows, 0))
        hi, lo = split(jnp.concatenate(both, 1))
        stack = jnp.concatenate([hi, lo, hi], 0)
        r = jnp.dot(cmy_m[:, 0:192], stack, preferred_element_type=f32)
        parts = []
        for p in range(2):
            part = r[:, 128 * p : 128 * p + 128]
            parts.append(jnp.where(lane40 < 64, part[0:40], part[40:80]))
        r = right_exact(jnp.concatenate(parts, 0), pz_m[...])
        g_ref[2 * h] = r[0:40]
        g_ref[2 * h + 1] = r[40:80]
        return carry

    lax.fori_loop(0, 11, conv_cy, 0, unroll=11)
    for x in range(36):
        h = x // 2
        if x % 2:
            far = g_ref[h + 2]
        else:
            far = 0.5625 * (g_ref[h + 1] + g_ref[h + 2]) - 0.0625 * (g_ref[h] + g_ref[h + 3])
        v_ref[x] = jnp.where(lane40 < 64, v_ref[x], 0.0) + far
    for copy in r_copies:
        copy.wait()
    for x in range(36):
        g, i = x // 32, x % 32
        above = pltpu.roll(rr[1, g], (64 - 4 * i) % 128, 1)
        below = pltpu.roll(rr[0, g], (124 - 4 * i) % 128, 1)
        rim = jnp.where((lane40 >= 64) & (lane40 < 67), above, 0.0)
        v_ref[x] += jnp.where(lane40 == 127, below, rim)


def field(inv, counts, taps, charge, positions):
    def scratch(*shape):
        return pltpu.VMEM(shape, f32)

    return pl.pallas_call(
        field_kernel,
        out_shape=(
            jax.ShapeDtypeStruct((36, 40, 128), f32),
            jax.ShapeDtypeStruct((1024, 2, 8, 128), f32),
            jax.ShapeDtypeStruct((1024, 2, 16, 128), bf16),
        ),
        in_specs=[SMEM, SMEM, SMEM, VMEM, VMEM],
        out_specs=(VMEM, VMEM, VMEM),
        scratch_shapes=[
            scratch(2, 36, 32, 128),
            pltpu.VMEM((256, 128), bf16),
            scratch(32, 8, 128),
            scratch(2, 128, 128),
            scratch(54, 40, 128),
            scratch(2, 5, 40, 128),
            scratch(2, 5, 40, 128),
            scratch(40, 40, 128),
            scratch(2, 40, 16, 128),
            scratch(2, 40, 16, 128),
            scratch(2, 15, 40, 128),
            scratch(58, 40, 128),
            scratch(2, 2, 40, 128),
            scratch(2, 2, 40, 128),
            scratch(24, 24, 128),
            scratch(2, 8, 24, 128),
            scratch(2, 8, 24, 128),
            scratch(43, 24, 128),
            scratch(24, 24, 128),
            scratch(2, 6, 24, 128),
            scratch(2, 6, 24, 128),
            scratch(24, 24, 128),
            scratch(2, 24, 16, 128),
            scratch(2, 24, 16, 128),
            scratch(22, 40, 128),
            pltpu.VMEM((384, 128), bf16),
            pltpu.VMEM((80, 256), bf16),
            pltpu.VMEM((256, 128), bf16),
            pltpu.VMEM((24, 96), bf16),
            pltpu.VMEM((384, 128), bf16),
            pltpu.VMEM((80, 256), bf16),
            pltpu.VMEM((256, 128), bf16),
            pltpu.SemaphoreType.DMA((2, 5, 2)),
            pltpu.SemaphoreType.DMA((2, 5, 2)),
            pltpu.SemaphoreType.DMA((2, 5)),
            pltpu.SemaphoreType.DMA((2, 3, 2)),
            pltpu.SemaphoreType.DMA((2, 2)),
        ],
        compiler_params=pltpu.CompilerParams(
            collective_id=0, has_side_effects=True, vmem_limit_bytes=30 * 1024 * 1024
        ),
    )(inv, counts, taps, charge, positions)


def body(charge, positions, counts, corner, fine_taps, coarse_taps):
    ext_y = CY + 6
    ext_z = CZ + 6
    count = corner.shape[0]
    spots = np.arange(count, dtype=np.int32)
    along_y, along_z = CY // 4, CZ // 4
    cell_x, cell_y, cell_z = spots // (along_y * along_z), spots // along_z % along_y, spots % along_z
    wanted = ((4 * cell_x + 2) * ext_y + 4 * cell_y + 2) * ext_z + 4 * cell_z + 2
    same = corner[None, :] == wanted[:, None]
    number = lax.broadcasted_iota(jnp.int32, (count, count), 1)
    inv = jnp.sum(jnp.where(same, number, 0), axis=1, dtype=jnp.int32)
    live = jnp.sum(jnp.where(same, counts[None, :], 0), axis=1, dtype=jnp.int32)
    taps = jnp.concatenate([fine_taps, coarse_taps], 0)
    values, planes, depths = field(inv, live, taps, charge, positions)
    return sample(inv, live, planes, depths, values)


def solution(mesh):
    placed = (
        P(("gx", "gy", "gz"), None),
        P(None, ("gx", "gy", "gz"), None),
        P(("gx", "gy", "gz")),
        P(("gx", "gy", "gz")),
        P(),
        P(),
    )
    return jax.shard_map(
        body,
        mesh=mesh,
        in_specs=placed,
        out_specs=(P(("gx", "gy", "gz"), None), P("gx", "gy", "gz")),
        check_vma=False,
    )
```

```python
import jax
import jax.numpy as jnp
import numpy as np
from jax import lax
from jax.experimental import pallas as pl
from jax.experimental.pallas import tpu as pltpu
from jax.sharding import PartitionSpec as P

CX = 32
CY = 32
CZ = 64
f32 = jnp.float32
bf16 = jnp.bfloat16


def split(v):
    hi = v.astype(bf16)
    return hi, (v - hi.astype(f32)).astype(bf16)


def spline8(u, node):
    m = jnp.abs(u - node)
    t = jnp.maximum(2.0 - m, 0.0)
    v = jnp.maximum(1.0 - m, 0.0)
    return t * t * t - 4.0 * (v * v * v)


def row8(ref, lead, n):
    v = ref[pl.ds(n, 1), :] if lead is None else ref[lead, pl.ds(n, 1), :]
    return jnp.broadcast_to(v, (8, 128))


def row8_at(ref, at, a):
    return jnp.broadcast_to(ref[at, 0, a : a + 1, :], (8, 128))


SMEM = pl.BlockSpec(memory_space=pltpu.SMEM)
VMEM = pl.BlockSpec(memory_space=pltpu.VMEM)


def sample_kernel(inv_ref, cnt_ref, xy_ref, z_ref, v_ref, out_ref, grid_ref, vs, place):
    lane = lax.broadcasted_iota(jnp.int32, (1, 128), 1)

    lin = lax.broadcasted_iota(jnp.int32, (256, 1024), 0)
    out = lax.broadcasted_iota(jnp.int32, (256, 1024), 1)
    within = out % 128
    z = (8 * (out // 128) + 4 * (within // 8 % 2) + within % 8 - 1) % 128
    part = within // 16
    hit = (z == lin % 128) & (part < 3) & ((part == 1) == (lin >= 128))
    place[...] = jnp.where(hit, 1.0, 0.0).astype(bf16)

    def open_rows(g, carry):
        rows = []
        for i in range(4):
            rows.append(v_ref[4 * g + i])
        hi, lo = split(jnp.concatenate(rows, 0) * (1.0 / 216.0))
        both = jnp.concatenate([hi, lo], 1)
        for k in range(0, 8, 2):
            r = jnp.dot(both, place[:, 128 * k : 128 * k + 256], preferred_element_type=f32)
            for i in range(4):
                for p in range(2):
                    here = r[40 * i : 40 * i + 40, 128 * p : 128 * p + 128]
                    vs[0, k + p, 4 * g + i] = here[0:32]
                    vs[1, k + p, 4 * g + i] = here[4:36]
        return carry

    lax.fori_loop(0, 9, open_rows, 0, unroll=3)
    for x in range(32):
        grid_ref[x] = v_ref[x + 1, 1:33, 0:64]

    def one(cx, start, odd, row):
        for k in range(8):
            spot = pl.ds(pl.multiple_of(start, 8), 8)
            left = vs[odd, k, pl.ds(4 * cx, 8), spot, :].reshape(64, 128).astype(bf16)
            at = row * 16 + 2 * k
            hi = jnp.concatenate([z_ref[at, 0], z_ref[at + 1, 0]], 1)
            lo = jnp.concatenate([z_ref[at, 1], z_ref[at + 1, 1]], 1)
            right_side = jnp.concatenate([hi, hi, lo], 0)
            f = jnp.dot(left[:, 0:48], right_side, preferred_element_type=f32)
            for p in range(2):
                here = slice(p * 128, p * 128 + 128)
                g = row8_at(xy_ref, at + p, 0) * f[0:8, here]
                for a in range(1, 8):
                    g = g + row8_at(xy_ref, at + p, a) * f[8 * a : 8 * a + 8, here]
                r = jnp.sum(g * xy_ref[at + p, 1], axis=0, keepdims=True)
                out_ref[pl.ds(inv_ref[at + p], 1), :] = jnp.where(lane < cnt_ref[at + p], r, 0.0)

    def step(i, carry):
        cx = i // 4
        start = (i % 4) * 8
        one(cx, start, 0, 2 * i)
        one(cx, start, 1, 2 * i + 1)
        return carry

    lax.fori_loop(0, 32, step, 0, unroll=4)


def sample(inv, counts, planes, depths, grid):
    return pl.pallas_call(
        sample_kernel,
        out_shape=(
            jax.ShapeDtypeStruct((1024, 128), f32),
            jax.ShapeDtypeStruct((32, 32, 64), f32),
        ),
        in_specs=[SMEM, SMEM, VMEM, VMEM, VMEM],
        out_specs=(VMEM, VMEM),
        scratch_shapes=[
            pltpu.VMEM((2, 8, 36, 32, 128), f32),
            pltpu.VMEM((256, 1024), bf16),
        ],
        compiler_params=pltpu.CompilerParams(vmem_limit_bytes=32 * 1024 * 1024),
    )(inv, counts, planes, depths, grid)


MESH = pl.DeviceIdType.MESH


def iota(shape, dim):
    return lax.broadcasted_iota(jnp.int32, shape, dim)


def weight_of(gap):
    size = jnp.abs(gap)
    return jnp.where(
        size == 0, 1.0, jnp.where(size == 1, 0.5625, jnp.where(size == 3, -0.0625, 0.0))
    )


def banded(gap, values, reach):
    total = jnp.zeros(gap.shape, f32)
    for m in range(-reach, reach + 1):
        total = jnp.where(gap == m, values[m + reach], total)
    return total


def right(v, twice, rest):
    hi, lo = split(v)
    r = jnp.dot(jnp.concatenate([hi, lo], 1), twice, preferred_element_type=f32)
    return r + jnp.dot(hi, rest, preferred_element_type=f32)


def right_exact(v, twice):
    hi, lo = split(v)
    return jnp.dot(jnp.concatenate([hi, lo], 1), twice, preferred_element_type=f32)


def field_kernel(
    inv_ref, cnt_ref, taps_ref, charge_ref, pos_ref, v_ref, xy_ref, z_ref,
    acc, place, qs, ts, q_ref,
    zs, zr, a_ref, ys, yr, xr, ext, rs, rr,
    c_ref, cxs, cxr, cext, d_ref, czs, czr, e_ref, cys, cyr, g_ref,
    cz_m, my_m, rz_m, ry_m, ccz_m, cmy_m, pz_m,
    zsem, ysem, xsem, csem, rsem,
):
    ids = {name: lax.axis_index(name) for name in ("gx", "gy", "gz")}
    size_of = {"gx": 4, "gy": 4, "gz": 8}

    def away(name, step):
        count = size_of[name]
        return {name: lax.rem(ids[name] + (step + count), count)}

    for s in range(2):
        for j in range(21, 24):
            cyr[s, j] = jnp.zeros((16, 128), f32)
    barrier = pltpu.get_barrier_semaphore()
    for name in ("gx", "gy", "gz"):
        for step in (1, -1):
            pl.semaphore_signal(barrier, inc=1, device_id=away(name, step), device_id_type=MESH)

    lane = iota((1, 128), 1)
    lane40 = iota((40, 128), 1)
    lane24 = iota((24, 128), 1)
    half24 = lane24 % 64

    def link(name, k, src, dst, sems, *spot):
        return pltpu.make_async_remote_copy(
            src_ref=src,
            dst_ref=dst,
            send_sem=sems.at[(0, *spot)],
            recv_sem=sems.at[(1, *spot)],
            device_id=away(name, 1 - 2 * k),
            device_id_type=MESH,
        )

    def send(*args):
        copy = link(*args)
        copy.start()
        return copy

    def links_z(g):
        return [link("gz", k, zs.at[k, g], zr.at[k, g], zsem, g, k) for k in range(2)]

    def links_y(g):
        own = pl.ds(8 * g, 8 if g < 4 else 4)
        return [link("gy", k, ys.at[k, own], yr.at[k, own], ysem, g, k) for k in range(2)]

    pieces = {0: (1, 0, 8), 1: (1, 8, 15), 2: (0, 21, 24), 3: (0, 24, 32), 4: (0, 32, 36)}

    def link_x(g):
        k, low, high = pieces[g]
        base = 0 if k else 21
        src = ext.at[pl.ds(11 + low, high - low)]
        dst = xr.at[k, pl.ds(low - base, high - low)]
        return link("gx", k, src, dst, xsem, g)

    knot = iota((8, 128), 0).astype(f32) - 1.0
    lane8 = iota((8, 128), 1)
    zero = jnp.zeros((8, 128), f32)
    acc[...] = jnp.zeros_like(acc)
    ts[...] = jnp.zeros_like(ts)
    for x in range(6):
        q_ref[x] = jnp.zeros((40, 128), f32)
    for x in range(42, 54):
        q_ref[x] = jnp.zeros((40, 128), f32)

    def cell(row, cz, spot):
        at = row * 16 + cz
        n = inv_ref[at]
        q = jnp.where(lane8 < cnt_ref[at], row8(charge_ref, None, n), 0.0)
        wx = spline8(row8(pos_ref, 0, n), knot)
        wy = spline8(row8(pos_ref, 1, n), knot)
        wz = spline8(row8(pos_ref, 2, n), knot)
        xy_ref[at, 0] = wx
        xy_ref[at, 1] = wy
        qs[spot] = q * wx
        prod = jnp.concatenate([row8(qs, spot, a) * wy for a in range(8)], axis=0)
        tile = jnp.concatenate([zero, wz] if cz % 2 else [wz, zero], axis=0)
        hi, lo = split(tile)
        z_ref[at, 0] = hi
        z_ref[at, 1] = lo
        return split(prod), (hi, lo)

    def line(odd, row):
        parts = []
        for k in range(8):
            (ah, al), (bh, bl) = cell(row, 2 * k, 16 * odd + 2 * k)
            (ch, cl), (dh, dl) = cell(row, 2 * k + 1, 16 * odd + 2 * k + 1)
            left = jnp.concatenate(
                [jnp.concatenate([ah, ch], 1), jnp.concatenate([al, cl], 1)], 0
            )
            down = jnp.concatenate(
                [jnp.concatenate([bh, dh], 1), jnp.concatenate([bl, dl], 1)], 0
            )
            r = lax.dot_general(down, left, (((1,), (1,)), ((), ())), preferred_element_type=f32)
            parts.append(r[0:16] + r[16:32])
        ts[odd] = jnp.concatenate(parts, 0)

    def slab_of(n):
        late = jnp.minimum(n // 2, 1)
        last = jnp.minimum(n // 5, 1)
        return n + (late - last) * (9 - 2 * n) - 3 * last

    def drain(i, odd):
        spot = pl.ds(pl.multiple_of(i % 4 * 8, 8), 8)
        t = ts[odd].T
        t = t[0:64] + t[64:128]
        for a in range(8):
            acc[odd, 4 * slab_of(i // 4) + a, spot, :] += t[8 * a : 8 * a + 8]

    def step(i, carry):
        before = jnp.maximum(i - 1, 0)
        drain(before, 0)
        drain(before, 1)
        row = 8 * slab_of(i // 4) + 2 * (i % 4)
        line(0, row)
        line(1, row + 1)
        return carry

    lin = iota((256, 128), 0) % 128
    place[...] = jnp.where(4 * (lin // 8) + lin % 8 + 11 == iota((256, 128), 1), 1.0, 0.0).astype(bf16)

    def close(g):
        count = 8 if g < 4 else 4
        joined = []
        for i in range(count):
            x = 8 * g + i
            pad = jnp.zeros((4, 128), f32)
            even = jnp.concatenate([acc[0, x], pad, pad], 0)
            odd = jnp.concatenate([pad, acc[1, x], pad], 0)
            joined.append(even + odd)
        hi, lo = split(jnp.concatenate(joined, 0))
        r = jnp.dot(jnp.concatenate([hi, lo], 1), place[...], preferred_element_type=f32)
        up = jnp.zeros((40, 128), f32)
        down = jnp.zeros((40, 128), f32)
        for i in range(count):
            v = r[40 * i : 40 * i + 40] * (1.0 / 216.0)
            q_ref[6 + 8 * g + i] = v
            here = lane40 // 16 == i
            up = jnp.where(here, pltpu.roll(v, (16 * i - 64) % 128, 1), up)
            down = jnp.where(here, pltpu.roll(v, (16 * i - 11) % 128, 1), down)
        zs[0, g] = up
        zs[1, g] = down
        for copy in links_z(g):
            copy.start()

    gap = iota((256, 128), 0) % 128 - 12 - 2 * (iota((256, 128), 1) % 64 - 13)
    node = iota((256, 128), 1) % 64 - 13
    rz_m[...] = jnp.where((node >= -2) & (node <= 34), weight_of(gap), 0.0).astype(bf16)
    gap = iota((24, 96), 1) % 48 - 2 * iota((24, 96), 0) + 3
    ry_m[...] = jnp.where(iota((24, 96), 1) % 48 < 40, weight_of(gap), 0.0).astype(bf16)

    def shrink(g, carry):
        rows = []
        for i in range(4):
            first = 2 * (4 * g + i)
            near = q_ref[first + 2] + q_ref[first + 4]
            wide = q_ref[first] + q_ref[first + 6]
            rows.append(q_ref[first + 3] + 0.5625 * near - 0.0625 * wide)
        r = right_exact(jnp.concatenate(rows, 0), rz_m[...])
        r = jnp.concatenate([r[40 * i : 40 * i + 40] for i in range(4)], 1)
        r = jnp.concatenate([r, jnp.zeros((8, 512), f32)], 0)
        hi, lo = split(r)
        r = jnp.dot(ry_m[...], jnp.concatenate([hi, lo], 0), preferred_element_type=f32)
        for i in range(4):
            c_ref[4 * g + i] = r[:, 128 * i : 128 * i + 128]
        return carry

    ftap = [jnp.where(lane < 64, taps_ref[0, m], taps_ref[1, m]) for m in range(23)]
    gap = iota((128, 128), 0) - 12 - iota((128, 128), 1) % 64
    hi, lo = split(banded(gap, ftap, 11))
    cz_m[0:128] = hi
    cz_m[128:256] = hi
    cz_m[256:384] = lo
    row40 = iota((40, 128), 0)

    def make_my():
        off = jnp.where(lane40 < 40, lane40, jnp.where(lane40 < 56, lane40 - 52, lane40 - 24))
        gap = jnp.where(lane40 < 72, off - row40, 99)
        for t in range(2):
            full = banded(gap, [taps_ref[t, m] for m in range(23)], 11)
            hi = full.astype(bf16).astype(f32)
            lo = full - hi
            turned = pltpu.roll(hi, 80, 1)
            first = jnp.where(lane40 < 80, hi, turned)
            second = jnp.where(lane40 < 32, turned, pltpu.roll(lo, 32, 1))
            my_m[40 * t : 40 * t + 40] = jnp.concatenate([first, second], 1).astype(bf16)

    make_my()

    def conv_z(g):
        for copy in links_z(g):
            copy.wait()
        up = zr[0, g]
        down = zr[1, g]
        rows = []
        count = 8 if g < 4 else 4
        for i in range(count):
            v = q_ref[6 + 8 * g + i]
            v = v + jnp.where(lane40 < 16, pltpu.roll(up, (-16 * i) % 128, 1), 0.0)
            here = (lane40 >= 75) & (lane40 < 91)
            v = v + jnp.where(here, pltpu.roll(down, (75 - 16 * i) % 128, 1), 0.0)
            rows.append(v)
        r = right(jnp.concatenate(rows, 0), cz_m[0:256], cz_m[256:384])
        for i in range(count):
            part = r[40 * i : 40 * i + 40]
            a_ref[8 * g + i] = part
            ys[0, 8 * g + i] = part[20:36]
            ys[1, 8 * g + i] = part[0:16]
        for copy in links_y(g):
            copy.start()

    def conv_y(g):
        for copy in links_y(g):
            copy.wait()
        for h in range(4 if g < 4 else 2):
            both = []
            for p in range(2):
                x = 8 * g + 2 * h + p
                rows = [a_ref[x], yr[0, x], yr[1, x], jnp.zeros((8, 128), f32)]
                both.append(jnp.concatenate(rows, 0))
            hi, lo = split(jnp.concatenate(both, 1))
            stack = jnp.concatenate([hi, lo, hi], 0)
            r = jnp.dot(my_m[:, 0:240], stack, preferred_element_type=f32)
            for p in range(2):
                part = r[:, 128 * p : 128 * p + 128]
                ext[11 + 8 * g + 2 * h + p] = jnp.where(lane40 < 64, part[0:40], part[40:80])
        link_x(g).start()
    def flush(i):
        for odd in range(2):
            drain(i, odd)
        ts[...] = jnp.zeros_like(ts)

    lax.fori_loop(0, 8, step, 0, unroll=2)
    flush(7)
    pl.semaphore_wait(barrier, 6)
    close(0)
    shrink(0, 0)

    def slab(n, carry):
        lax.fori_loop(0, 2, lambda m, c: step(4 * n + 2 * m + 1, step(4 * n + 2 * m, c)), 0)

        @pl.when(n == 2)
        def _():
            flush(11)
            close(4)
            shrink(5, 0)

        @pl.when(n == 3)
        def _():
            conv_z(0)

        @pl.when(n == 4)
        def _():
            flush(19)
            close(3)
            shrink(4, 0)
            conv_z(4)

        @pl.when(n == 5)
        def _():
            conv_y(0)

        @pl.when(n == 6)
        def _():
            flush(27)
            close(1)
            shrink(1, 0)
            conv_z(3)
            conv_y(4)

        return carry

    lax.fori_loop(2, 8, slab, 0)
    flush(31)
    close(2)
    shrink(2, 0)
    shrink(3, 0)
    for k in range(8):
        cxs[0, k] = jnp.where(lane24 < 64, c_ref[5 + k], c_ref[13 + k])
        cxs[1, k] = jnp.where(lane24 < 64, c_ref[k], c_ref[8 + k])
    cx_copies = [send("gx", k, cxs.at[k], cxr.at[k], csem, 0, k) for k in range(2)]

    conv_z(1)
    conv_y(3)
    conv_z(2)

    ctap = [jnp.where(lane < 64, taps_ref[2, m], taps_ref[3, m]) for m in range(23)]
    gap = iota((128, 128), 0) % 64 - iota((128, 128), 1) % 64 - 11
    gap = jnp.where(iota((128, 128), 0) // 64 == iota((128, 128), 1) // 64, gap, 99)
    hi, lo = split(banded(gap, ctap, 11))
    ccz_m[0:128] = hi
    ccz_m[128:256] = hi
    ccz_m[256:384] = lo
    for copy in cx_copies:
        copy.wait()
    for k in range(21):
        cext[11 + k] = c_ref[k]
    for s in range(2):
        for k in range(8):
            v = cxr[s, k]
            w = pltpu.roll(v, 64, 1)
            first = jnp.where(lane24 < 64, v, w)
            second = jnp.where(lane24 < 64, w, v)
            if s == 0:
                cext[k] = first
                if 8 + k >= 11:
                    cext[8 + k] += second
                else:
                    cext[8 + k] = second
            else:
                if 27 + k < 32:
                    cext[27 + k] += first
                else:
                    cext[27 + k] = first
                cext[35 + k] = second

    def conv_cx(c, carry):
        rows = pl.ds(pl.multiple_of(8 * c, 8), 8)
        for first in (0, 7, 14):
            acc = ctap[0] * cext[first : first + 7, rows, :]
            for m in range(1, 23):
                acc = acc + ctap[m] * cext[first + m : first + m + 7, rows, :]
            d_ref[first : first + 7, rows, :] = acc
        return carry

    lax.fori_loop(0, 3, conv_cx, 0)
    for j in range(21, 24):
        d_ref[j] = jnp.zeros((24, 128), f32)

    def pack_cz(g, carry):
        up = jnp.zeros((24, 128), f32)
        down = jnp.zeros((24, 128), f32)
        for i in range(4):
            v = d_ref[4 * g + i]
            here = half24 // 16 == i
            up = jnp.where(here, pltpu.roll(v, (16 * i - 32) % 128, 1), up)
            down = jnp.where(here, pltpu.roll(v, (16 * i - 11) % 128, 1), down)
        czs[0, g] = up
        czs[1, g] = down
        return carry

    lax.fori_loop(0, 6, pack_cz, 0, unroll=2)
    cz_copies = [send("gz", k, czs.at[k], czr.at[k], csem, 1, k) for k in range(2)]

    conv_y(1)
    conv_y(2)

    for copy in cz_copies:
        copy.wait()

    def conv_cz(g, carry):
        up = czr[0, g]
        down = czr[1, g]
        rows = []
        for i in range(4):
            v = d_ref[4 * g + i]
            v = v + jnp.where(half24 < 16, pltpu.roll(up, (-16 * i) % 128, 1), 0.0)
            here = (half24 >= 43) & (half24 < 59)
            v = v + jnp.where(here, pltpu.roll(down, (43 - 16 * i) % 128, 1), 0.0)
            rows.append(v)
        r = right(jnp.concatenate(rows, 0), ccz_m[0:256], ccz_m[256:384])
        for i in range(4):
            part = r[24 * i : 24 * i + 24]
            e_ref[4 * g + i] = part
            cys[0, 4 * g + i] = part[5:21]
            cys[1, 4 * g + i] = part[0:16]
        return carry

    lax.fori_loop(0, 6, conv_cz, 0, unroll=2)
    own = pl.ds(0, 21)
    cy_copies = [send("gy", k, cys.at[k, own], cyr.at[k, own], csem, 2, k) for k in range(2)]

    spot = jnp.where(lane40 < 24, lane40 - 2, jnp.where(lane40 < 40, lane40 - 37, lane40 - 26))
    valid = ((lane40 < 21) | (lane40 >= 24)) & (lane40 < 56)
    gap = jnp.where(valid, 2 * spot - (row40 - 1), 99)
    for t in range(2):
        taps = []
        for d in range(-25, 26):
            total = 0.0
            for g, weight in ((0, 1.0), (1, 0.5625), (-1, 0.5625), (3, -0.0625), (-3, -0.0625)):
                if (d + g) % 2 == 0 and abs((d + g) // 2) <= 11:
                    total = total + weight * taps_ref[2 + t, (d + g) // 2 + 11]
            taps.append(total)
        full = banded(gap, taps, 25)
        hi = full.astype(bf16).astype(f32)
        first = jnp.where(lane40 < 64, hi, pltpu.roll(hi, 64, 1))
        cmy_m[40 * t : 40 * t + 40] = jnp.concatenate([first, full - hi], 1).astype(bf16)
    spot = iota((256, 128), 0) % 64 - 2
    point = iota((256, 128), 1)
    point = jnp.where(point == 127, -1, point)
    good = (spot <= 34) & (point <= 66)
    pz_m[...] = jnp.where(good, weight_of(point - 2 * spot), 0.0).astype(bf16)

    for g in (0, 1, 3, 4):
        link_x(g).wait()
    ext[3:11] = xr[0, 3:11]
    ext[11:15] += xr[0, 11:15]
    ext[43:47] += xr[1, 0:4]
    ext[47:58] = xr[1, 4:15]

    def conv_x(k, carry):
        rows = pl.ds(pl.multiple_of(8 * (k % 5), 8), 8)
        first = 12 * (2 - k // 5)
        acc = ftap[0] * ext[pl.ds(first, 12), rows, :]
        for m in range(1, 23):
            acc = acc + ftap[m] * ext[pl.ds(first + m, 12), rows, :]
        for i in range(12):
            part = acc[i]
            v_ref[first + i, rows, :] = part + pltpu.roll(part, 64, 1)
        return carry

    lax.fori_loop(0, 10, conv_x, 0)
    link_x(2).wait()
    ext[0:3] = xr[0, 0:3]
    lax.fori_loop(10, 15, conv_x, 0)
    for g in range(2):
        up = jnp.zeros((40, 128), f32)
        down = jnp.zeros((40, 128), f32)
        for i in range(32 if g == 0 else 4):
            v = v_ref[32 * g + i]
            here = lane40 // 4 == i
            up = jnp.where(here, pltpu.roll(v, (4 * i - 60) % 128, 1), up)
            down = jnp.where(here, pltpu.roll(v, (4 * i) % 128, 1), down)
        rs[0, g] = up
        rs[1, g] = down
    r_copies = [send("gz", k, rs.at[k], rr.at[k], rsem, k) for k in range(2)]

    for copy in cy_copies:
        copy.wait()

    def conv_cy(h, carry):
        both = []
        for p in range(2):
            j = 2 * h + p
            rows = [e_ref[j], cyr[0, j], cyr[1, j], jnp.zeros((8, 128), f32)]
            both.append(jnp.concatenate(rows, 0))
        hi, lo = split(jnp.concatenate(both, 1))
        stack = jnp.concatenate([hi, lo, hi], 0)
        r = jnp.dot(cmy_m[:, 0:192], stack, preferred_element_type=f32)
        parts = []
        for p in range(2):
            part = r[:, 128 * p : 128 * p + 128]
            parts.append(jnp.where(lane40 < 64, part[0:40], part[40:80]))
        r = right_exact(jnp.concatenate(parts, 0), pz_m[...])
        g_ref[2 * h] = r[0:40]
        g_ref[2 * h + 1] = r[40:80]
        return carry

    lax.fori_loop(0, 11, conv_cy, 0, unroll=11)
    for x in range(36):
        h = x // 2
        if x % 2:
            far = g_ref[h + 2]
        else:
            far = 0.5625 * (g_ref[h + 1] + g_ref[h + 2]) - 0.0625 * (g_ref[h] + g_ref[h + 3])
        v_ref[x] = jnp.where(lane40 < 64, v_ref[x], 0.0) + far
    for copy in r_copies:
        copy.wait()
    for x in range(36):
        g, i = x // 32, x % 32
        above = pltpu.roll(rr[1, g], (64 - 4 * i) % 128, 1)
        below = pltpu.roll(rr[0, g], (124 - 4 * i) % 128, 1)
        rim = jnp.where((lane40 >= 64) & (lane40 < 67), above, 0.0)
        v_ref[x] += jnp.where(lane40 == 127, below, rim)


def field(inv, counts, taps, charge, positions):
    def scratch(*shape):
        return pltpu.VMEM(shape, f32)

    return pl.pallas_call(
        field_kernel,
        out_shape=(
            jax.ShapeDtypeStruct((36, 40, 128), f32),
            jax.ShapeDtypeStruct((1024, 2, 8, 128), f32),
            jax.ShapeDtypeStruct((1024, 2, 16, 128), bf16),
        ),
        in_specs=[SMEM, SMEM, SMEM, VMEM, VMEM],
        out_specs=(VMEM, VMEM, VMEM),
        scratch_shapes=[
            scratch(2, 36, 32, 128),
            pltpu.VMEM((256, 128), bf16),
            scratch(32, 8, 128),
            scratch(2, 128, 128),
            scratch(54, 40, 128),
            scratch(2, 5, 40, 128),
            scratch(2, 5, 40, 128),
            scratch(40, 40, 128),
            scratch(2, 40, 16, 128),
            scratch(2, 40, 16, 128),
            scratch(2, 15, 40, 128),
            scratch(58, 40, 128),
            scratch(2, 2, 40, 128),
            scratch(2, 2, 40, 128),
            scratch(24, 24, 128),
            scratch(2, 8, 24, 128),
            scratch(2, 8, 24, 128),
            scratch(43, 24, 128),
            scratch(24, 24, 128),
            scratch(2, 6, 24, 128),
            scratch(2, 6, 24, 128),
            scratch(24, 24, 128),
            scratch(2, 24, 16, 128),
            scratch(2, 24, 16, 128),
            scratch(22, 40, 128),
            pltpu.VMEM((384, 128), bf16),
            pltpu.VMEM((80, 256), bf16),
            pltpu.VMEM((256, 128), bf16),
            pltpu.VMEM((24, 96), bf16),
            pltpu.VMEM((384, 128), bf16),
            pltpu.VMEM((80, 256), bf16),
            pltpu.VMEM((256, 128), bf16),
            pltpu.SemaphoreType.DMA((2, 5, 2)),
            pltpu.SemaphoreType.DMA((2, 5, 2)),
            pltpu.SemaphoreType.DMA((2, 5)),
            pltpu.SemaphoreType.DMA((2, 3, 2)),
            pltpu.SemaphoreType.DMA((2, 2)),
        ],
        compiler_params=pltpu.CompilerParams(
            collective_id=0, has_side_effects=True, vmem_limit_bytes=30 * 1024 * 1024
        ),
    )(inv, counts, taps, charge, positions)


def body(charge, positions, counts, corner, fine_taps, coarse_taps):
    ext_y = CY + 6
    ext_z = CZ + 6
    count = corner.shape[0]
    spots = np.arange(count, dtype=np.int32)
    along_y, along_z = CY // 4, CZ // 4
    cell_x, cell_y, cell_z = spots // (along_y * along_z), spots // along_z % along_y, spots % along_z
    wanted = ((4 * cell_x + 2) * ext_y + 4 * cell_y + 2) * ext_z + 4 * cell_z + 2
    same = corner[:, None] == wanted[None, :]
    number = lax.broadcasted_iota(jnp.int32, (count, count), 0)
    inv = jnp.sum(jnp.where(same, number, 0), axis=0, dtype=jnp.int32)
    live = jnp.sum(jnp.where(same, counts[:, None], 0), axis=0, dtype=jnp.int32)
    taps = jnp.concatenate([fine_taps, coarse_taps], 0)
    values, planes, depths = field(inv, live, taps, charge, positions)
    return sample(inv, live, planes, depths, values)


def solution(mesh):
    placed = (
        P(("gx", "gy", "gz"), None),
        P(None, ("gx", "gy", "gz"), None),
        P(("gx", "gy", "gz")),
        P(("gx", "gy", "gz")),
        P(),
        P(),
    )
    return jax.shard_map(
        body,
        mesh=mesh,
        in_specs=placed,
        out_specs=(P(("gx", "gy", "gz"), None), P("gx", "gy", "gz")),
        check_vma=False,
    )
```

```python
import jax
import jax.numpy as jnp
import numpy as np
from jax import lax
from jax.experimental import pallas as pl
from jax.experimental.pallas import tpu as pltpu
from jax.sharding import PartitionSpec as P

CX = 32
CY = 32
CZ = 64
f32 = jnp.float32
bf16 = jnp.bfloat16


def split(v):
    hi = v.astype(bf16)
    return hi, (v - hi.astype(f32)).astype(bf16)


def spline8(u, node):
    m = jnp.abs(u - node)
    t = jnp.maximum(2.0 - m, 0.0)
    v = jnp.maximum(1.0 - m, 0.0)
    return t * t * t - 4.0 * (v * v * v)


def row8(ref, lead, n):
    v = ref[pl.ds(n, 1), :] if lead is None else ref[lead, pl.ds(n, 1), :]
    return jnp.broadcast_to(v, (8, 128))


def row8_at(ref, at, a):
    return jnp.broadcast_to(ref[at, 0, a : a + 1, :], (8, 128))


SMEM = pl.BlockSpec(memory_space=pltpu.SMEM)
VMEM = pl.BlockSpec(memory_space=pltpu.VMEM)


def sample_kernel(inv_ref, cnt_ref, xy_ref, z_ref, v_ref, out_ref, grid_ref, vs, place):
    lane = lax.broadcasted_iota(jnp.int32, (1, 128), 1)

    lin = lax.broadcasted_iota(jnp.int32, (256, 1024), 0)
    out = lax.broadcasted_iota(jnp.int32, (256, 1024), 1)
    within = out % 128
    z = (8 * (out // 128) + 4 * (within // 8 % 2) + within % 8 - 1) % 128
    part = within // 16
    hit = (z == lin % 128) & (part < 3) & ((part == 1) == (lin >= 128))
    place[...] = jnp.where(hit, 1.0, 0.0).astype(bf16)

    def open_rows(g, carry):
        rows = []
        for i in range(4):
            rows.append(v_ref[4 * g + i])
        hi, lo = split(jnp.concatenate(rows, 0) * (1.0 / 216.0))
        both = jnp.concatenate([hi, lo], 1)
        for k in range(0, 8, 2):
            r = jnp.dot(both, place[:, 128 * k : 128 * k + 256], preferred_element_type=f32)
            for i in range(4):
                for p in range(2):
                    here = r[40 * i : 40 * i + 40, 128 * p : 128 * p + 128]
                    vs[0, k + p, 4 * g + i] = here[0:32]
                    vs[1, k + p, 4 * g + i] = here[4:36]
        return carry

    lax.fori_loop(0, 9, open_rows, 0, unroll=3)
    for x in range(32):
        grid_ref[x] = v_ref[x + 1, 1:33, 0:64]

    def one(cx, start, odd, row):
        for k in range(8):
            spot = pl.ds(pl.multiple_of(start, 8), 8)
            left = vs[odd, k, pl.ds(4 * cx, 8), spot, :].reshape(64, 128).astype(bf16)
            at = row * 16 + 2 * k
            hi = jnp.concatenate([z_ref[at, 0], z_ref[at + 1, 0]], 1)
            lo = jnp.concatenate([z_ref[at, 1], z_ref[at + 1, 1]], 1)
            right_side = jnp.concatenate([hi, hi, lo], 0)
            f = jnp.dot(left[:, 0:48], right_side, preferred_element_type=f32)
            for p in range(2):
                here = slice(p * 128, p * 128 + 128)
                g = row8_at(xy_ref, at + p, 0) * f[0:8, here]
                for a in range(1, 8):
                    g = g + row8_at(xy_ref, at + p, a) * f[8 * a : 8 * a + 8, here]
                r = jnp.sum(g * xy_ref[at + p, 1], axis=0, keepdims=True)
                out_ref[pl.ds(inv_ref[at + p], 1), :] = jnp.where(lane < cnt_ref[at + p], r, 0.0)

    def step(i, carry):
        cx = i // 4
        start = (i % 4) * 8
        one(cx, start, 0, 2 * i)
        one(cx, start, 1, 2 * i + 1)
        return carry

    lax.fori_loop(0, 32, step, 0, unroll=8)


def sample(inv, counts, planes, depths, grid):
    return pl.pallas_call(
        sample_kernel,
        out_shape=(
            jax.ShapeDtypeStruct((1024, 128), f32),
            jax.ShapeDtypeStruct((32, 32, 64), f32),
        ),
        in_specs=[SMEM, SMEM, VMEM, VMEM, VMEM],
        out_specs=(VMEM, VMEM),
        scratch_shapes=[
            pltpu.VMEM((2, 8, 36, 32, 128), f32),
            pltpu.VMEM((256, 1024), bf16),
        ],
        compiler_params=pltpu.CompilerParams(vmem_limit_bytes=32 * 1024 * 1024),
    )(inv, counts, planes, depths, grid)


MESH = pl.DeviceIdType.MESH


def iota(shape, dim):
    return lax.broadcasted_iota(jnp.int32, shape, dim)


def weight_of(gap):
    size = jnp.abs(gap)
    return jnp.where(
        size == 0, 1.0, jnp.where(size == 1, 0.5625, jnp.where(size == 3, -0.0625, 0.0))
    )


def banded(gap, values, reach):
    total = jnp.zeros(gap.shape, f32)
    for m in range(-reach, reach + 1):
        total = jnp.where(gap == m, values[m + reach], total)
    return total


def right(v, twice, rest):
    hi, lo = split(v)
    r = jnp.dot(jnp.concatenate([hi, lo], 1), twice, preferred_element_type=f32)
    return r + jnp.dot(hi, rest, preferred_element_type=f32)


def right_exact(v, twice):
    hi, lo = split(v)
    return jnp.dot(jnp.concatenate([hi, lo], 1), twice, preferred_element_type=f32)


def field_kernel(
    inv_ref, cnt_ref, taps_ref, charge_ref, pos_ref, v_ref, xy_ref, z_ref,
    acc, place, qs, ts, q_ref,
    zs, zr, a_ref, ys, yr, xr, ext, rs, rr,
    c_ref, cxs, cxr, cext, d_ref, czs, czr, e_ref, cys, cyr, g_ref,
    cz_m, my_m, rz_m, ry_m, ccz_m, cmy_m, pz_m,
    zsem, ysem, xsem, csem, rsem,
):
    ids = {name: lax.axis_index(name) for name in ("gx", "gy", "gz")}
    size_of = {"gx": 4, "gy": 4, "gz": 8}

    def away(name, step):
        count = size_of[name]
        return {name: lax.rem(ids[name] + (step + count), count)}

    for s in range(2):
        for j in range(21, 24):
            cyr[s, j] = jnp.zeros((16, 128), f32)
    barrier = pltpu.get_barrier_semaphore()
    for name in ("gx", "gy", "gz"):
        for step in (1, -1):
            pl.semaphore_signal(barrier, inc=1, device_id=away(name, step), device_id_type=MESH)

    lane = iota((1, 128), 1)
    lane40 = iota((40, 128), 1)
    lane24 = iota((24, 128), 1)
    half24 = lane24 % 64

    def link(name, k, src, dst, sems, *spot):
        return pltpu.make_async_remote_copy(
            src_ref=src,
            dst_ref=dst,
            send_sem=sems.at[(0, *spot)],
            recv_sem=sems.at[(1, *spot)],
            device_id=away(name, 1 - 2 * k),
            device_id_type=MESH,
        )

    def send(*args):
        copy = link(*args)
        copy.start()
        return copy

    def links_z(g):
        return [link("gz", k, zs.at[k, g], zr.at[k, g], zsem, g, k) for k in range(2)]

    def links_y(g):
        own = pl.ds(8 * g, 8 if g < 4 else 4)
        return [link("gy", k, ys.at[k, own], yr.at[k, own], ysem, g, k) for k in range(2)]

    pieces = {0: (1, 0, 8), 1: (1, 8, 15), 2: (0, 21, 24), 3: (0, 24, 32), 4: (0, 32, 36)}

    def link_x(g):
        k, low, high = pieces[g]
        base = 0 if k else 21
        src = ext.at[pl.ds(11 + low, high - low)]
        dst = xr.at[k, pl.ds(low - base, high - low)]
        return link("gx", k, src, dst, xsem, g)

    knot = iota((8, 128), 0).astype(f32) - 1.0
    lane8 = iota((8, 128), 1)
    zero = jnp.zeros((8, 128), f32)
    acc[...] = jnp.zeros_like(acc)
    ts[...] = jnp.zeros_like(ts)
    for x in range(6):
        q_ref[x] = jnp.zeros((40, 128), f32)
    for x in range(42, 54):
        q_ref[x] = jnp.zeros((40, 128), f32)

    def cell(row, cz, spot):
        at = row * 16 + cz
        n = inv_ref[at]
        q = jnp.where(lane8 < cnt_ref[at], row8(charge_ref, None, n), 0.0)
        wx = spline8(row8(pos_ref, 0, n), knot)
        wy = spline8(row8(pos_ref, 1, n), knot)
        wz = spline8(row8(pos_ref, 2, n), knot)
        xy_ref[at, 0] = wx
        xy_ref[at, 1] = wy
        qs[spot] = q * wx
        prod = jnp.concatenate([row8(qs, spot, a) * wy for a in range(8)], axis=0)
        tile = jnp.concatenate([zero, wz] if cz % 2 else [wz, zero], axis=0)
        hi, lo = split(tile)
        z_ref[at, 0] = hi
        z_ref[at, 1] = lo
        return split(prod), (hi, lo)

    def line(odd, row):
        parts = []
        for k in range(8):
            (ah, al), (bh, bl) = cell(row, 2 * k, 16 * odd + 2 * k)
            (ch, cl), (dh, dl) = cell(row, 2 * k + 1, 16 * odd + 2 * k + 1)
            left = jnp.concatenate(
                [jnp.concatenate([ah, ch], 1), jnp.concatenate([al, cl], 1)], 0
            )
            down = jnp.concatenate(
                [jnp.concatenate([bh, dh], 1), jnp.concatenate([bl, dl], 1)], 0
            )
            r = lax.dot_general(down, left, (((1,), (1,)), ((), ())), preferred_element_type=f32)
            parts.append(r[0:16] + r[16:32])
        ts[odd] = jnp.concatenate(parts, 0)

    def slab_of(n):
        late = jnp.minimum(n // 2, 1)
        last = jnp.minimum(n // 5, 1)
        return n + (late - last) * (9 - 2 * n) - 3 * last

    def drain(i, odd):
        spot = pl.ds(pl.multiple_of(i % 4 * 8, 8), 8)
        t = ts[odd].T
        t = t[0:64] + t[64:128]
        for a in range(8):
            acc[odd, 4 * slab_of(i // 4) + a, spot, :] += t[8 * a : 8 * a + 8]

    def step(i, carry):
        before = jnp.maximum(i - 1, 0)
        drain(before, 0)
        drain(before, 1)
        row = 8 * slab_of(i // 4) + 2 * (i % 4)
        line(0, row)
        line(1, row + 1)
        return carry

    lin = iota((256, 128), 0) % 128
    place[...] = jnp.where(4 * (lin // 8) + lin % 8 + 11 == iota((256, 128), 1), 1.0, 0.0).astype(bf16)

    def close(g):
        count = 8 if g < 4 else 4
        joined = []
        for i in range(count):
            x = 8 * g + i
            pad = jnp.zeros((4, 128), f32)
            even = jnp.concatenate([acc[0, x], pad, pad], 0)
            odd = jnp.concatenate([pad, acc[1, x], pad], 0)
            joined.append(even + odd)
        hi, lo = split(jnp.concatenate(joined, 0))
        r = jnp.dot(jnp.concatenate([hi, lo], 1), place[...], preferred_element_type=f32)
        up = jnp.zeros((40, 128), f32)
        down = jnp.zeros((40, 128), f32)
        for i in range(count):
            v = r[40 * i : 40 * i + 40] * (1.0 / 216.0)
            q_ref[6 + 8 * g + i] = v
            here = lane40 // 16 == i
            up = jnp.where(here, pltpu.roll(v, (16 * i - 64) % 128, 1), up)
            down = jnp.where(here, pltpu.roll(v, (16 * i - 11) % 128, 1), down)
        zs[0, g] = up
        zs[1, g] = down
        for copy in links_z(g):
            copy.start()

    gap = iota((256, 128), 0) % 128 - 12 - 2 * (iota((256, 128), 1) % 64 - 13)
    node = iota((256, 128), 1) % 64 - 13
    rz_m[...] = jnp.where((node >= -2) & (node <= 34), weight_of(gap), 0.0).astype(bf16)
    gap = iota((24, 96), 1) % 48 - 2 * iota((24, 96), 0) + 3
    ry_m[...] = jnp.where(iota((24, 96), 1) % 48 < 40, weight_of(gap), 0.0).astype(bf16)

    def shrink(g, carry):
        rows = []
        for i in range(4):
            first = 2 * (4 * g + i)
            near = q_ref[first + 2] + q_ref[first + 4]
            wide = q_ref[first] + q_ref[first + 6]
            rows.append(q_ref[first + 3] + 0.5625 * near - 0.0625 * wide)
        r = right_exact(jnp.concatenate(rows, 0), rz_m[...])
        r = jnp.concatenate([r[40 * i : 40 * i + 40] for i in range(4)], 1)
        r = jnp.concatenate([r, jnp.zeros((8, 512), f32)], 0)
        hi, lo = split(r)
        r = jnp.dot(ry_m[...], jnp.concatenate([hi, lo], 0), preferred_element_type=f32)
        for i in range(4):
            c_ref[4 * g + i] = r[:, 128 * i : 128 * i + 128]
        return carry

    ftap = [jnp.where(lane < 64, taps_ref[0, m], taps_ref[1, m]) for m in range(23)]
    gap = iota((128, 128), 0) - 12 - iota((128, 128), 1) % 64
    hi, lo = split(banded(gap, ftap, 11))
    cz_m[0:128] = hi
    cz_m[128:256] = hi
    cz_m[256:384] = lo
    row40 = iota((40, 128), 0)

    def make_my():
        off = jnp.where(lane40 < 40, lane40, jnp.where(lane40 < 56, lane40 - 52, lane40 - 24))
        gap = jnp.where(lane40 < 72, off - row40, 99)
        for t in range(2):
            full = banded(gap, [taps_ref[t, m] for m in range(23)], 11)
            hi = full.astype(bf16).astype(f32)
            lo = full - hi
            turned = pltpu.roll(hi, 80, 1)
            first = jnp.where(lane40 < 80, hi, turned)
            second = jnp.where(lane40 < 32, turned, pltpu.roll(lo, 32, 1))
            my_m[40 * t : 40 * t + 40] = jnp.concatenate([first, second], 1).astype(bf16)

    make_my()

    def conv_z(g):
        for copy in links_z(g):
            copy.wait()
        up = zr[0, g]
        down = zr[1, g]
        rows = []
        count = 8 if g < 4 else 4
        for i in range(count):
            v = q_ref[6 + 8 * g + i]
            v = v + jnp.where(lane40 < 16, pltpu.roll(up, (-16 * i) % 128, 1), 0.0)
            here = (lane40 >= 75) & (lane40 < 91)
            v = v + jnp.where(here, pltpu.roll(down, (75 - 16 * i) % 128, 1), 0.0)
            rows.append(v)
        r = right(jnp.concatenate(rows, 0), cz_m[0:256], cz_m[256:384])
        for i in range(count):
            part = r[40 * i : 40 * i + 40]
            a_ref[8 * g + i] = part
            ys[0, 8 * g + i] = part[20:36]
            ys[1, 8 * g + i] = part[0:16]
        for copy in links_y(g):
            copy.start()

    def conv_y(g):
        for copy in links_y(g):
            copy.wait()
        for h in range(4 if g < 4 else 2):
            both = []
            for p in range(2):
                x = 8 * g + 2 * h + p
                rows = [a_ref[x], yr[0, x], yr[1, x], jnp.zeros((8, 128), f32)]
                both.append(jnp.concatenate(rows, 0))
            hi, lo = split(jnp.concatenate(both, 1))
            stack = jnp.concatenate([hi, lo, hi], 0)
            r = jnp.dot(my_m[:, 0:240], stack, preferred_element_type=f32)
            for p in range(2):
                part = r[:, 128 * p : 128 * p + 128]
                ext[11 + 8 * g + 2 * h + p] = jnp.where(lane40 < 64, part[0:40], part[40:80])
        link_x(g).start()
    up_early = ((5, 16), (6, 17), (7, 18), (19, 20))

    def links_cx(late):
        copies = []
        for k in range(2):
            src = cxs.at[0 if late else k, pl.ds(4 * late, 4)]
            dst = cxr.at[k, pl.ds(4 * late, 4)]
            copies.append(link("gx", k, src, dst, csem, 3 * late, k))
        return copies

    def flush(i):
        for odd in range(2):
            drain(i, odd)
        ts[...] = jnp.zeros_like(ts)

    lax.fori_loop(0, 8, step, 0, unroll=2)
    flush(7)
    pl.semaphore_wait(barrier, 6)
    close(0)
    shrink(0, 0)

    def slab(n, carry):
        for r in range(4):
            step(4 * n + r, 0)

        @pl.when(n == 2)
        def _():
            flush(11)
            close(4)
            shrink(5, 0)

        @pl.when(n == 3)
        def _():
            conv_z(0)

        @pl.when(n == 4)
        def _():
            flush(19)
            close(3)
            shrink(4, 0)
            conv_z(4)

        @pl.when(n == 5)
        def _():
            conv_y(0)

        @pl.when(n == 6)
        def _():
            flush(27)
            close(1)
            shrink(1, 0)
            for k, (first, second) in enumerate(up_early):
                cxs[0, k] = jnp.where(lane24 < 64, c_ref[first], c_ref[second])
                cxs[1, k] = jnp.where(lane24 < 64, c_ref[k], c_ref[4 + k])
            for copy in links_cx(0):
                copy.start()
            conv_z(3)
            conv_y(4)

        return carry

    lax.fori_loop(2, 8, slab, 0)
    flush(31)
    close(2)
    shrink(2, 0)
    shrink(3, 0)
    for k in range(4):
        cxs[0, 4 + k] = jnp.where(lane24 < 64, c_ref[8 + k], c_ref[12 + k])
    for copy in links_cx(1):
        copy.start()

    conv_z(1)
    conv_y(3)
    conv_z(2)

    ctap = [jnp.where(lane < 64, taps_ref[2, m], taps_ref[3, m]) for m in range(23)]
    gap = iota((128, 128), 0) % 64 - iota((128, 128), 1) % 64 - 11
    gap = jnp.where(iota((128, 128), 0) // 64 == iota((128, 128), 1) // 64, gap, 99)
    hi, lo = split(banded(gap, ctap, 11))
    ccz_m[0:128] = hi
    ccz_m[128:256] = hi
    ccz_m[256:384] = lo
    conv_y(1)
    for copy in links_cx(0) + links_cx(1):
        copy.wait()
    for k in range(21):
        cext[11 + k] = c_ref[k]

    def put(spot, v):
        if 11 <= spot < 32:
            cext[spot] += v
        else:
            cext[spot] = v

    for k in range(2):
        for i in range(8):
            v = cxr[k, i]
            w = pltpu.roll(v, 64, 1)
            if i >= 4:
                pair = (4 + i, 8 + i)
            else:
                pair = (i, 4 + i) if k else up_early[i]
            base = 27 if k else -5
            put(base + pair[0], jnp.where(lane24 < 64, v, w))
            put(base + pair[1], jnp.where(lane24 < 64, w, v))

    def conv_cx(c, carry):
        rows = pl.ds(pl.multiple_of(8 * c, 8), 8)
        for first in (0, 7, 14):
            acc = ctap[0] * cext[first : first + 7, rows, :]
            for m in range(1, 23):
                acc = acc + ctap[m] * cext[first + m : first + m + 7, rows, :]
            d_ref[first : first + 7, rows, :] = acc
        return carry

    lax.fori_loop(0, 3, conv_cx, 0)
    for j in range(21, 24):
        d_ref[j] = jnp.zeros((24, 128), f32)

    def pack_cz(g, carry):
        up = jnp.zeros((24, 128), f32)
        down = jnp.zeros((24, 128), f32)
        for i in range(4):
            v = d_ref[4 * g + i]
            here = half24 // 16 == i
            up = jnp.where(here, pltpu.roll(v, (16 * i - 32) % 128, 1), up)
            down = jnp.where(here, pltpu.roll(v, (16 * i - 11) % 128, 1), down)
        czs[0, g] = up
        czs[1, g] = down
        return carry

    lax.fori_loop(0, 6, pack_cz, 0, unroll=2)
    cz_copies = [send("gz", k, czs.at[k], czr.at[k], csem, 1, k) for k in range(2)]

    conv_y(2)

    for copy in cz_copies:
        copy.wait()

    def conv_cz(g, carry):
        up = czr[0, g]
        down = czr[1, g]
        rows = []
        for i in range(4):
            v = d_ref[4 * g + i]
            v = v + jnp.where(half24 < 16, pltpu.roll(up, (-16 * i) % 128, 1), 0.0)
            here = (half24 >= 43) & (half24 < 59)
            v = v + jnp.where(here, pltpu.roll(down, (43 - 16 * i) % 128, 1), 0.0)
            rows.append(v)
        r = right(jnp.concatenate(rows, 0), ccz_m[0:256], ccz_m[256:384])
        for i in range(4):
            part = r[24 * i : 24 * i + 24]
            e_ref[4 * g + i] = part
            cys[0, 4 * g + i] = part[5:21]
            cys[1, 4 * g + i] = part[0:16]
        return carry

    lax.fori_loop(0, 6, conv_cz, 0, unroll=2)
    own = pl.ds(0, 21)
    cy_copies = [send("gy", k, cys.at[k, own], cyr.at[k, own], csem, 2, k) for k in range(2)]

    spot = jnp.where(lane40 < 24, lane40 - 2, jnp.where(lane40 < 40, lane40 - 37, lane40 - 26))
    valid = ((lane40 < 21) | (lane40 >= 24)) & (lane40 < 56)
    gap = jnp.where(valid, 2 * spot - (row40 - 1), 99)
    for t in range(2):
        taps = []
        for d in range(-25, 26):
            total = 0.0
            for g, weight in ((0, 1.0), (1, 0.5625), (-1, 0.5625), (3, -0.0625), (-3, -0.0625)):
                if (d + g) % 2 == 0 and abs((d + g) // 2) <= 11:
                    total = total + weight * taps_ref[2 + t, (d + g) // 2 + 11]
            taps.append(total)
        full = banded(gap, taps, 25)
        hi = full.astype(bf16).astype(f32)
        first = jnp.where(lane40 < 64, hi, pltpu.roll(hi, 64, 1))
        cmy_m[40 * t : 40 * t + 40] = jnp.concatenate([first, full - hi], 1).astype(bf16)
    spot = iota((256, 128), 0) % 64 - 2
    point = iota((256, 128), 1)
    point = jnp.where(point == 127, -1, point)
    good = (spot <= 34) & (point <= 66)
    pz_m[...] = jnp.where(good, weight_of(point - 2 * spot), 0.0).astype(bf16)

    for g in (0, 1, 3, 4):
        link_x(g).wait()
    ext[3:11] = xr[0, 3:11]
    ext[11:15] += xr[0, 11:15]
    ext[43:47] += xr[1, 0:4]
    ext[47:58] = xr[1, 4:15]

    def conv_x(k, carry):
        rows = pl.ds(pl.multiple_of(8 * (k % 5), 8), 8)
        first = 12 * (2 - k // 5)
        acc = ftap[0] * ext[pl.ds(first, 12), rows, :]
        for m in range(1, 23):
            acc = acc + ftap[m] * ext[pl.ds(first + m, 12), rows, :]
        for i in range(12):
            part = acc[i]
            v_ref[first + i, rows, :] = part + pltpu.roll(part, 64, 1)
        return carry

    r_copies = []
    for g in (2, 1, 0):
        if g == 0:
            link_x(2).wait()
            ext[0:3] = xr[0, 0:3]
        lax.fori_loop(10 - 5 * g, 15 - 5 * g, conv_x, 0)
        up = jnp.zeros((40, 128), f32)
        down = jnp.zeros((40, 128), f32)
        for i in range(12):
            v = v_ref[12 * g + i]
            here = lane40 // 4 == i
            up = jnp.where(here, pltpu.roll(v, (4 * i - 60) % 128, 1), up)
            down = jnp.where(here, pltpu.roll(v, (4 * i) % 128, 1), down)
        rs[0, g] = up
        rs[1, g] = down
        for k in range(2):
            r_copies.append(send("gz", k, rs.at[k, g], rr.at[k, g], rsem, g, k))

    for copy in cy_copies:
        copy.wait()

    def conv_cy(h, carry):
        both = []
        for p in range(2):
            j = 2 * h + p
            rows = [e_ref[j], cyr[0, j], cyr[1, j], jnp.zeros((8, 128), f32)]
            both.append(jnp.concatenate(rows, 0))
        hi, lo = split(jnp.concatenate(both, 1))
        stack = jnp.concatenate([hi, lo, hi], 0)
        r = jnp.dot(cmy_m[:, 0:192], stack, preferred_element_type=f32)
        parts = []
        for p in range(2):
            part = r[:, 128 * p : 128 * p + 128]
            parts.append(jnp.where(lane40 < 64, part[0:40], part[40:80]))
        r = right_exact(jnp.concatenate(parts, 0), pz_m[...])
        g_ref[2 * h] = r[0:40]
        g_ref[2 * h + 1] = r[40:80]
        return carry

    lax.fori_loop(0, 11, conv_cy, 0, unroll=11)
    for x in range(36):
        h = x // 2
        if x % 2:
            far = g_ref[h + 2]
        else:
            far = 0.5625 * (g_ref[h + 1] + g_ref[h + 2]) - 0.0625 * (g_ref[h] + g_ref[h + 3])
        v_ref[x] = jnp.where(lane40 < 64, v_ref[x], 0.0) + far
    for copy in r_copies:
        copy.wait()
    for x in range(36):
        g, i = x // 12, x % 12
        above = pltpu.roll(rr[1, g], (64 - 4 * i) % 128, 1)
        below = pltpu.roll(rr[0, g], (124 - 4 * i) % 128, 1)
        rim = jnp.where((lane40 >= 64) & (lane40 < 67), above, 0.0)
        v_ref[x] += jnp.where(lane40 == 127, below, rim)


def field(inv, counts, taps, charge, positions):
    def scratch(*shape):
        return pltpu.VMEM(shape, f32)

    return pl.pallas_call(
        field_kernel,
        out_shape=(
            jax.ShapeDtypeStruct((36, 40, 128), f32),
            jax.ShapeDtypeStruct((1024, 2, 8, 128), f32),
            jax.ShapeDtypeStruct((1024, 2, 16, 128), bf16),
        ),
        in_specs=[SMEM, SMEM, SMEM, VMEM, VMEM],
        out_specs=(VMEM, VMEM, VMEM),
        scratch_shapes=[
            scratch(2, 36, 32, 128),
            pltpu.VMEM((256, 128), bf16),
            scratch(32, 8, 128),
            scratch(2, 128, 128),
            scratch(54, 40, 128),
            scratch(2, 5, 40, 128),
            scratch(2, 5, 40, 128),
            scratch(40, 40, 128),
            scratch(2, 40, 16, 128),
            scratch(2, 40, 16, 128),
            scratch(2, 15, 40, 128),
            scratch(58, 40, 128),
            scratch(2, 3, 40, 128),
            scratch(2, 3, 40, 128),
            scratch(24, 24, 128),
            scratch(2, 8, 24, 128),
            scratch(2, 8, 24, 128),
            scratch(43, 24, 128),
            scratch(24, 24, 128),
            scratch(2, 6, 24, 128),
            scratch(2, 6, 24, 128),
            scratch(24, 24, 128),
            scratch(2, 24, 16, 128),
            scratch(2, 24, 16, 128),
            scratch(22, 40, 128),
            pltpu.VMEM((384, 128), bf16),
            pltpu.VMEM((80, 256), bf16),
            pltpu.VMEM((256, 128), bf16),
            pltpu.VMEM((24, 96), bf16),
            pltpu.VMEM((384, 128), bf16),
            pltpu.VMEM((80, 256), bf16),
            pltpu.VMEM((256, 128), bf16),
            pltpu.SemaphoreType.DMA((2, 5, 2)),
            pltpu.SemaphoreType.DMA((2, 5, 2)),
            pltpu.SemaphoreType.DMA((2, 5)),
            pltpu.SemaphoreType.DMA((2, 4, 2)),
            pltpu.SemaphoreType.DMA((2, 3, 2)),
        ],
        compiler_params=pltpu.CompilerParams(
            collective_id=0, has_side_effects=True, vmem_limit_bytes=30 * 1024 * 1024
        ),
    )(inv, counts, taps, charge, positions)


def body(charge, positions, counts, corner, fine_taps, coarse_taps):
    ext_y = CY + 6
    ext_z = CZ + 6
    count = corner.shape[0]
    spots = np.arange(count, dtype=np.int32)
    along_y, along_z = CY // 4, CZ // 4
    cell_x, cell_y, cell_z = spots // (along_y * along_z), spots // along_z % along_y, spots % along_z
    wanted = ((4 * cell_x + 2) * ext_y + 4 * cell_y + 2) * ext_z + 4 * cell_z + 2
    same = corner[:, None] == wanted[None, :]
    number = lax.broadcasted_iota(jnp.int32, (count, count), 0)
    inv = jnp.sum(jnp.where(same, number, 0), axis=0, dtype=jnp.int32)
    live = jnp.sum(jnp.where(same, counts[:, None], 0), axis=0, dtype=jnp.int32)
    taps = jnp.concatenate([fine_taps, coarse_taps], 0)
    values, planes, depths = field(inv, live, taps, charge, positions)
    return sample(inv, live, planes, depths, values)


def solution(mesh):
    placed = (
        P(("gx", "gy", "gz"), None),
        P(None, ("gx", "gy", "gz"), None),
        P(("gx", "gy", "gz")),
        P(("gx", "gy", "gz")),
        P(),
        P(),
    )
    return jax.shard_map(
        body,
        mesh=mesh,
        in_specs=placed,
        out_specs=(P(("gx", "gy", "gz"), None), P("gx", "gy", "gz")),
        check_vma=False,
    )
```

```python
import jax
import jax.numpy as jnp
import numpy as np
from jax import lax
from jax.experimental import pallas as pl
from jax.experimental.pallas import tpu as pltpu
from jax.sharding import PartitionSpec as P

CX = 32
CY = 32
CZ = 64
f32 = jnp.float32
bf16 = jnp.bfloat16


def split(v):
    hi = v.astype(bf16)
    return hi, (v - hi.astype(f32)).astype(bf16)


def spline8(u, node):
    m = jnp.abs(u - node)
    t = jnp.maximum(2.0 - m, 0.0)
    v = jnp.maximum(1.0 - m, 0.0)
    return t * t * t - 4.0 * (v * v * v)


def row8(ref, lead, n):
    v = ref[pl.ds(n, 1), :] if lead is None else ref[lead, pl.ds(n, 1), :]
    return jnp.broadcast_to(v, (8, 128))


def row8_at(ref, at, a):
    return jnp.broadcast_to(ref[at, 0, a : a + 1, :], (8, 128))


SMEM = pl.BlockSpec(memory_space=pltpu.SMEM)
VMEM = pl.BlockSpec(memory_space=pltpu.VMEM)


def sample_kernel(inv_ref, cnt_ref, xy_ref, z_ref, v_ref, out_ref, grid_ref, vs, place):
    lane = lax.broadcasted_iota(jnp.int32, (1, 128), 1)

    lin = lax.broadcasted_iota(jnp.int32, (256, 1024), 0)
    out = lax.broadcasted_iota(jnp.int32, (256, 1024), 1)
    within = out % 128
    z = (8 * (out // 128) + 4 * (within // 8 % 2) + within % 8 - 1) % 128
    part = within // 16
    hit = (z == lin % 128) & (part < 3) & ((part == 1) == (lin >= 128))
    place[...] = jnp.where(hit, 1.0, 0.0).astype(bf16)

    def open_rows(g, carry):
        rows = []
        for i in range(4):
            rows.append(v_ref[4 * g + i])
        hi, lo = split(jnp.concatenate(rows, 0) * (1.0 / 216.0))
        both = jnp.concatenate([hi, lo], 1)
        for k in range(0, 8, 2):
            r = jnp.dot(both, place[:, 128 * k : 128 * k + 256], preferred_element_type=f32)
            for i in range(4):
                for p in range(2):
                    here = r[40 * i : 40 * i + 40, 128 * p : 128 * p + 128]
                    vs[0, k + p, 4 * g + i] = here[0:32]
                    vs[1, k + p, 4 * g + i] = here[4:36]
        return carry

    lax.fori_loop(0, 9, open_rows, 0, unroll=9)
    for x in range(32):
        grid_ref[x] = v_ref[x + 1, 1:33, 0:64]

    def one(cx, start, odd, row):
        for k in range(8):
            spot = pl.ds(pl.multiple_of(start, 8), 8)
            left = vs[odd, k, pl.ds(4 * cx, 8), spot, :].reshape(64, 128).astype(bf16)
            at = row * 16 + 2 * k
            hi = jnp.concatenate([z_ref[at, 0], z_ref[at + 1, 0]], 1)
            lo = jnp.concatenate([z_ref[at, 1], z_ref[at + 1, 1]], 1)
            right_side = jnp.concatenate([hi, hi, lo], 0)
            f = jnp.dot(left[:, 0:48], right_side, preferred_element_type=f32)
            for p in range(2):
                here = slice(p * 128, p * 128 + 128)
                g = row8_at(xy_ref, at + p, 0) * f[0:8, here]
                for a in range(1, 8):
                    g = g + row8_at(xy_ref, at + p, a) * f[8 * a : 8 * a + 8, here]
                r = jnp.sum(g * xy_ref[at + p, 1], axis=0, keepdims=True)
                out_ref[pl.ds(inv_ref[at + p], 1), :] = jnp.where(lane < cnt_ref[at + p], r, 0.0)

    def step(i, carry):
        cx = i // 4
        start = (i % 4) * 8
        one(cx, start, 0, 2 * i)
        one(cx, start, 1, 2 * i + 1)
        return carry

    lax.fori_loop(0, 32, step, 0, unroll=16)


def sample(inv, counts, planes, depths, grid):
    return pl.pallas_call(
        sample_kernel,
        out_shape=(
            jax.ShapeDtypeStruct((1024, 128), f32),
            jax.ShapeDtypeStruct((32, 32, 64), f32),
        ),
        in_specs=[SMEM, SMEM, VMEM, VMEM, VMEM],
        out_specs=(VMEM, VMEM),
        scratch_shapes=[
            pltpu.VMEM((2, 8, 36, 32, 128), f32),
            pltpu.VMEM((256, 1024), bf16),
        ],
        compiler_params=pltpu.CompilerParams(vmem_limit_bytes=32 * 1024 * 1024),
    )(inv, counts, planes, depths, grid)


MESH = pl.DeviceIdType.MESH


def iota(shape, dim):
    return lax.broadcasted_iota(jnp.int32, shape, dim)


def weight_of(gap):
    size = jnp.abs(gap)
    return jnp.where(
        size == 0, 1.0, jnp.where(size == 1, 0.5625, jnp.where(size == 3, -0.0625, 0.0))
    )


def banded(gap, values, reach):
    total = jnp.zeros(gap.shape, f32)
    for m in range(-reach, reach + 1):
        total = jnp.where(gap == m, values[m + reach], total)
    return total


def right(v, twice, rest):
    hi, lo = split(v)
    r = jnp.dot(jnp.concatenate([hi, lo], 1), twice, preferred_element_type=f32)
    return r + jnp.dot(hi, rest, preferred_element_type=f32)


def right_exact(v, twice):
    hi, lo = split(v)
    return jnp.dot(jnp.concatenate([hi, lo], 1), twice, preferred_element_type=f32)


def field_kernel(
    inv_ref, cnt_ref, taps_ref, charge_ref, pos_ref, v_ref, xy_ref, z_ref,
    acc, place, qs, ts, q_ref,
    zs, zr, a_ref, ys, yr, xr, ext, rs, rr,
    c_ref, cxs, cxr, cext, d_ref, czs, czr, e_ref, cys, cyr, g_ref,
    cz_m, my_m, rz_m, ry_m, ccz_m, cmy_m, pz_m,
    zsem, ysem, xsem, csem, rsem,
):
    ids = {name: lax.axis_index(name) for name in ("gx", "gy", "gz")}
    size_of = {"gx": 4, "gy": 4, "gz": 8}

    def away(name, step):
        count = size_of[name]
        return {name: lax.rem(ids[name] + (step + count), count)}

    for s in range(2):
        for j in range(21, 24):
            cyr[s, j] = jnp.zeros((16, 128), f32)
    barrier = pltpu.get_barrier_semaphore()
    for name in ("gx", "gy", "gz"):
        for step in (1, -1):
            pl.semaphore_signal(barrier, inc=1, device_id=away(name, step), device_id_type=MESH)

    lane = iota((1, 128), 1)
    lane40 = iota((40, 128), 1)
    lane24 = iota((24, 128), 1)
    half24 = lane24 % 64

    def link(name, k, src, dst, sems, *spot):
        return pltpu.make_async_remote_copy(
            src_ref=src,
            dst_ref=dst,
            send_sem=sems.at[(0, *spot)],
            recv_sem=sems.at[(1, *spot)],
            device_id=away(name, 1 - 2 * k),
            device_id_type=MESH,
        )

    def send(*args):
        copy = link(*args)
        copy.start()
        return copy

    def links_z(g):
        return [link("gz", k, zs.at[k, g], zr.at[k, g], zsem, g, k) for k in range(2)]

    def links_y(g):
        own = pl.ds(8 * g, 8 if g < 4 else 4)
        return [link("gy", k, ys.at[k, own], yr.at[k, own], ysem, g, k) for k in range(2)]

    pieces = {0: (1, 0, 8), 1: (1, 8, 15), 2: (0, 21, 24), 3: (0, 24, 32), 4: (0, 32, 36)}

    def link_x(g):
        k, low, high = pieces[g]
        base = 0 if k else 21
        src = ext.at[pl.ds(11 + low, high - low)]
        dst = xr.at[k, pl.ds(low - base, high - low)]
        return link("gx", k, src, dst, xsem, g)

    knot = iota((8, 128), 0).astype(f32) - 1.0
    lane8 = iota((8, 128), 1)
    zero = jnp.zeros((8, 128), f32)
    acc[...] = jnp.zeros_like(acc)
    ts[...] = jnp.zeros_like(ts)
    for x in range(6):
        q_ref[x] = jnp.zeros((40, 128), f32)
    for x in range(42, 54):
        q_ref[x] = jnp.zeros((40, 128), f32)

    def cell(row, cz, spot):
        at = row * 16 + cz
        n = inv_ref[at]
        q = jnp.where(lane8 < cnt_ref[at], row8(charge_ref, None, n), 0.0)
        wx = spline8(row8(pos_ref, 0, n), knot)
        wy = spline8(row8(pos_ref, 1, n), knot)
        wz = spline8(row8(pos_ref, 2, n), knot)
        xy_ref[at, 0] = wx
        xy_ref[at, 1] = wy
        qs[spot] = q * wx
        prod = jnp.concatenate([row8(qs, spot, a) * wy for a in range(8)], axis=0)
        tile = jnp.concatenate([zero, wz] if cz % 2 else [wz, zero], axis=0)
        hi, lo = split(tile)
        z_ref[at, 0] = hi
        z_ref[at, 1] = lo
        return split(prod), (hi, lo)

    def line(odd, row):
        parts = []
        for k in range(8):
            (ah, al), (bh, bl) = cell(row, 2 * k, 16 * odd + 2 * k)
            (ch, cl), (dh, dl) = cell(row, 2 * k + 1, 16 * odd + 2 * k + 1)
            left = jnp.concatenate(
                [jnp.concatenate([ah, ch], 1), jnp.concatenate([al, cl], 1)], 0
            )
            down = jnp.concatenate(
                [jnp.concatenate([bh, dh], 1), jnp.concatenate([bl, dl], 1)], 0
            )
            r = lax.dot_general(down, left, (((1,), (1,)), ((), ())), preferred_element_type=f32)
            parts.append(r[0:16] + r[16:32])
        ts[odd] = jnp.concatenate(parts, 0)

    def slab_of(n):
        late = jnp.minimum(n // 2, 1)
        last = jnp.minimum(n // 5, 1)
        return n + (late - last) * (9 - 2 * n) - 3 * last

    def drain(i, odd):
        spot = pl.ds(pl.multiple_of(i % 4 * 8, 8), 8)
        t = ts[odd].T
        t = t[0:64] + t[64:128]
        for a in range(8):
            acc[odd, 4 * slab_of(i // 4) + a, spot, :] += t[8 * a : 8 * a + 8]

    def step(i, carry):
        before = jnp.maximum(i - 1, 0)
        drain(before, 0)
        drain(before, 1)
        row = 8 * slab_of(i // 4) + 2 * (i % 4)
        line(0, row)
        line(1, row + 1)
        return carry

    lin = iota((256, 128), 0) % 128
    place[...] = jnp.where(4 * (lin // 8) + lin % 8 + 11 == iota((256, 128), 1), 1.0, 0.0).astype(bf16)

    def close(g):
        count = 8 if g < 4 else 4
        joined = []
        for i in range(count):
            x = 8 * g + i
            pad = jnp.zeros((4, 128), f32)
            even = jnp.concatenate([acc[0, x], pad, pad], 0)
            odd = jnp.concatenate([pad, acc[1, x], pad], 0)
            joined.append(even + odd)
        hi, lo = split(jnp.concatenate(joined, 0))
        r = jnp.dot(jnp.concatenate([hi, lo], 1), place[...], preferred_element_type=f32)
        up = jnp.zeros((40, 128), f32)
        down = jnp.zeros((40, 128), f32)
        for i in range(count):
            v = r[40 * i : 40 * i + 40] * (1.0 / 216.0)
            q_ref[6 + 8 * g + i] = v
            here = lane40 // 16 == i
            up = jnp.where(here, pltpu.roll(v, (16 * i - 64) % 128, 1), up)
            down = jnp.where(here, pltpu.roll(v, (16 * i - 11) % 128, 1), down)
        zs[0, g] = up
        zs[1, g] = down
        for copy in links_z(g):
            copy.start()

    gap = iota((256, 128), 0) % 128 - 12 - 2 * (iota((256, 128), 1) % 64 - 13)
    node = iota((256, 128), 1) % 64 - 13
    rz_m[...] = jnp.where((node >= -2) & (node <= 34), weight_of(gap), 0.0).astype(bf16)
    gap = iota((24, 96), 1) % 48 - 2 * iota((24, 96), 0) + 3
    ry_m[...] = jnp.where(iota((24, 96), 1) % 48 < 40, weight_of(gap), 0.0).astype(bf16)

    def shrink(g, carry):
        rows = []
        for i in range(4):
            first = 2 * (4 * g + i)
            near = q_ref[first + 2] + q_ref[first + 4]
            wide = q_ref[first] + q_ref[first + 6]
            rows.append(q_ref[first + 3] + 0.5625 * near - 0.0625 * wide)
        r = right_exact(jnp.concatenate(rows, 0), rz_m[...])
        r = jnp.concatenate([r[40 * i : 40 * i + 40] for i in range(4)], 1)
        r = jnp.concatenate([r, jnp.zeros((8, 512), f32)], 0)
        hi, lo = split(r)
        r = jnp.dot(ry_m[...], jnp.concatenate([hi, lo], 0), preferred_element_type=f32)
        for i in range(4):
            c_ref[4 * g + i] = r[:, 128 * i : 128 * i + 128]
        return carry

    ftap = [jnp.where(lane < 64, taps_ref[0, m], taps_ref[1, m]) for m in range(23)]
    gap = iota((128, 128), 0) - 12 - iota((128, 128), 1) % 64
    hi, lo = split(banded(gap, ftap, 11))
    cz_m[0:128] = hi
    cz_m[128:256] = hi
    cz_m[256:384] = lo
    row40 = iota((40, 128), 0)

    def make_my():
        off = jnp.where(lane40 < 40, lane40, jnp.where(lane40 < 56, lane40 - 52, lane40 - 24))
        gap = jnp.where(lane40 < 72, off - row40, 99)
        for t in range(2):
            full = banded(gap, [taps_ref[t, m] for m in range(23)], 11)
            hi = full.astype(bf16).astype(f32)
            lo = full - hi
            turned = pltpu.roll(hi, 80, 1)
            first = jnp.where(lane40 < 80, hi, turned)
            second = jnp.where(lane40 < 32, turned, pltpu.roll(lo, 32, 1))
            my_m[40 * t : 40 * t + 40] = jnp.concatenate([first, second], 1).astype(bf16)

    make_my()

    def conv_z(g):
        for copy in links_z(g):
            copy.wait()
        up = zr[0, g]
        down = zr[1, g]
        rows = []
        count = 8 if g < 4 else 4
        for i in range(count):
            v = q_ref[6 + 8 * g + i]
            v = v + jnp.where(lane40 < 16, pltpu.roll(up, (-16 * i) % 128, 1), 0.0)
            here = (lane40 >= 75) & (lane40 < 91)
            v = v + jnp.where(here, pltpu.roll(down, (75 - 16 * i) % 128, 1), 0.0)
            rows.append(v)
        r = right(jnp.concatenate(rows, 0), cz_m[0:256], cz_m[256:384])
        for i in range(count):
            part = r[40 * i : 40 * i + 40]
            a_ref[8 * g + i] = part
            ys[0, 8 * g + i] = part[20:36]
            ys[1, 8 * g + i] = part[0:16]
        for copy in links_y(g):
            copy.start()

    def conv_y(g):
        for copy in links_y(g):
            copy.wait()
        for h in range(4 if g < 4 else 2):
            both = []
            for p in range(2):
                x = 8 * g + 2 * h + p
                rows = [a_ref[x], yr[0, x], yr[1, x], jnp.zeros((8, 128), f32)]
                both.append(jnp.concatenate(rows, 0))
            hi, lo = split(jnp.concatenate(both, 1))
            stack = jnp.concatenate([hi, lo, hi], 0)
            r = jnp.dot(my_m[:, 0:240], stack, preferred_element_type=f32)
            for p in range(2):
                part = r[:, 128 * p : 128 * p + 128]
                ext[11 + 8 * g + 2 * h + p] = jnp.where(lane40 < 64, part[0:40], part[40:80])
        link_x(g).start()
    up_early = ((5, 16), (6, 17), (7, 18), (19, 20))

    def links_cx(late):
        copies = []
        for k in range(2):
            src = cxs.at[0 if late else k, pl.ds(4 * late, 4)]
            dst = cxr.at[k, pl.ds(4 * late, 4)]
            copies.append(link("gx", k, src, dst, csem, 3 * late, k))
        return copies

    def flush(i):
        for odd in range(2):
            drain(i, odd)
        ts[...] = jnp.zeros_like(ts)

    lax.fori_loop(0, 8, step, 0, unroll=4)
    flush(7)
    pl.semaphore_wait(barrier, 6)
    close(0)
    shrink(0, 0)

    def slab(n, carry):
        for r in range(4):
            step(4 * n + r, 0)

        @pl.when(n == 2)
        def _():
            flush(11)
            close(4)
            shrink(5, 0)

        @pl.when(n == 3)
        def _():
            conv_z(0)

        @pl.when(n == 4)
        def _():
            flush(19)
            close(3)
            shrink(4, 0)
            conv_z(4)

        @pl.when(n == 5)
        def _():
            conv_y(0)

        @pl.when(n == 6)
        def _():
            flush(27)
            close(1)
            shrink(1, 0)
            for k, (first, second) in enumerate(up_early):
                cxs[0, k] = jnp.where(lane24 < 64, c_ref[first], c_ref[second])
                cxs[1, k] = jnp.where(lane24 < 64, c_ref[k], c_ref[4 + k])
            for copy in links_cx(0):
                copy.start()
            conv_z(3)
            conv_y(4)

        return carry

    lax.fori_loop(2, 8, slab, 0)
    flush(31)
    close(2)
    shrink(2, 0)
    shrink(3, 0)
    for k in range(4):
        cxs[0, 4 + k] = jnp.where(lane24 < 64, c_ref[8 + k], c_ref[12 + k])
    for copy in links_cx(1):
        copy.start()

    conv_z(1)
    conv_y(3)
    conv_z(2)

    ctap = [jnp.where(lane < 64, taps_ref[2, m], taps_ref[3, m]) for m in range(23)]
    gap = iota((128, 128), 0) % 64 - iota((128, 128), 1) % 64 - 11
    gap = jnp.where(iota((128, 128), 0) // 64 == iota((128, 128), 1) // 64, gap, 99)
    hi, lo = split(banded(gap, ctap, 11))
    ccz_m[0:128] = hi
    ccz_m[128:256] = hi
    ccz_m[256:384] = lo
    conv_y(1)
    for copy in links_cx(0) + links_cx(1):
        copy.wait()
    for k in range(21):
        cext[11 + k] = c_ref[k]

    def put(spot, v):
        if 11 <= spot < 32:
            cext[spot] += v
        else:
            cext[spot] = v

    for k in range(2):
        for i in range(8):
            v = cxr[k, i]
            w = pltpu.roll(v, 64, 1)
            if i >= 4:
                pair = (4 + i, 8 + i)
            else:
                pair = (i, 4 + i) if k else up_early[i]
            base = 27 if k else -5
            put(base + pair[0], jnp.where(lane24 < 64, v, w))
            put(base + pair[1], jnp.where(lane24 < 64, w, v))

    def conv_cx(c, carry):
        rows = pl.ds(pl.multiple_of(8 * c, 8), 8)
        for first in (0, 7, 14):
            acc = ctap[0] * cext[first : first + 7, rows, :]
            for m in range(1, 23):
                acc = acc + ctap[m] * cext[first + m : first + m + 7, rows, :]
            d_ref[first : first + 7, rows, :] = acc
        return carry

    lax.fori_loop(0, 3, conv_cx, 0, unroll=3)
    for j in range(21, 24):
        d_ref[j] = jnp.zeros((24, 128), f32)

    def pack_cz(g, carry):
        up = jnp.zeros((24, 128), f32)
        down = jnp.zeros((24, 128), f32)
        for i in range(4):
            v = d_ref[4 * g + i]
            here = half24 // 16 == i
            up = jnp.where(here, pltpu.roll(v, (16 * i - 32) % 128, 1), up)
            down = jnp.where(here, pltpu.roll(v, (16 * i - 11) % 128, 1), down)
        czs[0, g] = up
        czs[1, g] = down
        return carry

    lax.fori_loop(0, 6, pack_cz, 0, unroll=6)
    cz_copies = [send("gz", k, czs.at[k], czr.at[k], csem, 1, k) for k in range(2)]

    conv_y(2)

    for copy in cz_copies:
        copy.wait()

    def conv_cz(g, carry):
        up = czr[0, g]
        down = czr[1, g]
        rows = []
        for i in range(4):
            v = d_ref[4 * g + i]
            v = v + jnp.where(half24 < 16, pltpu.roll(up, (-16 * i) % 128, 1), 0.0)
            here = (half24 >= 43) & (half24 < 59)
            v = v + jnp.where(here, pltpu.roll(down, (43 - 16 * i) % 128, 1), 0.0)
            rows.append(v)
        r = right(jnp.concatenate(rows, 0), ccz_m[0:256], ccz_m[256:384])
        for i in range(4):
            part = r[24 * i : 24 * i + 24]
            e_ref[4 * g + i] = part
            cys[0, 4 * g + i] = part[5:21]
            cys[1, 4 * g + i] = part[0:16]
        return carry

    lax.fori_loop(0, 6, conv_cz, 0, unroll=6)
    own = pl.ds(0, 21)
    cy_copies = [send("gy", k, cys.at[k, own], cyr.at[k, own], csem, 2, k) for k in range(2)]

    spot = jnp.where(lane40 < 24, lane40 - 2, jnp.where(lane40 < 40, lane40 - 37, lane40 - 26))
    valid = ((lane40 < 21) | (lane40 >= 24)) & (lane40 < 56)
    gap = jnp.where(valid, 2 * spot - (row40 - 1), 99)
    for t in range(2):
        taps = []
        for d in range(-25, 26):
            total = 0.0
            for g, weight in ((0, 1.0), (1, 0.5625), (-1, 0.5625), (3, -0.0625), (-3, -0.0625)):
                if (d + g) % 2 == 0 and abs((d + g) // 2) <= 11:
                    total = total + weight * taps_ref[2 + t, (d + g) // 2 + 11]
            taps.append(total)
        full = banded(gap, taps, 25)
        hi = full.astype(bf16).astype(f32)
        first = jnp.where(lane40 < 64, hi, pltpu.roll(hi, 64, 1))
        cmy_m[40 * t : 40 * t + 40] = jnp.concatenate([first, full - hi], 1).astype(bf16)
    spot = iota((256, 128), 0) % 64 - 2
    point = iota((256, 128), 1)
    point = jnp.where(point == 127, -1, point)
    good = (spot <= 34) & (point <= 66)
    pz_m[...] = jnp.where(good, weight_of(point - 2 * spot), 0.0).astype(bf16)

    for g in (0, 1, 3, 4):
        link_x(g).wait()
    ext[3:11] = xr[0, 3:11]
    ext[11:15] += xr[0, 11:15]
    ext[43:47] += xr[1, 0:4]
    ext[47:58] = xr[1, 4:15]

    def conv_x(k, carry):
        rows = pl.ds(pl.multiple_of(8 * (k % 5), 8), 8)
        first = 12 * (2 - k // 5)
        acc = ftap[0] * ext[pl.ds(first, 12), rows, :]
        for m in range(1, 23):
            acc = acc + ftap[m] * ext[pl.ds(first + m, 12), rows, :]
        for i in range(12):
            part = acc[i]
            v_ref[first + i, rows, :] = part + pltpu.roll(part, 64, 1)
        return carry

    r_copies = []
    for g in (2, 1, 0):
        if g == 0:
            link_x(2).wait()
            ext[0:3] = xr[0, 0:3]
        lax.fori_loop(10 - 5 * g, 15 - 5 * g, conv_x, 0, unroll=5)
        up = jnp.zeros((40, 128), f32)
        down = jnp.zeros((40, 128), f32)
        for i in range(12):
            v = v_ref[12 * g + i]
            here = lane40 // 4 == i
            up = jnp.where(here, pltpu.roll(v, (4 * i - 60) % 128, 1), up)
            down = jnp.where(here, pltpu.roll(v, (4 * i) % 128, 1), down)
        rs[0, g] = up
        rs[1, g] = down
        for k in range(2):
            r_copies.append(send("gz", k, rs.at[k, g], rr.at[k, g], rsem, g, k))

    for copy in cy_copies:
        copy.wait()

    def conv_cy(h, carry):
        both = []
        for p in range(2):
            j = 2 * h + p
            rows = [e_ref[j], cyr[0, j], cyr[1, j], jnp.zeros((8, 128), f32)]
            both.append(jnp.concatenate(rows, 0))
        hi, lo = split(jnp.concatenate(both, 1))
        stack = jnp.concatenate([hi, lo, hi], 0)
        r = jnp.dot(cmy_m[:, 0:192], stack, preferred_element_type=f32)
        parts = []
        for p in range(2):
            part = r[:, 128 * p : 128 * p + 128]
            parts.append(jnp.where(lane40 < 64, part[0:40], part[40:80]))
        r = right_exact(jnp.concatenate(parts, 0), pz_m[...])
        g_ref[2 * h] = r[0:40]
        g_ref[2 * h + 1] = r[40:80]
        return carry

    lax.fori_loop(0, 11, conv_cy, 0, unroll=11)
    for x in range(36):
        h = x // 2
        if x % 2:
            far = g_ref[h + 2]
        else:
            far = 0.5625 * (g_ref[h + 1] + g_ref[h + 2]) - 0.0625 * (g_ref[h] + g_ref[h + 3])
        v_ref[x] = jnp.where(lane40 < 64, v_ref[x], 0.0) + far
    for copy in r_copies:
        copy.wait()
    for x in range(36):
        g, i = x // 12, x % 12
        above = pltpu.roll(rr[1, g], (64 - 4 * i) % 128, 1)
        below = pltpu.roll(rr[0, g], (124 - 4 * i) % 128, 1)
        rim = jnp.where((lane40 >= 64) & (lane40 < 67), above, 0.0)
        v_ref[x] += jnp.where(lane40 == 127, below, rim)


def field(inv, counts, taps, charge, positions):
    def scratch(*shape):
        return pltpu.VMEM(shape, f32)

    return pl.pallas_call(
        field_kernel,
        out_shape=(
            jax.ShapeDtypeStruct((36, 40, 128), f32),
            jax.ShapeDtypeStruct((1024, 2, 8, 128), f32),
            jax.ShapeDtypeStruct((1024, 2, 16, 128), bf16),
        ),
        in_specs=[SMEM, SMEM, SMEM, VMEM, VMEM],
        out_specs=(VMEM, VMEM, VMEM),
        scratch_shapes=[
            scratch(2, 36, 32, 128),
            pltpu.VMEM((256, 128), bf16),
            scratch(32, 8, 128),
            scratch(2, 128, 128),
            scratch(54, 40, 128),
            scratch(2, 5, 40, 128),
            scratch(2, 5, 40, 128),
            scratch(40, 40, 128),
            scratch(2, 40, 16, 128),
            scratch(2, 40, 16, 128),
            scratch(2, 15, 40, 128),
            scratch(58, 40, 128),
            scratch(2, 3, 40, 128),
            scratch(2, 3, 40, 128),
            scratch(24, 24, 128),
            scratch(2, 8, 24, 128),
            scratch(2, 8, 24, 128),
            scratch(43, 24, 128),
            scratch(24, 24, 128),
            scratch(2, 6, 24, 128),
            scratch(2, 6, 24, 128),
            scratch(24, 24, 128),
            scratch(2, 24, 16, 128),
            scratch(2, 24, 16, 128),
            scratch(22, 40, 128),
            pltpu.VMEM((384, 128), bf16),
            pltpu.VMEM((80, 256), bf16),
            pltpu.VMEM((256, 128), bf16),
            pltpu.VMEM((24, 96), bf16),
            pltpu.VMEM((384, 128), bf16),
            pltpu.VMEM((80, 256), bf16),
            pltpu.VMEM((256, 128), bf16),
            pltpu.SemaphoreType.DMA((2, 5, 2)),
            pltpu.SemaphoreType.DMA((2, 5, 2)),
            pltpu.SemaphoreType.DMA((2, 5)),
            pltpu.SemaphoreType.DMA((2, 4, 2)),
            pltpu.SemaphoreType.DMA((2, 3, 2)),
        ],
        compiler_params=pltpu.CompilerParams(
            collective_id=0, has_side_effects=True, vmem_limit_bytes=30 * 1024 * 1024
        ),
    )(inv, counts, taps, charge, positions)


def body(charge, positions, counts, corner, fine_taps, coarse_taps):
    ext_y = CY + 6
    ext_z = CZ + 6
    count = corner.shape[0]
    spots = np.arange(count, dtype=np.int32)
    along_y, along_z = CY // 4, CZ // 4
    cell_x, cell_y, cell_z = spots // (along_y * along_z), spots // along_z % along_y, spots % along_z
    wanted = ((4 * cell_x + 2) * ext_y + 4 * cell_y + 2) * ext_z + 4 * cell_z + 2
    same = corner[:, None] == wanted[None, :]
    number = lax.broadcasted_iota(jnp.int32, (count, count), 0)
    inv = jnp.sum(jnp.where(same, number, 0), axis=0, dtype=jnp.int32)
    live = jnp.sum(jnp.where(same, counts[:, None], 0), axis=0, dtype=jnp.int32)
    taps = jnp.concatenate([fine_taps, coarse_taps], 0)
    values, planes, depths = field(inv, live, taps, charge, positions)
    return sample(inv, live, planes, depths, values)


def solution(mesh):
    placed = (
        P(("gx", "gy", "gz"), None),
        P(None, ("gx", "gy", "gz"), None),
        P(("gx", "gy", "gz")),
        P(("gx", "gy", "gz")),
        P(),
        P(),
    )
    return jax.shard_map(
        body,
        mesh=mesh,
        in_specs=placed,
        out_specs=(P(("gx", "gy", "gz"), None), P("gx", "gy", "gz")),
        check_vma=False,
    )
```
